256 devices in a mesh: dom: 256 (over y, x, z, core).
Axes of the slice: x: 4, y: 4, z: 8, core: 2. Of those that a mesh axis runs over, the one named last changes fastest.
Arguments:
- features: bfloat16 [1048576, 128], P('dom'), may hold values from -6 to 6
- local_tiles: bfloat16 [8192, 3, 128, 128], P('dom'), may hold values from 0 to 0.06982422
- local_src: int32 [8192, 3], P('dom'), may hold values from 0 to 31
- remote_tiles: bfloat16 [8192, 3, 128, 128], P('dom'), may hold values from 0 to 0.06982422
- remote_src: int32 [8192, 3], P('dom'), may hold values from 0 to 23, as said below
- send_blocks: int32 [1024, 4], P('dom'), may hold values from 0 to 31
- hub_rows: int32 [1024], P('dom'), may hold values from 0 to 4095
- w_self: bfloat16 [128, 256], replicated, may hold values from -0.5 to 0.5
- w_neigh: bfloat16 [128, 256], replicated, may hold values from -0.5 to 0.5
- bias: float32 [256], replicated, may hold values from -3 to 3
- d_hidden: bfloat16 [1048576, 256], P('dom'), may hold values from -24 to 24
Outputs:
- hidden: bfloat16 [1048576, 256], P('dom')
- grad_features: bfloat16 [1048576, 128], P('dom')
- grad_w_self: float32 [128, 256], P(None, 'dom')
- grad_w_neigh: float32 [128, 256], P(None, 'dom')
- grad_bias: float32 [256], P('dom')
The draws below stay inside these ranges and needn't reach their ends.
Inputs may be any that keep to these rules, and one draw needn't show every extreme that they name: `local_src`: local tile sources index the partition's own row blocks. `remote_src`: remote tile sources index the partition's remote table; in each partition every halo block of the table is the source of at least one remote tile. `send_blocks`: blocks may repeat in a list. `hub_rows`: two hubs may name the same row.
All inputs are finite; a program needn't handle non-finite values.
Results may differ from the reference program's by a relative error of at most 0.0065.
Values may be sent and summed in bfloat16 or wider, within the bound.
No kernel may reach another device: no remote copies, remote signals or barrier semaphores. Data moves between devices by JAX's collectives and lax.ppermute only.
A program may use at most 128 MiB of HBM per device.

```python
import jax
import jax.numpy as jnp
from jax import lax

F = 128
H = 256
TILE = 128
BLK_DEV = 32
LOCAL_TILES = 3
REMOTE_TILES = 3
HALO_BLK = 4
HUB_DEV = 4
NODE_DEV = 4096
NODES = 1048576
HUBS = 1024
REMOTE_BLK = 24
N_DOM = 256


def draw_remote_src(key, part):
    key = jax.random.fold_in(key, 11)
    slots = BLK_DEV * REMOTE_TILES
    halo_slots = 4 * HALO_BLK
    rank_keys = jax.random.split(jax.random.fold_in(key, 1), N_DOM)
    ranks = jax.vmap(lambda k: jax.random.permutation(k, slots))(rank_keys).astype(jnp.int32)
    loose = jax.random.randint(jax.random.fold_in(key, 2), (N_DOM, slots), 0, REMOTE_BLK).astype(jnp.int32)
    values = jnp.where(ranks < halo_slots, ranks, loose)
    values = jnp.where(ranks == halo_slots, REMOTE_BLK - 1, values)
    return values.reshape(N_DOM * BLK_DEV, REMOTE_TILES).astype(jnp.int32)


def touch_ends(drawn, key, smallest, top_value):
    extent = drawn.shape
    place = [jax.random.randint(jax.random.fold_in(key, axis), (), 0, extent[axis]) for axis in range(len(extent))]
    drawn = drawn.at[tuple(place)].set(smallest)
    longest = extent.index(max(extent))
    place[longest] = (place[longest] + 1) % extent[longest]
    return drawn.at[tuple(place)].set(top_value)


def spiked(values, rng, source, target, blocks, factor):
    def block_of(position):
        return (jnp.arange(values.shape[position]) // (values.shape[position] // blocks)).reshape((-1,) + (1,) * (values.ndim - 1 - position))

    one_side = jax.random.permutation(rng, blocks)[block_of(target)]
    other_side = (block_of(target) + blocks // 2) % blocks
    return jnp.where((block_of(source) == one_side) | (block_of(source) == other_side), factor * values, values)


def block_scale(rng, shape, cuts, smallest, top_value):
    gain, own = 1.0, jax.random.fold_in(rng, 6)
    for dim, blocks in cuts:
        heights = jnp.exp(jax.random.uniform(jax.random.fold_in(own, dim), (blocks,), jnp.float32, smallest / len(cuts), top_value / len(cuts)))
        gain = gain * jnp.repeat(heights, shape[dim] // blocks).reshape([-1 if axis == dim else 1 for axis in range(len(shape))])
    return gain


def gaussian(key, extent, scale, limit, cuts=(), held_as=jnp.bfloat16):
    factor_of = block_scale(key, extent, cuts, -0.22, 0.18) if cuts else 1.0
    drawn = jax.random.normal(key, extent, jnp.float32) * scale * factor_of
    return jnp.minimum(jnp.maximum(drawn, -limit), limit).astype(held_as)


def heavy_noise(rng, dims, deviation, bound, cuts, heavy, held_as=jnp.bfloat16):
    drawn = deviation * jax.random.normal(rng, dims, jnp.float32)
    if cuts:
        drawn = drawn * block_scale(rng, dims, cuts, -0.22, 0.18)
    return jnp.clip(spiked(drawn, jax.random.fold_in(rng, 3), *heavy), -bound, bound).astype(held_as)


def setup_inputs(seed: int = 0) -> dict:
    key_of = jax.random.split(jax.random.key(seed), 12)
    features = gaussian(key_of[0], (NODES, F), 1.0, 6.0, ((0, 256),))
    local_tiles = jnp.clip(0.06982422 * jax.random.uniform(key_of[1], (N_DOM * BLK_DEV, LOCAL_TILES, TILE, TILE), jnp.float32) ** block_scale(key_of[1], (N_DOM * BLK_DEV, LOCAL_TILES, TILE, TILE), ((0, 256),), -0.2, 0.2), 0.0, 0.06982422).astype(jnp.bfloat16)
    local_src = touch_ends(jax.random.randint(key_of[2], (N_DOM * BLK_DEV, LOCAL_TILES), 0, BLK_DEV), jax.random.fold_in(key_of[2], 1), 0, BLK_DEV - 1).astype(jnp.int32)
    remote_tiles = jnp.clip(0.06982422 * jax.random.uniform(key_of[3], (N_DOM * BLK_DEV, REMOTE_TILES, TILE, TILE), jnp.float32) ** block_scale(key_of[3], (N_DOM * BLK_DEV, REMOTE_TILES, TILE, TILE), ((0, 256),), -0.2, 0.2), 0.0, 0.06982422).astype(jnp.bfloat16)
    remote_src = draw_remote_src(jax.random.fold_in(key_of[11], 71), 0)
    send_blocks = touch_ends(jax.random.randint(key_of[5], (4 * N_DOM, HALO_BLK), 0, BLK_DEV), jax.random.fold_in(key_of[5], 1), 0, BLK_DEV - 1).astype(jnp.int32)
    hub_rows = touch_ends(jax.random.randint(key_of[6], (HUBS,), 0, NODE_DEV), jax.random.fold_in(key_of[6], 1), 0, NODE_DEV - 1).astype(jnp.int32)
    w_self = gaussian(key_of[7], (F, H), F ** -0.5, 0.5)
    w_neigh = gaussian(key_of[8], (F, H), F ** -0.5, 0.5)
    bias = gaussian(key_of[9], (H,), 0.5, 3.0, (), jnp.float32)
    d_hidden = heavy_noise(key_of[10], (NODES, H), 1.0, 24.0, ((0, 256),), (0, 1, 256, 6.0))
    return dict(features=features, local_tiles=local_tiles, local_src=local_src, remote_tiles=remote_tiles, remote_src=remote_src, send_blocks=send_blocks, hub_rows=hub_rows, w_self=w_self, w_neigh=w_neigh, bias=bias, d_hidden=d_hidden)


OFFSETS = (1, -1, 2, -2)


def reference(features, local_tiles, local_src, remote_tiles, remote_src, send_blocks, hub_rows, w_self, w_neigh, bias, d_hidden):
    blocks = features.reshape(N_DOM, BLK_DEV, TILE, F)
    sends = send_blocks.reshape(N_DOM, 4, HALO_BLK)
    owners = jnp.arange(HUB_DEV * N_DOM, dtype=jnp.int32) // HUB_DEV
    flat_index = (owners * NODE_DEV + hub_rows).astype(jnp.int32)
    hub_feat = features[flat_index].reshape(-1, TILE, F)
    ltiles = local_tiles.reshape(N_DOM, BLK_DEV, LOCAL_TILES, TILE, TILE)
    lsource = local_src.reshape(N_DOM, BLK_DEV, LOCAL_TILES)
    rtiles = remote_tiles.reshape(N_DOM, BLK_DEV, REMOTE_TILES, TILE, TILE)
    rsource = remote_src.reshape(N_DOM, BLK_DEV, REMOTE_TILES)
    dhid = d_hidden.reshape(N_DOM, NODE_DEV, H)

    def one(carry, device):
        hub_acc, acc_self, acc_neigh, acc_bias = carry
        own = blocks[device]
        halos = []
        for j, step in enumerate(OFFSETS):
            source = (device - step) % N_DOM
            halos.append(blocks[source][sends[source, j]].reshape(-1, TILE, F))
        remote = jnp.concatenate(halos + [hub_feat], 0)
        ltile = ltiles[device].astype(jnp.float32)
        rtile = rtiles[device].astype(jnp.float32)
        lidx = lsource[device]
        ridx = rsource[device]
        agg = jnp.einsum("bkij,bkjf->bif", ltile, own[lidx].astype(jnp.float32))
        agg = agg + jnp.einsum("bkij,bkjf->bif", rtile, remote[ridx].astype(jnp.float32))
        agg_b = agg.reshape(NODE_DEV, F).astype(jnp.bfloat16)
        rows = own.reshape(NODE_DEV, F)
        pre = jnp.dot(rows, w_self, preferred_element_type=jnp.float32) + jnp.dot(agg_b, w_neigh, preferred_element_type=jnp.float32) + bias
        sig = jax.nn.sigmoid(pre)
        hidden = (pre * sig).astype(jnp.bfloat16)
        d_pre = dhid[device].astype(jnp.float32) * sig * (1.0 + pre * (1.0 - sig))
        d_pre_b = d_pre.astype(jnp.bfloat16)
        acc_self = acc_self + jnp.dot(rows.T, d_pre_b, preferred_element_type=jnp.float32)
        acc_neigh = acc_neigh + jnp.dot(agg_b.T, d_pre_b, preferred_element_type=jnp.float32)
        acc_bias = acc_bias + jnp.sum(d_pre, 0)
        d_self = jnp.dot(d_pre_b, w_self.T, preferred_element_type=jnp.float32)
        d_agg = jnp.dot(d_pre_b, w_neigh.T, preferred_element_type=jnp.float32).astype(jnp.bfloat16)
        d_agg = d_agg.reshape(BLK_DEV, TILE, F).astype(jnp.float32)
        d_loc = jnp.zeros((BLK_DEV, TILE, F), jnp.float32).at[lidx].add(jnp.einsum("bkij,bif->bkjf", ltile, d_agg))
        d_rem = jnp.zeros((REMOTE_BLK, TILE, F), jnp.float32).at[ridx].add(jnp.einsum("bkij,bif->bkjf", rtile, d_agg))
        local_grad = d_self + d_loc.reshape(NODE_DEV, F)
        halo_grad = d_rem[:4 * HALO_BLK]
        hub_acc = hub_acc + d_rem[4 * HALO_BLK:].reshape(-1, F)
        return (hub_acc, acc_self, acc_neigh, acc_bias), (hidden, local_grad, halo_grad)

    init = (jnp.zeros((HUB_DEV * N_DOM, F), jnp.float32), jnp.zeros((F, H), jnp.float32), jnp.zeros((F, H), jnp.float32), jnp.zeros((H,), jnp.float32))
    carry, stacked = lax.scan(one, init, jnp.arange(N_DOM, dtype=jnp.int32))
    hub_acc, grad_w_self, grad_w_neigh, grad_bias = carry
    hidden, local_grad, halo_grad = stacked
    halo_grad = halo_grad.reshape(N_DOM, 4, HALO_BLK, TILE, F)
    grad_blocks = local_grad.reshape(N_DOM, BLK_DEV, TILE, F)

    def add_into(grid, index, update):
        return grid.at[index].add(update)

    for j, step in enumerate(OFFSETS):
        returned = jnp.roll(halo_grad[:, j], -step, axis=0)
        grad_blocks = jax.vmap(add_into)(grad_blocks, sends[:, j], returned)
    grad_flat = grad_blocks.reshape(NODES, F).at[flat_index].add(hub_acc)
    return hidden.reshape(NODES, H), grad_flat.astype(jnp.bfloat16), grad_w_self, grad_w_neigh, grad_bias
```

```python
import functools

import jax
import jax.numpy as jnp
from jax import lax
from jax.experimental import pallas as pl
from jax.experimental.pallas import tpu as pltpu
from jax.sharding import PartitionSpec as P

OFFSETS = (1, -1, 2, -2)
F32 = jnp.float32
BF16 = jnp.bfloat16
NT = (((1,), (1,)), ((), ()))
TN = (((0,), (0,)), ((), ()))
GROUP = 16
CHUNK = 8
STEP = 4


def shifted(block, axis, distance):
    devices = range(lax.axis_size(axis))
    route = [((i - distance) % len(devices), i) for i in devices]
    return lax.ppermute(block, axis, route)


def params(mib, **more):
    return pltpu.CompilerParams(vmem_limit_bytes=mib << 20, **more)


def whole(shape):
    return pl.BlockSpec(shape, lambda *_: (0,) * len(shape))


def send_kernel(send, hubs, blocks, *refs):
    lists, per_list = send.shape
    outs, hub_out = refs[:lists], refs[lists]
    near, sem_a, sem_b = refs[lists + 1 :]
    owned = hubs.shape[0]
    tile = blocks.shape[1]
    copies = []
    for i in range(owned):
        row = hubs[i]
        base = pl.multiple_of(lax.rem(row, tile) // GROUP * GROUP, GROUP)
        copies.append(
            pltpu.make_async_copy(
                blocks.at[row // tile, pl.ds(base, GROUP), :], near.at[i], sem_a.at[i]
            )
        )
    for c in copies:
        c.start()
    moves = []
    for j in range(lists):
        for h in range(per_list):
            moves.append(
                pltpu.make_async_copy(
                    blocks.at[send[j, h]], outs[j].at[h], sem_b.at[j * per_list + h]
                )
            )
    for c in moves:
        c.start()
    for c in copies:
        c.wait()
    place = lax.broadcasted_iota(jnp.int32, (GROUP, near.shape[-1]), 0)
    rows = []
    for i in range(owned):
        chosen = jnp.where(place == lax.rem(hubs[i], GROUP), near[i].astype(F32), 0.0)
        rows.append(jnp.sum(chosen, 0, keepdims=True))
    rows.append(jnp.zeros((hub_out.shape[0] - owned, near.shape[-1]), F32))
    hub_out[...] = jnp.concatenate(rows, 0)
    for c in moves:
        c.wait()


def gather_sends(send, hubs, blocks):
    lists, per_list = send.shape
    _, tile, width = blocks.shape
    owned = hubs.shape[0]
    any_spec = pl.BlockSpec(memory_space=pl.ANY)
    return pl.pallas_call(
        send_kernel,
        out_shape=[jax.ShapeDtypeStruct((per_list, tile, width), blocks.dtype)] * lists
        + [jax.ShapeDtypeStruct((8, width), F32)],
        in_specs=[
            pl.BlockSpec(memory_space=pltpu.SMEM),
            pl.BlockSpec(memory_space=pltpu.SMEM),
            any_spec,
        ],
        out_specs=[any_spec] * lists + [pl.BlockSpec(memory_space=pltpu.VMEM)],
        scratch_shapes=[
            pltpu.VMEM((owned, GROUP, width), blocks.dtype),
            pltpu.SemaphoreType.DMA((owned,)),
            pltpu.SemaphoreType.DMA((lists * per_list,)),
        ],
        compiler_params=params(8),
        name="sends",
    )(send, hubs, blocks)


def local_kernel(src, tiles, blocks, agg):
    first = pl.program_id(0) * STEP
    tile = tiles.shape[-1]
    for b in range(STEP):
        taken = [blocks[src[k, first + b]] for k in range(tiles.shape[1])]
        edges = [tiles[b, k] for k in range(tiles.shape[1])]
        agg[b * tile : (b + 1) * tile, :] = jnp.dot(
            jnp.concatenate(edges, 1), jnp.concatenate(taken, 0), preferred_element_type=F32
        )


def local_aggregate(src, tiles, blocks):
    count, per_block, tile, _ = tiles.shape
    width = blocks.shape[-1]
    return pl.pallas_call(
        local_kernel,
        out_shape=jax.ShapeDtypeStruct((count * tile, width), F32),
        grid_spec=pltpu.PrefetchScalarGridSpec(
            num_scalar_prefetch=1,
            grid=(count // STEP,),
            in_specs=[
                pl.BlockSpec((STEP, per_block, tile, tile), lambda i, *_: (i, 0, 0, 0)),
                whole(blocks.shape),
            ],
            out_specs=pl.BlockSpec((STEP * tile, width), lambda i, *_: (i, 0)),
        ),
        compiler_params=params(12),
        cost_estimate=pl.CostEstimate(
            flops=2 * tiles.size * width, bytes_accessed=8 << 20, transcendentals=0
        ),
        name="local_aggregate",
    )(src, tiles, blocks)


def layer_kernel(src, tiles, rows, agg_local, *refs):
    lists = len(OFFSETS)
    halos, refs = refs[:lists], refs[lists:]
    hub, weights, bias, d_hidden, hidden, d_pre_out, d_agg_out = refs[:7]
    backs, refs = refs[7 : 7 + lists], refs[7 + lists :]
    packed, table, rem_grad, w_grad, b_grad, spread, sems = refs
    step = pl.program_id(0)
    tile = tiles.shape[-1]
    width = rows.shape[-1]
    per_list = halos[0].shape[0]
    halo_count = lists * per_list
    hub_blocks = hub.shape[0]

    @pl.when(step == 0)
    def _():
        moves = []
        for j in range(lists):
            moves.append(
                pltpu.make_async_copy(
                    halos[j], table.at[pl.ds(j * per_list, per_list)], sems.at[j]
                )
            )
        moves.append(
            pltpu.make_async_copy(hub, table.at[pl.ds(halo_count, hub_blocks)], sems.at[lists])
        )
        for c in moves:
            c.start()
        rem_grad[...] = jnp.zeros_like(rem_grad)
        w_grad[...] = jnp.zeros_like(w_grad)
        b_grad[...] = jnp.zeros_like(b_grad)
        for c in moves:
            c.wait()

    for b in range(STEP):
        block = slice(b * tile, (b + 1) * tile)
        sources = [src[k, step * STEP + b] for k in range(tiles.shape[1])]
        edges = jnp.concatenate([tiles[b, k] for k in range(tiles.shape[1])], 1)
        taken = jnp.concatenate([table[s] for s in sources], 0)
        agg = agg_local[block, :] + jnp.dot(edges, taken, preferred_element_type=F32)
        both = jnp.concatenate([rows[block, :], agg.astype(BF16)], 1)
        pre = jnp.dot(both, weights[...], preferred_element_type=F32) + bias[...]
        sig = jax.nn.sigmoid(pre)
        hidden[block, :] = (pre * sig).astype(BF16)
        d_pre = d_hidden[block, :].astype(F32) * (sig * (1.0 + pre * (1.0 - sig)))
        b_grad[...] += jnp.sum(d_pre.reshape(tile // 8, 8, d_pre.shape[-1]), 0)
        d_pre_b = d_pre.astype(BF16)
        d_pre_out[block, :] = d_pre_b
        w_grad[...] += lax.dot_general(d_pre_b, both, TN, preferred_element_type=F32)
        d_agg = lax.dot_general(weights[width:, :], d_pre_b, NT, preferred_element_type=F32)
        d_agg = d_agg.astype(BF16)
        d_agg_out[b] = d_agg
        terms = jnp.dot(d_agg, edges, preferred_element_type=F32)
        for k, s in enumerate(sources):
            rem_grad[s] += terms[:, k * tile : (k + 1) * tile]

    @pl.when(step == pl.num_programs(0) - 1)
    def _():
        for j in range(lists):
            backs[j][...] = rem_grad[j * per_list : (j + 1) * per_list].astype(BF16)
        parts, chunk, _ = packed.shape
        owned = hub_blocks * tile // parts
        hub_rows = jnp.concatenate(
            [jnp.transpose(rem_grad[halo_count + q]) for q in range(hub_blocks)], 0
        )
        spread[...] = jnp.zeros_like(spread)
        split = hub_rows.reshape(parts, owned, width)
        for i in range(owned):
            spread[pl.ds(i, parts, stride=chunk), :] = split[:, i, :]
        spread[pl.ds(owned, parts, stride=chunk), :] = w_grad[:, :width]
        spread[pl.ds(owned + 1, parts, stride=chunk), :] = w_grad[:, width:]
        total = jnp.sum(b_grad[...], 0, keepdims=True)
        high = total.astype(BF16).astype(F32)
        lane = lax.broadcasted_iota(jnp.int32, (width, parts), 0)
        two = jnp.where(lane == 0, high, jnp.where(lane == 1, total - high, 0.0))
        spread[pl.ds(owned + 2, parts, stride=chunk), :] = jnp.transpose(two)
        packed[...] = spread[...].reshape(parts, chunk, width).astype(BF16)


def layer(src, tiles, rows, agg_local, halos, hub, weights, bias, d_hidden, parts):
    count, per_block, tile, _ = tiles.shape
    nodes, width = rows.shape
    units = d_hidden.shape[-1]
    per_list = halos[0].shape[0]
    table = len(halos) * per_list + hub.shape[0]
    any_spec = pl.BlockSpec(memory_space=pl.ANY)

    def by_step(*shape):
        return pl.BlockSpec(shape, lambda i, *_: (i,) + (0,) * (len(shape) - 1))

    return pl.pallas_call(
        layer_kernel,
        out_shape=[
            jax.ShapeDtypeStruct((nodes, units), BF16),
            jax.ShapeDtypeStruct((nodes, units), BF16),
            jax.ShapeDtypeStruct((count, width, tile), BF16),
        ]
        + [jax.ShapeDtypeStruct((per_list, width, tile), BF16)] * len(halos)
        + [jax.ShapeDtypeStruct((parts, CHUNK, width), BF16)],
        grid_spec=pltpu.PrefetchScalarGridSpec(
            num_scalar_prefetch=1,
            grid=(count // STEP,),
            in_specs=[
                by_step(STEP, per_block, tile, tile),
                by_step(STEP * tile, width),
                by_step(STEP * tile, width),
            ]
            + [any_spec] * (len(halos) + 1)
            + [
                whole(weights.shape),
                whole(bias.shape),
                by_step(STEP * tile, units),
            ],
            out_specs=[
                by_step(STEP * tile, units),
                by_step(STEP * tile, units),
                by_step(STEP, width, tile),
            ]
            + [whole((per_list, width, tile))] * len(halos)
            + [whole((parts, CHUNK, width))],
            scratch_shapes=[
                pltpu.VMEM((table, tile, width), BF16),
                pltpu.VMEM((table, width, tile), F32),
                pltpu.VMEM((units, 2 * width), F32),
                pltpu.VMEM((8, units), F32),
                pltpu.VMEM((parts * CHUNK, width), F32),
                pltpu.SemaphoreType.DMA((len(halos) + 1,)),
            ],
        ),
        compiler_params=params(24),
        cost_estimate=pl.CostEstimate(
            flops=4 * tiles.size * width + 12 * nodes * width * units,
            bytes_accessed=14 << 20,
            transcendentals=nodes * units,
        ),
        name="layer",
    )(src, tiles, rows, agg_local, *halos, hub, weights, bias, d_hidden)


def back_kernel(src, tiles, d_pre, d_agg, weight, grad):
    step = pl.program_id(0)
    tile = tiles.shape[-1]

    @pl.when(step == 0)
    def _():
        grad[...] = jnp.zeros_like(grad)

    for b in range(STEP):
        own = lax.dot_general(
            weight[...], d_pre[b * tile : (b + 1) * tile, :], NT, preferred_element_type=F32
        )
        grad[step * STEP + b] += own
        edges = jnp.concatenate([tiles[b, k] for k in range(tiles.shape[1])], 1)
        terms = jnp.dot(d_agg[b], edges, preferred_element_type=F32)
        for k in range(tiles.shape[1]):
            s = src[k, step * STEP + b]
            grad[s] += terms[:, k * tile : (k + 1) * tile]


def local_backward(src, tiles, d_pre, d_agg, weight):
    count, per_block, tile, _ = tiles.shape
    width, units = weight.shape
    return pl.pallas_call(
        back_kernel,
        out_shape=jax.ShapeDtypeStruct((count, width, tile), F32),
        grid_spec=pltpu.PrefetchScalarGridSpec(
            num_scalar_prefetch=1,
            grid=(count // STEP,),
            in_specs=[
                pl.BlockSpec((STEP, per_block, tile, tile), lambda i, *_: (i, 0, 0, 0)),
                pl.BlockSpec((STEP * tile, units), lambda i, *_: (i, 0)),
                pl.BlockSpec((STEP, width, tile), lambda i, *_: (i, 0, 0)),
                whole(weight.shape),
            ],
            out_specs=whole((count, width, tile)),
        ),
        compiler_params=params(16),
        cost_estimate=pl.CostEstimate(
            flops=2 * tiles.size * width + 2 * d_pre.size * width,
            bytes_accessed=8 << 20,
            transcendentals=0,
        ),
        name="local_backward",
    )(src, tiles, d_pre, d_agg, weight)


def collect_kernel(send, hubs, grad, *refs):
    lists, per_list = send.shape
    halos = refs[:lists]
    out, near, total = refs[lists:]
    count, width, tile = grad.shape
    total[...] = grad[...]
    for j in range(lists):
        for h in range(per_list):
            total[send[j, h]] += halos[j][h].astype(F32)
    for b in range(count):
        out[b * tile : (b + 1) * tile, :] = jnp.transpose(total[b]).astype(BF16)
    for i in range(hubs.shape[0]):
        row = hubs[i]
        turned = jnp.transpose(total[row // tile])
        want = lax.rem(row, tile) // GROUP
        part = jnp.zeros((GROUP, width), F32)
        for g in range(tile // GROUP):
            part = jnp.where(want == g, turned[g * GROUP : (g + 1) * GROUP], part)
        near[i] = part


def collect(send, hubs, grad, halos):
    count, width, tile = grad.shape
    smem = pl.BlockSpec(memory_space=pltpu.SMEM)
    vmem = pl.BlockSpec(memory_space=pltpu.VMEM)
    return pl.pallas_call(
        collect_kernel,
        out_shape=[
            jax.ShapeDtypeStruct((count * tile, width), BF16),
            jax.ShapeDtypeStruct((hubs.shape[0], GROUP, width), F32),
        ],
        in_specs=[smem, smem] + [vmem] * (1 + len(halos)),
        out_specs=[vmem, vmem],
        scratch_shapes=[pltpu.VMEM((count, width, tile), F32)],
        compiler_params=params(16),
        cost_estimate=pl.CostEstimate(
            flops=grad.size * 8, bytes_accessed=4 << 20, transcendentals=0
        ),
        name="collect",
    )(send, hubs, grad, *halos)


def finish_kernel(hubs, pieces, near, _, grad, g_self, g_neigh, g_bias, rows, sems):
    owned = hubs.shape[0]
    total = jnp.sum(pieces[...].astype(F32), 0)
    g_self[...] = total[owned : owned + 1, :]
    g_neigh[...] = total[owned + 1 : owned + 2, :]
    last = total[owned + 2 : owned + 3, :]
    g_bias[...] = jnp.broadcast_to(last[:, 0:1] + last[:, 1:2], last.shape)
    place = lax.broadcasted_iota(jnp.int32, (GROUP, total.shape[-1]), 0)
    for i in range(owned):
        value = near[i]
        for m in range(owned):
            same = hubs[m] // GROUP == hubs[i] // GROUP
            hit = jnp.logical_and(place == lax.rem(hubs[m], GROUP), same)
            value = value + jnp.where(hit, total[m : m + 1, :], 0.0)
        rows[i] = value.astype(BF16)

    def fresh(i):
        new = hubs[i] >= 0
        for m in range(i):
            new = jnp.logical_and(new, hubs[m] // GROUP != hubs[i] // GROUP)
        return new

    def move(i):
        base = pl.multiple_of(hubs[i] // GROUP * GROUP, GROUP)
        return pltpu.make_async_copy(rows.at[i], grad.at[pl.ds(base, GROUP), :], sems.at[i])

    for i in range(owned):
        pl.when(fresh(i))(lambda i=i: move(i).start())
    for i in range(owned):
        pl.when(fresh(i))(lambda i=i: move(i).wait())


def finish(hubs, pieces, near, grad):
    owned, _, width = near.shape
    smem = pl.BlockSpec(memory_space=pltpu.SMEM)
    vmem = pl.BlockSpec(memory_space=pltpu.VMEM)
    any_spec = pl.BlockSpec(memory_space=pl.ANY)
    line = jax.ShapeDtypeStruct((1, width), F32)
    return pl.pallas_call(
        finish_kernel,
        out_shape=[jax.ShapeDtypeStruct(grad.shape, grad.dtype), line, line, line],
        in_specs=[smem, vmem, vmem, any_spec],
        out_specs=[any_spec, vmem, vmem, vmem],
        scratch_shapes=[
            pltpu.VMEM((owned, GROUP, width), BF16),
            pltpu.SemaphoreType.DMA((owned,)),
        ],
        input_output_aliases={3: 0},
        compiler_params=params(8),
        name="finish",
    )(hubs, pieces, near, grad)


def shards(
    features,
    local_tiles,
    local_src,
    remote_tiles,
    remote_src,
    send_blocks,
    hub_rows,
    w_self,
    w_neigh,
    bias,
    d_hidden,
):
    parts = lax.axis_size("dom")
    nodes, width = features.shape
    tile = local_tiles.shape[-1]
    owned = hub_rows.shape[0]
    blocks = features.reshape(nodes // tile, tile, width)
    *sends, hub_mine = gather_sends(send_blocks, hub_rows, blocks)
    everywhere = jnp.broadcast_to(hub_mine[:owned].astype(BF16)[None], (parts, owned, width))
    hub_all = lax.all_to_all(everywhere, "dom", 0, 0)
    halos = [shifted(b, "dom", step) for b, step in zip(sends, OFFSETS)]
    agg_local = local_aggregate(local_src.T, local_tiles, blocks)
    weights = jnp.concatenate([w_self, w_neigh], 0)
    hidden, d_pre, d_agg, *rest = layer(
        remote_src.T,
        remote_tiles,
        features,
        agg_local,
        halos,
        hub_all.reshape(parts * owned // tile, tile, width),
        weights,
        bias[None],
        d_hidden,
        parts,
    )
    *backs, packed = rest
    pieces = lax.all_to_all(packed, "dom", 0, 0)
    returned = [shifted(b, "dom", -step) for b, step in zip(backs, OFFSETS)]
    grad_t = local_backward(local_src.T, local_tiles, d_pre, d_agg, w_self)
    rough, near = collect(send_blocks, hub_rows, grad_t, returned)
    grad, g_self, g_neigh, g_bias = finish(hub_rows, pieces, near, rough)
    return (hidden, grad, g_self.reshape(width, 1), g_neigh.reshape(width, 1), g_bias[0, :1])


def solution(mesh):
    in_specs = (
        P("dom", None),
        P("dom", None, None, None),
        P("dom", None),
        P("dom", None, None, None),
        P("dom", None),
        P("dom", None),
        P("dom"),
        P(),
        P(),
        P(),
        P("dom", None),
    )
    out_specs = (P("dom", None), P("dom", None), P(None, "dom"), P(None, "dom"), P("dom"))
    return jax.shard_map(shards, mesh=mesh, in_specs=in_specs, out_specs=out_specs, check_vma=False)
```

```python
import functools

import jax
import jax.numpy as jnp
from jax import lax
from jax.experimental import pallas as pl
from jax.experimental.pallas import tpu as pltpu
from jax.sharding import PartitionSpec as P

OFFSETS = (1, -1, 2, -2)
F32 = jnp.float32
BF16 = jnp.bfloat16
NT = (((1,), (1,)), ((), ()))
TN = (((0,), (0,)), ((), ()))
GROUP = 16
CHUNK = 8
STEP = 8


def partner(i, way, n):
    if way == 0:
        return i ^ 1
    if way == 1:
        return (i + (1 if i & 1 else -1)) % n
    ahead = (i >> 1) & 1 == way - 2
    return (i + (2 if ahead else -2)) % n


def swapped(block, way):
    n = lax.axis_size("dom")
    return lax.ppermute(block, "dom", [(i, partner(i, way, n)) for i in range(n)])


def lists_of_ways():
    me = lax.axis_index("dom")
    odd, odd_chip = me & 1, (me >> 1) & 1
    return odd, 1 - odd, 2 + odd_chip, 3 - odd_chip


def rows_of(chunk, size):
    return pl.ds(pl.multiple_of(chunk * size, size), size)


def params():
    return pltpu.CompilerParams(vmem_limit_bytes=40 << 20)


def hbm(x):
    return pltpu.with_memory_space_constraint(x, pltpu.HBM)


def vmem(x):
    return pltpu.with_memory_space_constraint(x, pltpu.VMEM)


ANY_SPEC = pl.BlockSpec(memory_space=pl.ANY)
HBM_SPEC = pl.BlockSpec(memory_space=pltpu.HBM)
VMEM_SPEC = pl.BlockSpec(memory_space=pltpu.VMEM)


def start(copies):
    for c in copies:
        c.start()


def wait(copies):
    for c in copies:
        c.wait()


def whole(shape):
    return pl.BlockSpec(shape, lambda *_: (0,) * len(shape))


def send_kernel(send_hbm, hubs_hbm, blocks_hbm, *refs):
    lists, per_list = send_hbm.shape
    outs, refs = refs[:lists], refs[lists:]
    hub_out, blocks, send, hubs, sem_in, sems = refs
    owned = hubs.shape[0]
    count, tile, width = blocks.shape
    pairs = [(send_hbm, send), (hubs_hbm, hubs)]
    half = count // 2
    for part in (pl.ds(0, half), pl.ds(half, half)):
        pairs.append((blocks_hbm.at[part], blocks.at[part]))
    loads = [pltpu.make_async_copy(*p, sem_in.at[n]) for n, p in enumerate(pairs)]
    start(loads)
    wait(loads)
    moves = []
    for way, j in enumerate(lists_of_ways()):
        for h in range(per_list):
            moves.append(
                pltpu.make_async_copy(
                    blocks.at[send[j, h]], outs[way].at[h], sems.at[way * per_list + h]
                )
            )
    start(moves)
    place = lax.broadcasted_iota(jnp.int32, (GROUP, width), 0)
    rows = []
    for i in range(owned):
        row = hubs[i]
        base = pl.multiple_of(lax.rem(row, tile) // GROUP * GROUP, GROUP)
        near = blocks[row // tile, pl.ds(base, GROUP), :].astype(F32)
        chosen = jnp.where(place == lax.rem(row, GROUP), near, 0.0)
        rows.append(jnp.sum(chosen, 0, keepdims=True))
    hub_out[...] = jnp.broadcast_to(jnp.concatenate(rows, 0).astype(BF16)[None], hub_out.shape)
    wait(moves)


def gather_sends(send, hubs, blocks, parts):
    lists, per_list = send.shape
    _, tile, width = blocks.shape
    return pl.pallas_call(
        send_kernel,
        out_shape=[jax.ShapeDtypeStruct((per_list, tile, width), BF16)] * lists
        + [
            jax.ShapeDtypeStruct((parts, hubs.shape[0], width), BF16),
            pltpu.VMEM(blocks.shape, BF16),
        ],
        in_specs=[HBM_SPEC] * 3,
        out_specs=[ANY_SPEC] * lists + [VMEM_SPEC, VMEM_SPEC],
        scratch_shapes=[
            pltpu.SMEM(send.shape, jnp.int32),
            pltpu.SMEM(hubs.shape, jnp.int32),
            pltpu.SemaphoreType.DMA((4,)),
            pltpu.SemaphoreType.DMA((lists * per_list,)),
        ],
        compiler_params=params(),
        name="sends",
    )(hbm(send), hbm(hubs), hbm(blocks))


def local_kernel(
    src_hbm, tiles_hbm, remote_hbm, d_hbm, blocks, agg, tiles, remote, d_hidden, src, sem, sem_in
):
    count, per_block, tile, _ = tiles.shape
    chunks = count // STEP

    def fetch(i):
        part = pl.ds(i * STEP, STEP)
        return pltpu.make_async_copy(tiles_hbm.at[part], tiles.at[part], sem_in.at[i])

    index = pltpu.make_async_copy(src_hbm, src, sem.at[0])
    index.start()
    for i in range(chunks):
        fetch(i).start()
    later = [
        pltpu.make_async_copy(remote_hbm, remote, sem.at[1]),
        pltpu.make_async_copy(d_hbm, d_hidden, sem.at[2]),
    ]
    start(later)
    index.wait()

    @pl.loop(0, chunks)
    def _(i):
        fetch(i).wait()
        for b in range(STEP):
            at = i * STEP + b
            taken = [blocks[src[k, at]] for k in range(per_block)]
            edges = [tiles[at, k] for k in range(per_block)]
            agg[rows_of(at, tile), :] = jnp.dot(
                jnp.concatenate(edges, 1), jnp.concatenate(taken, 0), preferred_element_type=F32
            )

    wait(later)


def local_aggregate(src, tiles, remote, d_hidden, blocks):
    count, per_block, tile, _ = tiles.shape
    width = blocks.shape[-1]
    return pl.pallas_call(
        local_kernel,
        out_shape=[
            pltpu.VMEM((count * tile, width), F32),
            pltpu.VMEM(tiles.shape, BF16),
            pltpu.VMEM(remote.shape, BF16),
            pltpu.VMEM(d_hidden.shape, BF16),
        ],
        in_specs=[HBM_SPEC] * 4 + [VMEM_SPEC],
        out_specs=[VMEM_SPEC] * 4,
        scratch_shapes=[
            pltpu.SMEM(src.shape, jnp.int32),
            pltpu.SemaphoreType.DMA((3,)),
            pltpu.SemaphoreType.DMA((count // STEP,)),
        ],
        compiler_params=params(),
        cost_estimate=pl.CostEstimate(
            flops=2 * tiles.size * width, bytes_accessed=8 << 20, transcendentals=0
        ),
        name="local_aggregate",
    )(hbm(src), hbm(tiles), hbm(remote), hbm(d_hidden), vmem(blocks))


def layer_kernel(src_hbm, *refs):
    lists = len(OFFSETS)
    tiles, rows, agg_local, d_hidden = refs[:4]
    halos, refs = refs[4 : 4 + lists], refs[4 + lists :]
    hub, self_hbm, neigh_hbm, bias_hbm, hidden, d_pre_out, d_agg_out = refs[:7]
    backs, refs = refs[7 : 7 + lists], refs[7 + lists :]
    packed, src, weights, bias, table, rem_grad, backs_out, w_grad, b_grad, spread = refs[:10]
    pack_out, sem_t, sem_back = refs[10:]
    count, per_block, tile, _ = tiles.shape
    width = rows.shape[-1]
    per_list = halos[0].shape[0]
    halo_count = lists * per_list
    hub_blocks = hub.shape[0]
    slots = [j ^ 1 for j in lists_of_ways()]
    pairs = [
        (src_hbm, src),
        (hub, table.at[pl.ds(halo_count, hub_blocks)]),
        (self_hbm, weights.at[pl.ds(0, width)]),
        (neigh_hbm, weights.at[pl.ds(width, width)]),
        (bias_hbm, bias),
    ]
    for w, s in enumerate(slots):
        pairs.append((halos[w], table.at[pl.ds(s * per_list, per_list)]))
    moves = [pltpu.make_async_copy(*p, sem_t.at[n]) for n, p in enumerate(pairs)]
    start(moves)
    rem_grad[...] = jnp.zeros_like(rem_grad)
    w_grad[...] = jnp.zeros_like(w_grad)
    b_grad[...] = jnp.zeros_like(b_grad)
    wait(moves)

    @pl.loop(0, count // STEP)
    def _(i):
        many = rows_of(i, STEP * tile)

        def edges(b):
            return jnp.concatenate([tiles[i * STEP + b, k] for k in range(per_block)], 1)

        sources = [[src[k, i * STEP + b] for k in range(per_block)] for b in range(STEP)]
        remote = [
            jnp.dot(
                edges(b),
                jnp.concatenate([table[s] for s in sources[b]], 0),
                preferred_element_type=F32,
            )
            for b in range(STEP)
        ]
        agg = agg_local[many, :] + jnp.concatenate(remote, 0)
        both = jnp.concatenate([rows[many, :], agg.astype(BF16)], 1)
        pre = jnp.dot(both, weights[...], preferred_element_type=F32) + bias[...]
        sig = jax.nn.sigmoid(pre)
        hidden[many, :] = (pre * sig).astype(BF16)
        d_pre = d_hidden[many, :].astype(F32) * (sig * (1.0 + pre * (1.0 - sig)))
        b_grad[...] += jnp.sum(d_pre.reshape(-1, 8, d_pre.shape[-1]), 0)
        d_pre_b = d_pre.astype(BF16)
        d_pre_out[many, :] = d_pre_b
        d_agg = lax.dot_general(weights[width:, :], d_pre_b, NT, preferred_element_type=F32)
        d_agg = d_agg.astype(BF16)
        for b in range(STEP):
            own = d_agg[:, b * tile : (b + 1) * tile]
            d_agg_out[i * STEP + b] = own
            terms = jnp.dot(own, edges(b), preferred_element_type=F32)
            for k, s in enumerate(sources[b]):
                rem_grad[s] += terms[:, k * tile : (k + 1) * tile]
        w_grad[...] += lax.dot_general(d_pre_b, both, TN, preferred_element_type=F32)

    sent = []
    for w, s in enumerate(slots):
        backs_out[w] = rem_grad[pl.ds(s * per_list, per_list)].astype(BF16)
        sent.append(pltpu.make_async_copy(backs_out.at[w], backs[w], sem_back.at[w]))
    start(sent)
    parts, chunk, _ = packed.shape
    owned = hub_blocks * tile // parts
    hub_rows = jnp.concatenate(
        [jnp.transpose(rem_grad[halo_count + q]) for q in range(hub_blocks)], 0
    )
    split = hub_rows.reshape(parts, owned, width)
    for i in range(owned):
        spread[pl.ds(i, parts, stride=chunk), :] = split[:, i, :]
    spread[pl.ds(owned, parts, stride=chunk), :] = w_grad[:, :width]
    spread[pl.ds(owned + 1, parts, stride=chunk), :] = w_grad[:, width:]
    total = jnp.sum(b_grad[...], 0, keepdims=True)
    high = total.astype(BF16).astype(F32)
    lane = lax.broadcasted_iota(jnp.int32, (width, parts), 0)
    two = jnp.where(lane == 0, high, jnp.where(lane == 1, total - high, 0.0))
    spread[pl.ds(owned + 2, parts, stride=chunk), :] = jnp.transpose(two)
    for i in range(owned + 3, chunk):
        spread[pl.ds(i, parts, stride=chunk), :] = jnp.zeros((parts, width), F32)
    pack_out[...] = spread[...].reshape(parts, chunk, width).astype(BF16)
    last = pltpu.make_async_copy(pack_out, packed, sem_back.at[lists])
    last.start()
    wait(sent)
    last.wait()


def layer(src, tiles, rows, agg_local, halos, hub, w_self, w_neigh, bias, d_hidden, parts):
    count, per_block, tile, _ = tiles.shape
    nodes, width = rows.shape
    units = d_hidden.shape[-1]
    lists, per_list = len(halos), halos[0].shape[0]
    table = lists * per_list + hub.shape[0]
    packed = (parts, CHUNK, width)
    return pl.pallas_call(
        layer_kernel,
        out_shape=[
            pltpu.VMEM((nodes, units), BF16),
            pltpu.VMEM((nodes, units), BF16),
            pltpu.VMEM((count, width, tile), BF16),
        ]
        + [jax.ShapeDtypeStruct((per_list, width, tile), BF16)] * lists
        + [jax.ShapeDtypeStruct(packed, BF16)],
        in_specs=[HBM_SPEC] + [VMEM_SPEC] * 4 + [HBM_SPEC] * (lists + 4),
        out_specs=[VMEM_SPEC] * 3 + [ANY_SPEC] * (lists + 1),
        scratch_shapes=[
            pltpu.SMEM(src.shape, jnp.int32),
            pltpu.VMEM((2 * width, units), BF16),
            pltpu.VMEM((1, units), F32),
            pltpu.VMEM((table, tile, width), BF16),
            pltpu.VMEM((table, width, tile), F32),
            pltpu.VMEM((lists, per_list, width, tile), BF16),
            pltpu.VMEM((units, 2 * width), F32),
            pltpu.VMEM((8, units), F32),
            pltpu.VMEM((parts * CHUNK, width), F32),
            pltpu.VMEM(packed, BF16),
            pltpu.SemaphoreType.DMA((lists + 5,)),
            pltpu.SemaphoreType.DMA((lists + 1,)),
        ],
        compiler_params=params(),
        cost_estimate=pl.CostEstimate(
            flops=4 * tiles.size * width + 12 * nodes * width * units,
            bytes_accessed=14 << 20,
            transcendentals=nodes * units,
        ),
        name="layer",
    )(
        hbm(src),
        vmem(tiles),
        vmem(rows),
        vmem(agg_local),
        vmem(d_hidden),
        *[hbm(x) for x in (*halos, hub, w_self, w_neigh, bias)],
    )


def back_kernel(src_hbm, weight_hbm, tiles, d_pre, d_agg, hidden, out, total, src, weight, sems):
    count, per_block, tile, _ = tiles.shape
    size = STEP * tile
    result = pltpu.make_async_copy(hidden, out, sems.at[0])
    result.start()
    loads = [
        pltpu.make_async_copy(src_hbm, src, sems.at[1]),
        pltpu.make_async_copy(weight_hbm, weight, sems.at[2]),
    ]
    start(loads)
    total[...] = jnp.zeros_like(total)
    wait(loads)

    @pl.loop(0, count // STEP)
    def _(i):
        own = lax.dot_general(
            weight[...], d_pre[rows_of(i, size), :], NT, preferred_element_type=F32
        )
        for b in range(STEP):
            at = i * STEP + b
            total[at] += own[:, b * tile : (b + 1) * tile]
            edges = jnp.concatenate([tiles[at, k] for k in range(per_block)], 1)
            terms = jnp.dot(d_agg[at], edges, preferred_element_type=F32)
            for k in range(per_block):
                s = src[k, at]
                total[s] += terms[:, k * tile : (k + 1) * tile]

    result.wait()


def local_backward(src, tiles, d_pre, d_agg, weight, hidden):
    count, per_block, tile, _ = tiles.shape
    width, units = weight.shape
    return pl.pallas_call(
        back_kernel,
        out_shape=[
            jax.ShapeDtypeStruct(hidden.shape, BF16),
            pltpu.VMEM((count, width, tile), F32),
        ],
        in_specs=[HBM_SPEC] * 2 + [VMEM_SPEC] * 4,
        out_specs=[ANY_SPEC, VMEM_SPEC],
        scratch_shapes=[
            pltpu.SMEM(src.shape, jnp.int32),
            pltpu.VMEM(weight.shape, BF16),
            pltpu.SemaphoreType.DMA((3,)),
        ],
        compiler_params=params(),
        cost_estimate=pl.CostEstimate(
            flops=2 * tiles.size * width + 2 * d_pre.size * width,
            bytes_accessed=8 << 20,
            transcendentals=0,
        ),
        name="local_backward",
    )(hbm(src), hbm(weight), vmem(tiles), vmem(d_pre), vmem(d_agg), vmem(hidden))


def collect_kernel(send_hbm, hubs_hbm, _, *refs):
    lists, per_list = send_hbm.shape
    halos_hbm = refs[:lists]
    total, out, near, send, hubs, halos, turned, sem_in, sem_out = refs[lists:]
    count, width, tile = total.shape
    pairs = [(send_hbm, send), (hubs_hbm, hubs)]
    pairs += [(halos_hbm[way], halos.at[way]) for way in range(lists)]
    loads = [pltpu.make_async_copy(*p, sem_in.at[n]) for n, p in enumerate(pairs)]
    start(loads)
    wait(loads)
    for way, j in enumerate(lists_of_ways()):
        for h in range(per_list):
            total[send[j, h]] += halos[way, h].astype(F32)
    chunks = sem_out.shape[0]
    each = count // chunks
    stores = []
    for c in range(chunks):
        for b in range(c * each, (c + 1) * each):
            turned[b * tile : (b + 1) * tile, :] = jnp.transpose(total[b]).astype(BF16)
        part = pl.ds(c * each * tile, each * tile)
        stores.append(pltpu.make_async_copy(turned.at[part], out.at[part], sem_out.at[c]))
        stores[-1].start()
    for i in range(hubs.shape[0]):
        row = hubs[i]
        block = jnp.transpose(total[row // tile])
        want = lax.rem(row, tile) // GROUP
        part = jnp.zeros((GROUP, width), F32)
        for g in range(tile // GROUP):
            part = jnp.where(want == g, block[g * GROUP : (g + 1) * GROUP], part)
        near[i] = part
    wait(stores)


def collect(send, hubs, grad, halos):
    count, width, tile = grad.shape
    lists = len(halos)
    near = (hubs.shape[0], GROUP, width)
    return pl.pallas_call(
        collect_kernel,
        out_shape=[
            pltpu.VMEM(grad.shape, F32),
            jax.ShapeDtypeStruct((count * tile, width), BF16),
            pltpu.VMEM(near, F32),
        ],
        in_specs=[HBM_SPEC] * 2 + [VMEM_SPEC] + [HBM_SPEC] * lists,
        out_specs=[VMEM_SPEC, ANY_SPEC, VMEM_SPEC],
        scratch_shapes=[
            pltpu.SMEM(send.shape, jnp.int32),
            pltpu.SMEM(hubs.shape, jnp.int32),
            pltpu.VMEM((lists,) + halos[0].shape, BF16),
            pltpu.VMEM((count * tile, width), BF16),
            pltpu.SemaphoreType.DMA((2 + lists,)),
            pltpu.SemaphoreType.DMA((4,)),
        ],
        input_output_aliases={2: 0},
        compiler_params=params(),
        cost_estimate=pl.CostEstimate(
            flops=grad.size * 8, bytes_accessed=4 << 20, transcendentals=0
        ),
        name="collect",
    )(hbm(send), hbm(hubs), vmem(grad), *[hbm(x) for x in halos])[1:]


def finish_kernel(
    hubs_hbm, pieces_hbm, near, _, grad, g_self, g_neigh, g_bias, hubs, pieces, rows, sem_in, sems
):
    owned = hubs.shape[0]
    chunks = sem_in.shape[0] - 1
    each = pieces.shape[0] // chunks
    index = pltpu.make_async_copy(hubs_hbm, hubs, sem_in.at[chunks])
    index.start()
    loads = []
    for c in range(chunks):
        part = pl.ds(c * each, each)
        loads.append(pltpu.make_async_copy(pieces_hbm.at[part], pieces.at[part], sem_in.at[c]))
    start(loads)
    index.wait()
    total = jnp.zeros(pieces.shape[1:], F32)
    for c in range(chunks):
        loads[c].wait()
        total += jnp.sum(pieces[c * each : (c + 1) * each].astype(F32), 0)
    g_self[...] = total[owned : owned + 1, :]
    g_neigh[...] = total[owned + 1 : owned + 2, :]
    last = total[owned + 2 : owned + 3, :]
    g_bias[...] = jnp.broadcast_to(last[:, 0:1] + last[:, 1:2], last.shape)
    place = lax.broadcasted_iota(jnp.int32, (GROUP, total.shape[-1]), 0)
    for i in range(owned):
        value = near[i]
        for m in range(owned):
            same = hubs[m] // GROUP == hubs[i] // GROUP
            hit = jnp.logical_and(place == lax.rem(hubs[m], GROUP), same)
            value = value + jnp.where(hit, total[m : m + 1, :], 0.0)
        rows[i] = value.astype(BF16)

    def fresh(i):
        new = hubs[i] >= 0
        for m in range(i):
            new = jnp.logical_and(new, hubs[m] // GROUP != hubs[i] // GROUP)
        return new

    def move(i):
        base = pl.multiple_of(hubs[i] // GROUP * GROUP, GROUP)
        return pltpu.make_async_copy(rows.at[i], grad.at[pl.ds(base, GROUP), :], sems.at[i])

    for i in range(owned):
        pl.when(fresh(i))(lambda i=i: move(i).start())
    for i in range(owned):
        pl.when(fresh(i))(lambda i=i: move(i).wait())


def finish(hubs, pieces, near, grad):
    owned, _, width = near.shape
    line = jax.ShapeDtypeStruct((1, width), F32)
    return pl.pallas_call(
        finish_kernel,
        out_shape=[jax.ShapeDtypeStruct(grad.shape, grad.dtype), line, line, line],
        in_specs=[HBM_SPEC, HBM_SPEC, VMEM_SPEC, ANY_SPEC],
        out_specs=[ANY_SPEC, VMEM_SPEC, VMEM_SPEC, VMEM_SPEC],
        scratch_shapes=[
            pltpu.SMEM(hubs.shape, jnp.int32),
            pltpu.VMEM(pieces.shape, BF16),
            pltpu.VMEM((owned, GROUP, width), BF16),
            pltpu.SemaphoreType.DMA((5,)),
            pltpu.SemaphoreType.DMA((owned,)),
        ],
        input_output_aliases={3: 0},
        compiler_params=params(),
        name="finish",
    )(hbm(hubs), hbm(pieces), vmem(near), grad)


def shards(
    features,
    local_tiles,
    local_src,
    remote_tiles,
    remote_src,
    send_blocks,
    hub_rows,
    w_self,
    w_neigh,
    bias,
    d_hidden,
):
    parts = lax.axis_size("dom")
    nodes, width = features.shape
    tile = local_tiles.shape[-1]
    owned = hub_rows.shape[0]
    blocks = features.reshape(nodes // tile, tile, width)
    *sends, hub_mine, own = gather_sends(send_blocks, hub_rows, blocks, parts)
    hub_all = lax.all_to_all(hub_mine, "dom", 0, 0)
    halos = [swapped(b, way) for way, b in enumerate(sends)]
    agg_local, tiles_l, tiles_r, d_hid = local_aggregate(
        local_src.T, local_tiles, remote_tiles, d_hidden, own
    )
    hidden, d_pre, d_agg, *rest = layer(
        remote_src.T,
        tiles_r,
        own.reshape(nodes, width),
        agg_local,
        halos,
        hub_all.reshape(parts * owned // tile, tile, width),
        w_self,
        w_neigh,
        bias[None],
        d_hid,
        parts,
    )
    *backs, packed = rest
    pieces = lax.all_to_all(packed, "dom", 0, 0)
    returned = [swapped(b, way) for way, b in enumerate(backs)]
    out, grad_t = local_backward(local_src.T, tiles_l, d_pre, d_agg, w_self, hidden)
    rough, near = collect(send_blocks, hub_rows, grad_t, returned)
    grad, g_self, g_neigh, g_bias = finish(hub_rows, pieces, near, rough)
    return (out, grad, g_self.reshape(width, 1), g_neigh.reshape(width, 1), g_bias[0, :1])


def solution(mesh):
    in_specs = (
        P("dom", None),
        P("dom", None, None, None),
        P("dom", None),
        P("dom", None, None, None),
        P("dom", None),
        P("dom", None),
        P("dom"),
        P(),
        P(),
        P(),
        P("dom", None),
    )
    out_specs = (P("dom", None), P("dom", None), P(None, "dom"), P(None, "dom"), P("dom"))
    return jax.shard_map(shards, mesh=mesh, in_specs=in_specs, out_specs=out_specs, check_vma=False)
```

```python
import functools

import jax
import jax.numpy as jnp
from jax import lax
from jax.experimental import pallas as pl
from jax.experimental.pallas import tpu as pltpu
from jax.sharding import PartitionSpec as P

OFFSETS = (1, -1, 2, -2)
F32 = jnp.float32
BF16 = jnp.bfloat16
NT = (((1,), (1,)), ((), ()))
TN = (((0,), (0,)), ((), ()))
GROUP = 16
CHUNK = 8
STEP = 8


def partner(i, way, n):
    if way == 0:
        return i ^ 1
    if way == 1:
        return (i + (1 if i & 1 else -1)) % n
    ahead = (i >> 1) & 1 == way - 2
    return (i + (2 if ahead else -2)) % n


def swapped(block, way):
    n = lax.axis_size("dom")
    return lax.ppermute(block, "dom", [(i, partner(i, way, n)) for i in range(n)])


def lists_of_ways():
    me = lax.axis_index("dom")
    odd, odd_chip = me & 1, (me >> 1) & 1
    return odd, 1 - odd, 2 + odd_chip, 3 - odd_chip


def rows_of(chunk, size):
    return pl.ds(pl.multiple_of(chunk * size, size), size)


def params():
    return pltpu.CompilerParams(vmem_limit_bytes=40 << 20)


def hbm(x):
    return pltpu.with_memory_space_constraint(x, pltpu.HBM)


def vmem(x):
    return pltpu.with_memory_space_constraint(x, pltpu.VMEM)


ANY_SPEC = pl.BlockSpec(memory_space=pl.ANY)
HBM_SPEC = pl.BlockSpec(memory_space=pltpu.HBM)
VMEM_SPEC = pl.BlockSpec(memory_space=pltpu.VMEM)


def start(copies):
    for c in copies:
        c.start()


def wait(copies):
    for c in copies:
        c.wait()


def whole(shape):
    return pl.BlockSpec(shape, lambda *_: (0,) * len(shape))


def send_kernel(send_hbm, hubs_hbm, blocks_hbm, *refs):
    lists, per_list = send_hbm.shape
    outs, refs = refs[:lists], refs[lists:]
    hub_out, blocks, send, hubs, sem_in, sems = refs
    owned = hubs.shape[0]
    count, tile, width = blocks.shape
    pairs = [(send_hbm, send), (hubs_hbm, hubs)]
    half = count // 2
    for part in (pl.ds(0, half), pl.ds(half, half)):
        pairs.append((blocks_hbm.at[part], blocks.at[part]))
    loads = [pltpu.make_async_copy(*p, sem_in.at[n]) for n, p in enumerate(pairs)]
    start(loads)
    wait(loads)
    moves = []
    for way, j in enumerate(lists_of_ways()):
        for h in range(per_list):
            moves.append(
                pltpu.make_async_copy(
                    blocks.at[send[j, h]], outs[way].at[h], sems.at[way * per_list + h]
                )
            )
    start(moves)
    place = lax.broadcasted_iota(jnp.int32, (GROUP, width), 0)
    rows = []
    for i in range(owned):
        row = hubs[i]
        base = pl.multiple_of(lax.rem(row, tile) // GROUP * GROUP, GROUP)
        near = blocks[row // tile, pl.ds(base, GROUP), :].astype(F32)
        chosen = jnp.where(place == lax.rem(row, GROUP), near, 0.0)
        rows.append(jnp.sum(chosen, 0, keepdims=True))
    hub_out[...] = jnp.broadcast_to(jnp.concatenate(rows, 0).astype(BF16)[None], hub_out.shape)
    wait(moves)


def gather_sends(send, hubs, blocks, parts):
    lists, per_list = send.shape
    _, tile, width = blocks.shape
    return pl.pallas_call(
        send_kernel,
        out_shape=[pltpu.HBM((per_list, tile, width), BF16)] * lists
        + [
            jax.ShapeDtypeStruct((parts, hubs.shape[0], width), BF16),
            pltpu.VMEM(blocks.shape, BF16),
        ],
        in_specs=[HBM_SPEC] * 3,
        out_specs=[HBM_SPEC] * lists + [VMEM_SPEC, VMEM_SPEC],
        scratch_shapes=[
            pltpu.SMEM(send.shape, jnp.int32),
            pltpu.SMEM(hubs.shape, jnp.int32),
            pltpu.SemaphoreType.DMA((4,)),
            pltpu.SemaphoreType.DMA((lists * per_list,)),
        ],
        compiler_params=params(),
        name="sends",
    )(hbm(send), hbm(hubs), hbm(blocks))


def local_kernel(
    src_hbm, tiles_hbm, d_hbm, blocks, agg_hbm, d_hidden, src, tiles, agg, sem, sem_in, sem_out
):
    count, per_block, tile, _ = tiles.shape
    chunks = count // STEP

    def fetch(i):
        part = pl.ds(i * STEP, STEP)
        return pltpu.make_async_copy(tiles_hbm.at[part], tiles.at[part], sem_in.at[i])

    def store(i):
        part = rows_of(i, STEP * tile)
        return pltpu.make_async_copy(agg.at[part], agg_hbm.at[part], sem_out.at[i])

    index = pltpu.make_async_copy(src_hbm, src, sem.at[0])
    index.start()
    for i in range(chunks):
        fetch(i).start()
    later = pltpu.make_async_copy(d_hbm, d_hidden, sem.at[1])
    later.start()
    index.wait()

    @pl.loop(0, chunks)
    def _(i):
        fetch(i).wait()
        for b in range(STEP):
            at = i * STEP + b
            taken = [blocks[src[k, at]] for k in range(per_block)]
            edges = [tiles[at, k] for k in range(per_block)]
            agg[rows_of(at, tile), :] = jnp.dot(
                jnp.concatenate(edges, 1), jnp.concatenate(taken, 0), preferred_element_type=F32
            )
        store(i).start()

    later.wait()
    wait([store(i) for i in range(chunks)])


def local_aggregate(src, tiles, d_hidden, blocks):
    count, per_block, tile, _ = tiles.shape
    width = blocks.shape[-1]
    agg = (count * tile, width)
    return pl.pallas_call(
        local_kernel,
        out_shape=[pltpu.HBM(agg, F32), pltpu.VMEM(d_hidden.shape, BF16)],
        in_specs=[HBM_SPEC] * 3 + [VMEM_SPEC],
        out_specs=[HBM_SPEC, VMEM_SPEC],
        scratch_shapes=[
            pltpu.SMEM(src.shape, jnp.int32),
            pltpu.VMEM(tiles.shape, BF16),
            pltpu.VMEM(agg, F32),
            pltpu.SemaphoreType.DMA((2,)),
            pltpu.SemaphoreType.DMA((count // STEP,)),
            pltpu.SemaphoreType.DMA((count // STEP,)),
        ],
        compiler_params=params(),
        cost_estimate=pl.CostEstimate(
            flops=2 * tiles.size * width, bytes_accessed=8 << 20, transcendentals=0
        ),
        name="local_aggregate",
    )(hbm(src), hbm(tiles), hbm(d_hidden), vmem(blocks))


def layer_kernel(src_hbm, *refs):
    lists = len(OFFSETS)
    tiles_hbm, rows_hbm, agg_hbm, d_hidden = refs[:4]
    halos, refs = refs[4 : 4 + lists], refs[4 + lists :]
    hub, self_hbm, neigh_hbm, bias_hbm, hidden_hbm, d_pre_out, d_agg_out = refs[:7]
    backs, refs = refs[7 : 7 + lists], refs[7 + lists :]
    packed, src, weights, bias, table, rem_grad, backs_out, w_grad, b_grad, spread = refs[:10]
    pack_out, tiles, rows, agg_local, hidden, sem_t, sem_back, sem_in, sem_out = refs[10:]
    count, per_block, tile, _ = tiles.shape
    width = rows.shape[-1]
    per_list = halos[0].shape[0]
    halo_count = lists * per_list
    hub_blocks = hub.shape[0]
    slots = [j ^ 1 for j in lists_of_ways()]
    pairs = [
        (src_hbm, src),
        (hub, table.at[pl.ds(halo_count, hub_blocks)]),
        (self_hbm, weights.at[pl.ds(0, width)]),
        (neigh_hbm, weights.at[pl.ds(width, width)]),
        (bias_hbm, bias),
    ]
    for w, s in enumerate(slots):
        pairs.append((halos[w], table.at[pl.ds(s * per_list, per_list)]))
    moves = [pltpu.make_async_copy(*p, sem_t.at[n]) for n, p in enumerate(pairs)]
    chunks = count // STEP

    def fetch(i):
        few, many = pl.ds(i * STEP, STEP), rows_of(i, STEP * tile)
        pairs = (
            (tiles_hbm.at[few], tiles.at[few]),
            (agg_hbm.at[many], agg_local.at[many]),
            (rows_hbm.at[many], rows.at[many]),
        )
        return [pltpu.make_async_copy(*p, sem_in.at[i, n]) for n, p in enumerate(pairs)]

    def store(i):
        many = rows_of(i, STEP * tile)
        return pltpu.make_async_copy(hidden.at[many], hidden_hbm.at[many], sem_out.at[i])

    start(moves)
    for i in range(chunks):
        start(fetch(i))
    rem_grad[...] = jnp.zeros_like(rem_grad)
    w_grad[...] = jnp.zeros_like(w_grad)
    b_grad[...] = jnp.zeros_like(b_grad)
    wait(moves)

    @pl.loop(0, chunks)
    def _(i):
        wait(fetch(i))
        many = rows_of(i, STEP * tile)

        def edges(b):
            return jnp.concatenate([tiles[i * STEP + b, k] for k in range(per_block)], 1)

        sources = [[src[k, i * STEP + b] for k in range(per_block)] for b in range(STEP)]
        remote = [
            jnp.dot(
                edges(b),
                jnp.concatenate([table[s] for s in sources[b]], 0),
                preferred_element_type=F32,
            )
            for b in range(STEP)
        ]
        agg = agg_local[many, :] + jnp.concatenate(remote, 0)
        both = jnp.concatenate([rows[many, :], agg.astype(BF16)], 1)
        pre = jnp.dot(both, weights[...], preferred_element_type=F32) + bias[...]
        sig = jax.nn.sigmoid(pre)
        hidden[many, :] = (pre * sig).astype(BF16)
        store(i).start()
        d_pre = d_hidden[many, :].astype(F32) * (sig * (1.0 + pre * (1.0 - sig)))
        b_grad[...] += jnp.sum(d_pre.reshape(-1, 8, d_pre.shape[-1]), 0)
        d_pre_b = d_pre.astype(BF16)
        d_pre_out[many, :] = d_pre_b
        d_agg = lax.dot_general(weights[width:, :], d_pre_b, NT, preferred_element_type=F32)
        d_agg = d_agg.astype(BF16)
        for b in range(STEP):
            own = d_agg[:, b * tile : (b + 1) * tile]
            d_agg_out[i * STEP + b] = own
            terms = jnp.dot(own, edges(b), preferred_element_type=F32)
            for k, s in enumerate(sources[b]):
                rem_grad[s] += terms[:, k * tile : (k + 1) * tile]
        w_grad[...] += lax.dot_general(d_pre_b, both, TN, preferred_element_type=F32)

    sent = []
    for w, s in enumerate(slots):
        backs_out[w] = rem_grad[pl.ds(s * per_list, per_list)].astype(BF16)
        sent.append(pltpu.make_async_copy(backs_out.at[w], backs[w], sem_back.at[w]))
    start(sent)
    parts, chunk, _ = packed.shape
    owned = hub_blocks * tile // parts
    hub_rows = jnp.concatenate(
        [jnp.transpose(rem_grad[halo_count + q]) for q in range(hub_blocks)], 0
    )
    split = hub_rows.reshape(parts, owned, width)
    for i in range(owned):
        spread[pl.ds(i, parts, stride=chunk), :] = split[:, i, :]
    spread[pl.ds(owned, parts, stride=chunk), :] = w_grad[:, :width]
    spread[pl.ds(owned + 1, parts, stride=chunk), :] = w_grad[:, width:]
    total = jnp.sum(b_grad[...], 0, keepdims=True)
    high = total.astype(BF16).astype(F32)
    lane = lax.broadcasted_iota(jnp.int32, (width, parts), 0)
    two = jnp.where(lane == 0, high, jnp.where(lane == 1, total - high, 0.0))
    spread[pl.ds(owned + 2, parts, stride=chunk), :] = jnp.transpose(two)
    for i in range(owned + 3, chunk):
        spread[pl.ds(i, parts, stride=chunk), :] = jnp.zeros((parts, width), F32)
    pack_out[...] = spread[...].reshape(parts, chunk, width).astype(BF16)
    last = pltpu.make_async_copy(pack_out, packed, sem_back.at[lists])
    last.start()
    wait(sent)
    wait([store(i) for i in range(chunks)])
    last.wait()


def layer(src, tiles, rows, agg_local, halos, hub, w_self, w_neigh, bias, d_hidden, parts):
    count, per_block, tile, _ = tiles.shape
    nodes, width = rows.shape
    units = d_hidden.shape[-1]
    lists, per_list = len(halos), halos[0].shape[0]
    table = lists * per_list + hub.shape[0]
    packed = (parts, CHUNK, width)
    chunks = count // STEP
    return pl.pallas_call(
        layer_kernel,
        out_shape=[
            pltpu.HBM((nodes, units), BF16),
            pltpu.VMEM((nodes, units), BF16),
            pltpu.VMEM((count, width, tile), BF16),
        ]
        + [pltpu.HBM((per_list, width, tile), BF16)] * lists
        + [pltpu.HBM(packed, BF16)],
        in_specs=[HBM_SPEC] * 4 + [VMEM_SPEC] + [ANY_SPEC] * (lists + 1) + [HBM_SPEC] * 3,
        out_specs=[HBM_SPEC] + [VMEM_SPEC] * 2 + [HBM_SPEC] * (lists + 1),
        scratch_shapes=[
            pltpu.SMEM(src.shape, jnp.int32),
            pltpu.VMEM((2 * width, units), BF16),
            pltpu.VMEM((1, units), F32),
            pltpu.VMEM((table, tile, width), BF16),
            pltpu.VMEM((table, width, tile), F32),
            pltpu.VMEM((lists, per_list, width, tile), BF16),
            pltpu.VMEM((units, 2 * width), F32),
            pltpu.VMEM((8, units), F32),
            pltpu.VMEM((parts * CHUNK, width), F32),
            pltpu.VMEM(packed, BF16),
            pltpu.VMEM(tiles.shape, BF16),
            pltpu.VMEM((nodes, width), BF16),
            pltpu.VMEM((nodes, width), F32),
            pltpu.VMEM((nodes, units), BF16),
            pltpu.SemaphoreType.DMA((lists + 5,)),
            pltpu.SemaphoreType.DMA((lists + 1,)),
            pltpu.SemaphoreType.DMA((chunks, 3)),
            pltpu.SemaphoreType.DMA((chunks,)),
        ],
        compiler_params=params(),
        cost_estimate=pl.CostEstimate(
            flops=4 * tiles.size * width + 12 * nodes * width * units,
            bytes_accessed=14 << 20,
            transcendentals=nodes * units,
        ),
        name="layer",
    )(
        hbm(src),
        hbm(tiles),
        hbm(rows),
        hbm(agg_local),
        vmem(d_hidden),
        *halos,
        hub,
        hbm(w_self),
        hbm(w_neigh),
        hbm(bias),
    )


def back_kernel(
    src_hbm, weight_hbm, tiles_hbm, d_pre, d_agg, total, src, weight, tiles, sems, sem_in
):
    count, per_block, tile, _ = tiles.shape
    size = STEP * tile

    def fetch(i):
        part = pl.ds(i * STEP, STEP)
        return pltpu.make_async_copy(tiles_hbm.at[part], tiles.at[part], sem_in.at[i])

    loads = [
        pltpu.make_async_copy(src_hbm, src, sems.at[0]),
        pltpu.make_async_copy(weight_hbm, weight, sems.at[1]),
    ]
    start(loads)
    start([fetch(i) for i in range(count // STEP)])
    total[...] = jnp.zeros_like(total)
    wait(loads)

    @pl.loop(0, count // STEP)
    def _(i):
        fetch(i).wait()
        own = lax.dot_general(
            weight[...], d_pre[rows_of(i, size), :], NT, preferred_element_type=F32
        )
        for b in range(STEP):
            at = i * STEP + b
            total[at] += own[:, b * tile : (b + 1) * tile]
            edges = jnp.concatenate([tiles[at, k] for k in range(per_block)], 1)
            terms = jnp.dot(d_agg[at], edges, preferred_element_type=F32)
            for k in range(per_block):
                s = src[k, at]
                total[s] += terms[:, k * tile : (k + 1) * tile]


def local_backward(src, tiles, d_pre, d_agg, weight):
    count, per_block, tile, _ = tiles.shape
    width, units = weight.shape
    return pl.pallas_call(
        back_kernel,
        out_shape=pltpu.VMEM((count, width, tile), F32),
        in_specs=[HBM_SPEC] * 3 + [VMEM_SPEC] * 2,
        out_specs=VMEM_SPEC,
        scratch_shapes=[
            pltpu.SMEM(src.shape, jnp.int32),
            pltpu.VMEM(weight.shape, BF16),
            pltpu.VMEM(tiles.shape, BF16),
            pltpu.SemaphoreType.DMA((2,)),
            pltpu.SemaphoreType.DMA((count // STEP,)),
        ],
        compiler_params=params(),
        cost_estimate=pl.CostEstimate(
            flops=2 * tiles.size * width + 2 * d_pre.size * width,
            bytes_accessed=8 << 20,
            transcendentals=0,
        ),
        name="local_backward",
    )(hbm(src), hbm(weight), hbm(tiles), vmem(d_pre), vmem(d_agg))


def collect_kernel(send_hbm, hubs_hbm, _, *refs):
    lists, per_list = send_hbm.shape
    halos_hbm = refs[:lists]
    total, out, near, send, hubs, halos, turned, sem_in, sem_out = refs[lists:]
    count, width, tile = total.shape
    pairs = [(send_hbm, send), (hubs_hbm, hubs)]
    pairs += [(halos_hbm[way], halos.at[way]) for way in range(lists)]
    loads = [pltpu.make_async_copy(*p, sem_in.at[n]) for n, p in enumerate(pairs)]
    start(loads)
    wait(loads)
    for way, j in enumerate(lists_of_ways()):
        for h in range(per_list):
            total[send[j, h]] += halos[way, h].astype(F32)
    chunks = sem_out.shape[0]
    each = count // chunks
    stores = []
    for c in range(chunks):
        for b in range(c * each, (c + 1) * each):
            turned[b * tile : (b + 1) * tile, :] = jnp.transpose(total[b]).astype(BF16)
        part = pl.ds(c * each * tile, each * tile)
        stores.append(pltpu.make_async_copy(turned.at[part], out.at[part], sem_out.at[c]))
        stores[-1].start()
    for i in range(hubs.shape[0]):
        row = hubs[i]
        block = jnp.transpose(total[row // tile])
        want = lax.rem(row, tile) // GROUP
        part = jnp.zeros((GROUP, width), F32)
        for g in range(tile // GROUP):
            part = jnp.where(want == g, block[g * GROUP : (g + 1) * GROUP], part)
        near[i] = part
    wait(stores)


def collect(send, hubs, grad, halos):
    count, width, tile = grad.shape
    lists = len(halos)
    near = (hubs.shape[0], GROUP, width)
    return pl.pallas_call(
        collect_kernel,
        out_shape=[
            pltpu.VMEM(grad.shape, F32),
            pltpu.HBM((count * tile, width), BF16),
            pltpu.VMEM(near, F32),
        ],
        in_specs=[HBM_SPEC] * 2 + [VMEM_SPEC] + [ANY_SPEC] * lists,
        out_specs=[VMEM_SPEC, HBM_SPEC, VMEM_SPEC],
        scratch_shapes=[
            pltpu.SMEM(send.shape, jnp.int32),
            pltpu.SMEM(hubs.shape, jnp.int32),
            pltpu.VMEM((lists,) + halos[0].shape, BF16),
            pltpu.VMEM((count * tile, width), BF16),
            pltpu.SemaphoreType.DMA((2 + lists,)),
            pltpu.SemaphoreType.DMA((4,)),
        ],
        input_output_aliases={2: 0},
        compiler_params=params(),
        cost_estimate=pl.CostEstimate(
            flops=grad.size * 8, bytes_accessed=4 << 20, transcendentals=0
        ),
        name="collect",
    )(hbm(send), hbm(hubs), vmem(grad), *halos)[1:]


def finish_kernel(
    hubs_hbm, pieces_hbm, near, _, grad, g_self, g_neigh, g_bias, hubs, pieces, rows, sem_in, sems
):
    owned = hubs.shape[0]
    chunks = sem_in.shape[0] - 1
    each = pieces.shape[0] // chunks
    index = pltpu.make_async_copy(hubs_hbm, hubs, sem_in.at[chunks])
    index.start()
    loads = []
    for c in range(chunks):
        part = pl.ds(c * each, each)
        loads.append(pltpu.make_async_copy(pieces_hbm.at[part], pieces.at[part], sem_in.at[c]))
    start(loads)
    index.wait()
    total = jnp.zeros(pieces.shape[1:], F32)
    for c in range(chunks):
        loads[c].wait()
        total += jnp.sum(pieces[c * each : (c + 1) * each].astype(F32), 0)
    g_self[...] = total[owned : owned + 1, :]
    g_neigh[...] = total[owned + 1 : owned + 2, :]
    last = total[owned + 2 : owned + 3, :]
    g_bias[...] = jnp.broadcast_to(last[:, 0:1] + last[:, 1:2], last.shape)
    place = lax.broadcasted_iota(jnp.int32, (GROUP, total.shape[-1]), 0)
    for i in range(owned):
        value = near[i]
        for m in range(owned):
            same = hubs[m] // GROUP == hubs[i] // GROUP
            hit = jnp.logical_and(place == lax.rem(hubs[m], GROUP), same)
            value = value + jnp.where(hit, total[m : m + 1, :], 0.0)
        rows[i] = value.astype(BF16)

    def fresh(i):
        new = hubs[i] >= 0
        for m in range(i):
            new = jnp.logical_and(new, hubs[m] // GROUP != hubs[i] // GROUP)
        return new

    def move(i):
        base = pl.multiple_of(hubs[i] // GROUP * GROUP, GROUP)
        return pltpu.make_async_copy(rows.at[i], grad.at[pl.ds(base, GROUP), :], sems.at[i])

    for i in range(owned):
        pl.when(fresh(i))(lambda i=i: move(i).start())
    for i in range(owned):
        pl.when(fresh(i))(lambda i=i: move(i).wait())


def finish(hubs, pieces, near, grad):
    owned, _, width = near.shape
    line = jax.ShapeDtypeStruct((1, width), F32)
    return pl.pallas_call(
        finish_kernel,
        out_shape=[pltpu.HBM(grad.shape, grad.dtype), line, line, line],
        in_specs=[HBM_SPEC, ANY_SPEC, VMEM_SPEC, HBM_SPEC],
        out_specs=[HBM_SPEC, VMEM_SPEC, VMEM_SPEC, VMEM_SPEC],
        scratch_shapes=[
            pltpu.SMEM(hubs.shape, jnp.int32),
            pltpu.VMEM(pieces.shape, BF16),
            pltpu.VMEM((owned, GROUP, width), BF16),
            pltpu.SemaphoreType.DMA((5,)),
            pltpu.SemaphoreType.DMA((owned,)),
        ],
        input_output_aliases={3: 0},
        compiler_params=params(),
        name="finish",
    )(hbm(hubs), pieces, vmem(near), hbm(grad))


def shards(
    features,
    local_tiles,
    local_src,
    remote_tiles,
    remote_src,
    send_blocks,
    hub_rows,
    w_self,
    w_neigh,
    bias,
    d_hidden,
):
    parts = lax.axis_size("dom")
    nodes, width = features.shape
    tile = local_tiles.shape[-1]
    owned = hub_rows.shape[0]
    blocks = features.reshape(nodes // tile, tile, width)
    *sends, hub_mine, own = gather_sends(send_blocks, hub_rows, blocks, parts)
    hub_all = lax.all_to_all(hub_mine, "dom", 0, 0)
    halos = [swapped(b, way) for way, b in enumerate(sends)]
    agg_local, d_hid = local_aggregate(local_src.T, local_tiles, d_hidden, own)
    hidden, d_pre, d_agg, *rest = layer(
        remote_src.T,
        remote_tiles,
        features,
        agg_local,
        halos,
        hub_all.reshape(parts * owned // tile, tile, width),
        w_self,
        w_neigh,
        bias[None],
        d_hid,
        parts,
    )
    *backs, packed = rest
    pieces = lax.all_to_all(packed, "dom", 0, 0)
    returned = [swapped(b, way) for way, b in enumerate(backs)]
    grad_t = local_backward(local_src.T, local_tiles, d_pre, d_agg, w_self)
    rough, near = collect(send_blocks, hub_rows, grad_t, returned)
    grad, g_self, g_neigh, g_bias = finish(hub_rows, pieces, near, rough)
    return (hidden, grad, g_self.reshape(width, 1), g_neigh.reshape(width, 1), g_bias[0, :1])


def solution(mesh):
    in_specs = (
        P("dom", None),
        P("dom", None, None, None),
        P("dom", None),
        P("dom", None, None, None),
        P("dom", None),
        P("dom", None),
        P("dom"),
        P(),
        P(),
        P(),
        P("dom", None),
    )
    out_specs = (P("dom", None), P("dom", None), P(None, "dom"), P(None, "dom"), P("dom"))
    return jax.shard_map(shards, mesh=mesh, in_specs=in_specs, out_specs=out_specs, check_vma=False)
```

```python
import functools

import jax
import jax.numpy as jnp
from jax import lax
from jax.experimental import pallas as pl
from jax.experimental.pallas import tpu as pltpu
from jax.sharding import PartitionSpec as P

OFFSETS = (1, -1, 2, -2)
F32 = jnp.float32
BF16 = jnp.bfloat16
NT = (((1,), (1,)), ((), ()))
TN = (((0,), (0,)), ((), ()))
GROUP = 16
CHUNK = 8
STEP = 8


def partner(i, way, n):
    if way == 0:
        return i ^ 1
    if way == 1:
        return (i + (1 if i & 1 else -1)) % n
    ahead = (i >> 1) & 1 == way - 2
    return (i + (2 if ahead else -2)) % n


def swapped(block, way):
    n = lax.axis_size("dom")
    return lax.ppermute(block, "dom", [(i, partner(i, way, n)) for i in range(n)])


def lists_of_ways():
    me = lax.axis_index("dom")
    odd, odd_chip = me & 1, (me >> 1) & 1
    return odd, 1 - odd, 2 + odd_chip, 3 - odd_chip


def rows_of(chunk, size):
    return pl.ds(pl.multiple_of(chunk * size, size), size)


def params():
    return pltpu.CompilerParams(vmem_limit_bytes=40 << 20)


def hbm(x):
    return pltpu.with_memory_space_constraint(x, pltpu.HBM)


def vmem(x):
    return pltpu.with_memory_space_constraint(x, pltpu.VMEM)


ANY_SPEC = pl.BlockSpec(memory_space=pl.ANY)
HBM_SPEC = pl.BlockSpec(memory_space=pltpu.HBM)
VMEM_SPEC = pl.BlockSpec(memory_space=pltpu.VMEM)


def start(copies):
    for c in copies:
        c.start()


def wait(copies):
    for c in copies:
        c.wait()


def whole(shape):
    return pl.BlockSpec(shape, lambda *_: (0,) * len(shape))


def send_kernel(send_hbm, hubs_hbm, blocks_hbm, *refs):
    lists, per_list = send_hbm.shape
    outs, refs = refs[:lists], refs[lists:]
    hub_out, blocks, send, hubs, sem_in, sems = refs
    owned = hubs.shape[0]
    count, tile, width = blocks.shape
    pairs = [(send_hbm, send), (hubs_hbm, hubs)]
    half = count // 2
    for part in (pl.ds(0, half), pl.ds(half, half)):
        pairs.append((blocks_hbm.at[part], blocks.at[part]))
    loads = [pltpu.make_async_copy(*p, sem_in.at[n]) for n, p in enumerate(pairs)]
    start(loads)
    wait(loads)
    moves = []
    for way, j in enumerate(lists_of_ways()):
        for h in range(per_list):
            moves.append(
                pltpu.make_async_copy(
                    blocks.at[send[j, h]], outs[way].at[h], sems.at[way * per_list + h]
                )
            )
    start(moves)
    place = lax.broadcasted_iota(jnp.int32, (GROUP, width), 0)
    rows = []
    for i in range(owned):
        row = hubs[i]
        base = pl.multiple_of(lax.rem(row, tile) // GROUP * GROUP, GROUP)
        near = blocks[row // tile, pl.ds(base, GROUP), :].astype(F32)
        chosen = jnp.where(place == lax.rem(row, GROUP), near, 0.0)
        rows.append(jnp.sum(chosen, 0, keepdims=True))
    hub_out[...] = jnp.broadcast_to(jnp.concatenate(rows, 0).astype(BF16)[None], hub_out.shape)
    wait(moves)


def gather_sends(send, hubs, blocks, parts):
    lists, per_list = send.shape
    _, tile, width = blocks.shape
    return pl.pallas_call(
        send_kernel,
        out_shape=[pltpu.HBM((per_list, tile, width), BF16)] * lists
        + [
            jax.ShapeDtypeStruct((parts, hubs.shape[0], width), BF16),
            pltpu.VMEM(blocks.shape, BF16),
        ],
        in_specs=[HBM_SPEC] * 3,
        out_specs=[HBM_SPEC] * lists + [VMEM_SPEC, VMEM_SPEC],
        scratch_shapes=[
            pltpu.SMEM(send.shape, jnp.int32),
            pltpu.SMEM(hubs.shape, jnp.int32),
            pltpu.SemaphoreType.DMA((4,)),
            pltpu.SemaphoreType.DMA((lists * per_list,)),
        ],
        compiler_params=params(),
        name="sends",
    )(hbm(send), hbm(hubs), hbm(blocks))


def local_kernel(
    src_hbm, tiles_hbm, blocks, agg_hbm, src, tiles, agg, sem, sem_in, sem_out
):
    count, per_block, tile, _ = tiles.shape
    chunks = count // STEP

    def fetch(i):
        part = pl.ds(i * STEP, STEP)
        return pltpu.make_async_copy(tiles_hbm.at[part], tiles.at[part], sem_in.at[i])

    def store(i):
        part = rows_of(i, STEP * tile)
        return pltpu.make_async_copy(agg.at[part], agg_hbm.at[part], sem_out.at[i])

    index = pltpu.make_async_copy(src_hbm, src, sem)
    index.start()
    for i in range(chunks):
        fetch(i).start()
    index.wait()

    @pl.loop(0, chunks)
    def _(i):
        fetch(i).wait()
        for b in range(STEP):
            at = i * STEP + b
            taken = [blocks[src[k, at]] for k in range(per_block)]
            edges = [tiles[at, k] for k in range(per_block)]
            agg[rows_of(at, tile), :] = jnp.dot(
                jnp.concatenate(edges, 1), jnp.concatenate(taken, 0), preferred_element_type=F32
            )
        store(i).start()

    wait([store(i) for i in range(chunks)])


def local_aggregate(src, tiles, blocks):
    count, per_block, tile, _ = tiles.shape
    width = blocks.shape[-1]
    agg = (count * tile, width)
    return pl.pallas_call(
        local_kernel,
        out_shape=pltpu.HBM(agg, F32),
        in_specs=[HBM_SPEC] * 2 + [VMEM_SPEC],
        out_specs=HBM_SPEC,
        scratch_shapes=[
            pltpu.SMEM(src.shape, jnp.int32),
            pltpu.VMEM(tiles.shape, BF16),
            pltpu.VMEM(agg, F32),
            pltpu.SemaphoreType.DMA,
            pltpu.SemaphoreType.DMA((count // STEP,)),
            pltpu.SemaphoreType.DMA((count // STEP,)),
        ],
        compiler_params=params(),
        cost_estimate=pl.CostEstimate(
            flops=2 * tiles.size * width, bytes_accessed=8 << 20, transcendentals=0
        ),
        name="local_aggregate",
    )(hbm(src), hbm(tiles), vmem(blocks))


def layer_kernel(src_hbm, *refs):
    lists = len(OFFSETS)
    tiles_hbm, rows_hbm, agg_hbm, d_hbm = refs[:4]
    halos, refs = refs[4 : 4 + lists], refs[4 + lists :]
    hub, self_hbm, neigh_hbm, bias_hbm, hidden_hbm, d_pre_out, d_agg_hbm = refs[:7]
    backs, refs = refs[7 : 7 + lists], refs[7 + lists :]
    mine, theirs, src, weights, bias, table, rem_grad, backs_out, w_grad, b_grad = refs[:10]
    spread, pack_out, tiles, rows, agg_local, d_hidden, hidden, d_agg_out = refs[10:18]
    sem_t, sem_back, sem_in, sem_out = refs[18:]
    count, per_block, tile, _ = tiles.shape
    width = rows.shape[-1]
    per_list = halos[0].shape[0]
    halo_count = lists * per_list
    hub_blocks = hub.shape[0]
    slots = [j ^ 1 for j in lists_of_ways()]
    pairs = [
        (src_hbm, src),
        (hub, table.at[pl.ds(halo_count, hub_blocks)]),
        (self_hbm, weights.at[pl.ds(0, width)]),
        (neigh_hbm, weights.at[pl.ds(width, width)]),
        (bias_hbm, bias),
    ]
    for w, s in enumerate(slots):
        pairs.append((halos[w], table.at[pl.ds(s * per_list, per_list)]))
    moves = [pltpu.make_async_copy(*p, sem_t.at[n]) for n, p in enumerate(pairs)]
    chunks = count // STEP

    def fetch(i):
        few, many = pl.ds(i * STEP, STEP), rows_of(i, STEP * tile)
        pairs = (
            (tiles_hbm.at[few], tiles.at[few]),
            (agg_hbm.at[many], agg_local.at[many]),
            (rows_hbm.at[many], rows.at[many]),
            (d_hbm.at[many], d_hidden.at[many]),
        )
        return [pltpu.make_async_copy(*p, sem_in.at[i, n]) for n, p in enumerate(pairs)]

    def store(i):
        few, many = pl.ds(i * STEP, STEP), rows_of(i, STEP * tile)
        pairs = (
            (hidden.at[many], hidden_hbm.at[many]),
            (d_agg_out.at[few], d_agg_hbm.at[few]),
        )
        return [pltpu.make_async_copy(*p, sem_out.at[i, n]) for n, p in enumerate(pairs)]

    start(moves)
    for i in range(chunks):
        start(fetch(i))
    rem_grad[...] = jnp.zeros_like(rem_grad)
    w_grad[...] = jnp.zeros_like(w_grad)
    b_grad[...] = jnp.zeros_like(b_grad)
    wait(moves)

    @pl.loop(0, chunks)
    def _(i):
        wait(fetch(i))
        many = rows_of(i, STEP * tile)

        def edges(b):
            return jnp.concatenate([tiles[i * STEP + b, k] for k in range(per_block)], 1)

        sources = [[src[k, i * STEP + b] for k in range(per_block)] for b in range(STEP)]
        remote = [
            jnp.dot(
                edges(b),
                jnp.concatenate([table[s] for s in sources[b]], 0),
                preferred_element_type=F32,
            )
            for b in range(STEP)
        ]
        agg = agg_local[many, :] + jnp.concatenate(remote, 0)
        both = jnp.concatenate([rows[many, :], agg.astype(BF16)], 1)
        pre = jnp.dot(both, weights[...], preferred_element_type=F32) + bias[...]
        sig = jax.nn.sigmoid(pre)
        hidden[many, :] = (pre * sig).astype(BF16)
        d_pre = d_hidden[many, :].astype(F32) * (sig * (1.0 + pre * (1.0 - sig)))
        b_grad[...] += jnp.sum(d_pre.reshape(-1, 8, d_pre.shape[-1]), 0)
        d_pre_b = d_pre.astype(BF16)
        d_pre_out[many, :] = d_pre_b
        d_agg = lax.dot_general(weights[width:, :], d_pre_b, NT, preferred_element_type=F32)
        d_agg = d_agg.astype(BF16)
        for b in range(STEP):
            own = d_agg[:, b * tile : (b + 1) * tile]
            d_agg_out[i * STEP + b] = own
            terms = jnp.dot(own, edges(b), preferred_element_type=F32)
            for k, s in enumerate(sources[b]):
                rem_grad[s] += terms[:, k * tile : (k + 1) * tile]
        start(store(i))
        w_grad[...] += lax.dot_general(d_pre_b, both, TN, preferred_element_type=F32)

    sent = []
    for w, s in enumerate(slots):
        backs_out[w] = rem_grad[pl.ds(s * per_list, per_list)].astype(BF16)
        sent.append(pltpu.make_async_copy(backs_out.at[w], backs[w], sem_back.at[w]))
    start(sent)
    half, chunk, _ = mine.shape
    parts = 2 * half
    owned = hub_blocks * tile // parts
    hub_rows = jnp.concatenate(
        [jnp.transpose(rem_grad[halo_count + q]) for q in range(hub_blocks)], 0
    )
    split = hub_rows.reshape(parts, owned, width)
    for i in range(owned):
        spread[pl.ds(i, parts, stride=chunk), :] = split[:, i, :]
    spread[pl.ds(owned, parts, stride=chunk), :] = w_grad[:, :width]
    spread[pl.ds(owned + 1, parts, stride=chunk), :] = w_grad[:, width:]
    total = jnp.sum(b_grad[...], 0, keepdims=True)
    high = total.astype(BF16).astype(F32)
    lane = lax.broadcasted_iota(jnp.int32, (width, parts), 0)
    two = jnp.where(lane == 0, high, jnp.where(lane == 1, total - high, 0.0))
    spread[pl.ds(owned + 2, parts, stride=chunk), :] = jnp.transpose(two)
    for i in range(owned + 3, chunk):
        spread[pl.ds(i, parts, stride=chunk), :] = jnp.zeros((parts, width), F32)
    by_core = spread[...].reshape(half, 2, chunk, width)
    odd = lists_of_ways()[0] == 1
    pack_out[...] = jnp.where(odd, by_core[:, 0], by_core[:, 1]).astype(BF16)
    last = pltpu.make_async_copy(pack_out, theirs, sem_back.at[lists])
    last.start()
    mine[...] = jnp.where(odd, by_core[:, 1], by_core[:, 0])
    wait(sent)
    for i in range(chunks):
        wait(store(i))
    last.wait()


def layer(src, tiles, rows, agg_local, halos, hub, w_self, w_neigh, bias, d_hidden, parts):
    count, per_block, tile, _ = tiles.shape
    nodes, width = rows.shape
    units = d_hidden.shape[-1]
    lists, per_list = len(halos), halos[0].shape[0]
    table = lists * per_list + hub.shape[0]
    pieces = (parts // 2, CHUNK, width)
    chunks = count // STEP
    return pl.pallas_call(
        layer_kernel,
        out_shape=[
            pltpu.HBM((nodes, units), BF16),
            pltpu.VMEM((nodes, units), BF16),
            pltpu.HBM((count, width, tile), BF16),
        ]
        + [pltpu.HBM((per_list, width, tile), BF16)] * lists
        + [pltpu.VMEM(pieces, F32), pltpu.HBM(pieces, BF16)],
        in_specs=[HBM_SPEC] * 5 + [ANY_SPEC] * (lists + 1) + [HBM_SPEC] * 3,
        out_specs=[HBM_SPEC, VMEM_SPEC] + [HBM_SPEC] * (lists + 1) + [VMEM_SPEC, HBM_SPEC],
        scratch_shapes=[
            pltpu.SMEM(src.shape, jnp.int32),
            pltpu.VMEM((2 * width, units), BF16),
            pltpu.VMEM((1, units), F32),
            pltpu.VMEM((table, tile, width), BF16),
            pltpu.VMEM((table, width, tile), F32),
            pltpu.VMEM((lists, per_list, width, tile), BF16),
            pltpu.VMEM((units, 2 * width), F32),
            pltpu.VMEM((8, units), F32),
            pltpu.VMEM((parts * CHUNK, width), F32),
            pltpu.VMEM(pieces, BF16),
            pltpu.VMEM(tiles.shape, BF16),
            pltpu.VMEM((nodes, width), BF16),
            pltpu.VMEM((nodes, width), F32),
            pltpu.VMEM((nodes, units), BF16),
            pltpu.VMEM((nodes, units), BF16),
            pltpu.VMEM((count, width, tile), BF16),
            pltpu.SemaphoreType.DMA((lists + 5,)),
            pltpu.SemaphoreType.DMA((lists + 1,)),
            pltpu.SemaphoreType.DMA((chunks, 4)),
            pltpu.SemaphoreType.DMA((chunks, 2)),
        ],
        compiler_params=params(),
        cost_estimate=pl.CostEstimate(
            flops=4 * tiles.size * width + 12 * nodes * width * units,
            bytes_accessed=14 << 20,
            transcendentals=nodes * units,
        ),
        name="layer",
    )(
        hbm(src),
        hbm(tiles),
        hbm(rows),
        hbm(agg_local),
        hbm(d_hidden),
        *halos,
        hub,
        hbm(w_self),
        hbm(w_neigh),
        hbm(bias),
    )


def add_kernel(mine, theirs_any, out_hbm, theirs, out, sems):
    load = pltpu.make_async_copy(theirs_any, theirs, sems.at[0])
    load.start()
    load.wait()
    out[...] = (mine[...] + theirs[...].astype(F32)).astype(BF16)
    save = pltpu.make_async_copy(out, out_hbm, sems.at[1])
    save.start()
    save.wait()


def add_pieces(mine, theirs):
    return pl.pallas_call(
        add_kernel,
        out_shape=pltpu.HBM(theirs.shape, BF16),
        in_specs=[VMEM_SPEC, ANY_SPEC],
        out_specs=HBM_SPEC,
        scratch_shapes=[
            pltpu.VMEM(theirs.shape, BF16),
            pltpu.VMEM(theirs.shape, BF16),
            pltpu.SemaphoreType.DMA((2,)),
        ],
        compiler_params=params(),
        name="add_pieces",
    )(vmem(mine), theirs)


def back_kernel(
    src_hbm, weight_hbm, tiles_hbm, d_hbm, d_pre, total, src, weight, tiles, d_agg, sems, sem_in
):
    count, per_block, tile, _ = tiles.shape
    size = STEP * tile

    def fetch(i):
        part = pl.ds(i * STEP, STEP)
        pairs = ((tiles_hbm.at[part], tiles.at[part]), (d_hbm.at[part], d_agg.at[part]))
        return [pltpu.make_async_copy(*p, sem_in.at[i, n]) for n, p in enumerate(pairs)]

    loads = [
        pltpu.make_async_copy(src_hbm, src, sems.at[0]),
        pltpu.make_async_copy(weight_hbm, weight, sems.at[1]),
    ]
    start(loads)
    for i in range(count // STEP):
        start(fetch(i))
    total[...] = jnp.zeros_like(total)
    wait(loads)

    @pl.loop(0, count // STEP)
    def _(i):
        wait(fetch(i))
        own = lax.dot_general(
            weight[...], d_pre[rows_of(i, size), :], NT, preferred_element_type=F32
        )
        for b in range(STEP):
            at = i * STEP + b
            total[at] += own[:, b * tile : (b + 1) * tile]
            edges = jnp.concatenate([tiles[at, k] for k in range(per_block)], 1)
            terms = jnp.dot(d_agg[at], edges, preferred_element_type=F32)
            for k in range(per_block):
                s = src[k, at]
                total[s] += terms[:, k * tile : (k + 1) * tile]


def local_backward(src, tiles, d_pre, d_agg, weight):
    count, per_block, tile, _ = tiles.shape
    width, units = weight.shape
    return pl.pallas_call(
        back_kernel,
        out_shape=pltpu.VMEM((count, width, tile), F32),
        in_specs=[HBM_SPEC] * 4 + [VMEM_SPEC],
        out_specs=VMEM_SPEC,
        scratch_shapes=[
            pltpu.SMEM(src.shape, jnp.int32),
            pltpu.VMEM(weight.shape, BF16),
            pltpu.VMEM(tiles.shape, BF16),
            pltpu.VMEM(d_agg.shape, BF16),
            pltpu.SemaphoreType.DMA((2,)),
            pltpu.SemaphoreType.DMA((count // STEP, 2)),
        ],
        compiler_params=params(),
        cost_estimate=pl.CostEstimate(
            flops=2 * tiles.size * width + 2 * d_pre.size * width,
            bytes_accessed=8 << 20,
            transcendentals=0,
        ),
        name="local_backward",
    )(hbm(src), hbm(weight), hbm(tiles), hbm(d_agg), vmem(d_pre))


def collect_kernel(send_hbm, hubs_hbm, _, *refs):
    lists, per_list = send_hbm.shape
    halos_hbm = refs[:lists]
    total, out, near, send, hubs, halos, turned, sem_in, sem_out = refs[lists:]
    count, width, tile = total.shape
    pairs = [(send_hbm, send), (hubs_hbm, hubs)]
    pairs += [(halos_hbm[way], halos.at[way]) for way in range(lists)]
    loads = [pltpu.make_async_copy(*p, sem_in.at[n]) for n, p in enumerate(pairs)]
    start(loads)
    wait(loads)
    for way, j in enumerate(lists_of_ways()):
        for h in range(per_list):
            total[send[j, h]] += halos[way, h].astype(F32)
    chunks = sem_out.shape[0]
    each = count // chunks
    stores = []
    for c in range(chunks):
        for b in range(c * each, (c + 1) * each):
            turned[b * tile : (b + 1) * tile, :] = jnp.transpose(total[b]).astype(BF16)
        part = pl.ds(c * each * tile, each * tile)
        stores.append(pltpu.make_async_copy(turned.at[part], out.at[part], sem_out.at[c]))
        stores[-1].start()
    for i in range(hubs.shape[0]):
        row = hubs[i]
        block = jnp.transpose(total[row // tile])
        want = lax.rem(row, tile) // GROUP
        part = jnp.zeros((GROUP, width), F32)
        for g in range(tile // GROUP):
            part = jnp.where(want == g, block[g * GROUP : (g + 1) * GROUP], part)
        near[i] = part
    wait(stores)


def collect(send, hubs, grad, halos):
    count, width, tile = grad.shape
    lists = len(halos)
    near = (hubs.shape[0], GROUP, width)
    return pl.pallas_call(
        collect_kernel,
        out_shape=[
            pltpu.VMEM(grad.shape, F32),
            pltpu.HBM((count * tile, width), BF16),
            pltpu.VMEM(near, F32),
        ],
        in_specs=[HBM_SPEC] * 2 + [VMEM_SPEC] + [ANY_SPEC] * lists,
        out_specs=[VMEM_SPEC, HBM_SPEC, VMEM_SPEC],
        scratch_shapes=[
            pltpu.SMEM(send.shape, jnp.int32),
            pltpu.SMEM(hubs.shape, jnp.int32),
            pltpu.VMEM((lists,) + halos[0].shape, BF16),
            pltpu.VMEM((count * tile, width), BF16),
            pltpu.SemaphoreType.DMA((2 + lists,)),
            pltpu.SemaphoreType.DMA((4,)),
        ],
        input_output_aliases={2: 0},
        compiler_params=params(),
        cost_estimate=pl.CostEstimate(
            flops=grad.size * 8, bytes_accessed=4 << 20, transcendentals=0
        ),
        name="collect",
    )(hbm(send), hbm(hubs), vmem(grad), *halos)[1:]


def finish_kernel(
    hubs_hbm, pieces_hbm, near, _, grad, g_self, g_neigh, g_bias, hubs, pieces, rows, sem_in, sems
):
    owned = hubs.shape[0]
    chunks = sem_in.shape[0] - 1
    each = pieces.shape[0] // chunks
    index = pltpu.make_async_copy(hubs_hbm, hubs, sem_in.at[chunks])
    index.start()
    loads = []
    for c in range(chunks):
        part = pl.ds(c * each, each)
        loads.append(pltpu.make_async_copy(pieces_hbm.at[part], pieces.at[part], sem_in.at[c]))
    start(loads)
    index.wait()
    total = jnp.zeros(pieces.shape[1:], F32)
    for c in range(chunks):
        loads[c].wait()
        total += jnp.sum(pieces[c * each : (c + 1) * each].astype(F32), 0)
    g_self[...] = total[owned : owned + 1, :]
    g_neigh[...] = total[owned + 1 : owned + 2, :]
    last = total[owned + 2 : owned + 3, :]
    g_bias[...] = jnp.broadcast_to(last[:, 0:1] + last[:, 1:2], last.shape)
    place = lax.broadcasted_iota(jnp.int32, (GROUP, total.shape[-1]), 0)
    for i in range(owned):
        value = near[i]
        for m in range(owned):
            same = hubs[m] // GROUP == hubs[i] // GROUP
            hit = jnp.logical_and(place == lax.rem(hubs[m], GROUP), same)
            value = value + jnp.where(hit, total[m : m + 1, :], 0.0)
        rows[i] = value.astype(BF16)

    def fresh(i):
        new = hubs[i] >= 0
        for m in range(i):
            new = jnp.logical_and(new, hubs[m] // GROUP != hubs[i] // GROUP)
        return new

    def move(i):
        base = pl.multiple_of(hubs[i] // GROUP * GROUP, GROUP)
        return pltpu.make_async_copy(rows.at[i], grad.at[pl.ds(base, GROUP), :], sems.at[i])

    for i in range(owned):
        pl.when(fresh(i))(lambda i=i: move(i).start())
    for i in range(owned):
        pl.when(fresh(i))(lambda i=i: move(i).wait())


def finish(hubs, pieces, near, grad):
    owned, _, width = near.shape
    line = jax.ShapeDtypeStruct((1, width), F32)
    return pl.pallas_call(
        finish_kernel,
        out_shape=[pltpu.HBM(grad.shape, grad.dtype), line, line, line],
        in_specs=[HBM_SPEC, ANY_SPEC, VMEM_SPEC, HBM_SPEC],
        out_specs=[HBM_SPEC, VMEM_SPEC, VMEM_SPEC, VMEM_SPEC],
        scratch_shapes=[
            pltpu.SMEM(hubs.shape, jnp.int32),
            pltpu.VMEM(pieces.shape, BF16),
            pltpu.VMEM((owned, GROUP, width), BF16),
            pltpu.SemaphoreType.DMA((5,)),
            pltpu.SemaphoreType.DMA((owned,)),
        ],
        input_output_aliases={3: 0},
        compiler_params=params(),
        name="finish",
    )(hbm(hubs), pieces, vmem(near), hbm(grad))


def shards(
    features,
    local_tiles,
    local_src,
    remote_tiles,
    remote_src,
    send_blocks,
    hub_rows,
    w_self,
    w_neigh,
    bias,
    d_hidden,
):
    parts = lax.axis_size("dom")
    nodes, width = features.shape
    tile = local_tiles.shape[-1]
    owned = hub_rows.shape[0]
    blocks = features.reshape(nodes // tile, tile, width)
    *sends, hub_mine, own = gather_sends(send_blocks, hub_rows, blocks, parts)
    hub_all = lax.all_to_all(hub_mine, "dom", 0, 0)
    halos = [swapped(b, way) for way, b in enumerate(sends)]
    agg_local = local_aggregate(local_src.T, local_tiles, own)
    hidden, d_pre, d_agg, *rest = layer(
        remote_src.T,
        remote_tiles,
        features,
        agg_local,
        halos,
        hub_all.reshape(parts * owned // tile, tile, width),
        w_self,
        w_neigh,
        bias[None],
        d_hidden,
        parts,
    )
    *backs, mine, theirs = rest
    packed = add_pieces(mine, swapped(theirs, 0))
    same_core = [list(range(c, parts, 2)) for c in range(2)]
    pieces = lax.all_to_all(packed, "dom", 0, 0, axis_index_groups=same_core)
    returned = [swapped(b, way) for way, b in enumerate(backs)]
    grad_t = local_backward(local_src.T, local_tiles, d_pre, d_agg, w_self)
    rough, near = collect(send_blocks, hub_rows, grad_t, returned)
    grad, g_self, g_neigh, g_bias = finish(hub_rows, pieces, near, rough)
    return (hidden, grad, g_self.reshape(width, 1), g_neigh.reshape(width, 1), g_bias[0, :1])


def solution(mesh):
    in_specs = (
        P("dom", None),
        P("dom", None, None, None),
        P("dom", None),
        P("dom", None, None, None),
        P("dom", None),
        P("dom", None),
        P("dom"),
        P(),
        P(),
        P(),
        P("dom", None),
    )
    out_specs = (P("dom", None), P("dom", None), P(None, "dom"), P(None, "dom"), P("dom"))
    return jax.shard_map(shards, mesh=mesh, in_specs=in_specs, out_specs=out_specs, check_vma=False)
```

```python
import functools

import jax
import jax.numpy as jnp
from jax import lax
from jax.experimental import pallas as pl
from jax.experimental.pallas import tpu as pltpu
from jax.sharding import PartitionSpec as P

OFFSETS = (1, -1, 2, -2)
F32 = jnp.float32
BF16 = jnp.bfloat16
NT = (((1,), (1,)), ((), ()))
TN = (((0,), (0,)), ((), ()))
GROUP = 16
CHUNK = 8
STEP = 8


def partner(i, way, n):
    if way == 0:
        return i ^ 1
    if way == 1:
        return (i + (1 if i & 1 else -1)) % n
    ahead = (i >> 1) & 1 == way - 2
    return (i + (2 if ahead else -2)) % n


def swapped(block, way):
    n = lax.axis_size("dom")
    return lax.ppermute(block, "dom", [(i, partner(i, way, n)) for i in range(n)])


def lists_of_ways():
    me = lax.axis_index("dom")
    odd, odd_chip = me & 1, (me >> 1) & 1
    return odd, 1 - odd, 2 + odd_chip, 3 - odd_chip


def rows_of(chunk, size):
    return pl.ds(pl.multiple_of(chunk * size, size), size)


def params():
    return pltpu.CompilerParams(vmem_limit_bytes=40 << 20)


def hbm(x):
    return pltpu.with_memory_space_constraint(x, pltpu.HBM)


def vmem(x):
    return pltpu.with_memory_space_constraint(x, pltpu.VMEM)


ANY_SPEC = pl.BlockSpec(memory_space=pl.ANY)
HBM_SPEC = pl.BlockSpec(memory_space=pltpu.HBM)
VMEM_SPEC = pl.BlockSpec(memory_space=pltpu.VMEM)


def start(copies):
    for c in copies:
        c.start()


def wait(copies):
    for c in copies:
        c.wait()


def whole(shape):
    return pl.BlockSpec(shape, lambda *_: (0,) * len(shape))


def send_kernel(send_hbm, hubs_hbm, blocks_hbm, *refs):
    lists, per_list = send_hbm.shape
    outs, refs = refs[:lists], refs[lists:]
    hub_out, blocks, send, hubs, sem_in, sems = refs
    owned = hubs.shape[0]
    count, tile, width = blocks.shape
    pairs = [(send_hbm, send), (hubs_hbm, hubs)]
    half = count // 2
    for part in (pl.ds(0, half), pl.ds(half, half)):
        pairs.append((blocks_hbm.at[part], blocks.at[part]))
    loads = [pltpu.make_async_copy(*p, sem_in.at[n]) for n, p in enumerate(pairs)]
    start(loads)
    wait(loads)
    moves = []
    for way, j in enumerate(lists_of_ways()):
        for h in range(per_list):
            moves.append(
                pltpu.make_async_copy(
                    blocks.at[send[j, h]], outs[way].at[h], sems.at[way * per_list + h]
                )
            )
    start(moves)
    place = lax.broadcasted_iota(jnp.int32, (GROUP, width), 0)
    rows = []
    for i in range(owned):
        row = hubs[i]
        base = pl.multiple_of(lax.rem(row, tile) // GROUP * GROUP, GROUP)
        near = blocks[row // tile, pl.ds(base, GROUP), :].astype(F32)
        chosen = jnp.where(place == lax.rem(row, GROUP), near, 0.0)
        rows.append(jnp.sum(chosen, 0, keepdims=True))
    hub_out[...] = jnp.concatenate(rows, 0)
    wait(moves)


def spread_kernel(hub, _, out):
    out[...] = jnp.broadcast_to(hub[...].astype(BF16)[None], out.shape)


def spread_hubs(hub, after, parts):
    return pl.pallas_call(
        spread_kernel,
        out_shape=jax.ShapeDtypeStruct((parts,) + hub.shape, BF16),
        in_specs=[VMEM_SPEC, ANY_SPEC],
        out_specs=VMEM_SPEC,
        compiler_params=params(),
        name="spread_hubs",
    )(hub, after)


def gather_sends(send, hubs, blocks, parts):
    lists, per_list = send.shape
    _, tile, width = blocks.shape
    return pl.pallas_call(
        send_kernel,
        out_shape=[pltpu.HBM((per_list, tile, width), BF16)] * lists
        + [
            pltpu.VMEM((hubs.shape[0], width), F32),
            pltpu.VMEM(blocks.shape, BF16),
        ],
        in_specs=[HBM_SPEC] * 3,
        out_specs=[HBM_SPEC] * lists + [VMEM_SPEC, VMEM_SPEC],
        scratch_shapes=[
            pltpu.SMEM(send.shape, jnp.int32),
            pltpu.SMEM(hubs.shape, jnp.int32),
            pltpu.SemaphoreType.DMA((4,)),
            pltpu.SemaphoreType.DMA((lists * per_list,)),
        ],
        compiler_params=params(),
        name="sends",
    )(hbm(send), hbm(hubs), hbm(blocks))


def local_kernel(
    src_hbm, tiles_hbm, blocks, agg_hbm, src, tiles, agg, sem, sem_in, sem_out
):
    count, per_block, tile, _ = tiles.shape
    chunks = count // STEP

    def fetch(i):
        part = pl.ds(i * STEP, STEP)
        return pltpu.make_async_copy(tiles_hbm.at[part], tiles.at[part], sem_in.at[i])

    def store(i):
        part = rows_of(i, STEP * tile)
        return pltpu.make_async_copy(agg.at[part], agg_hbm.at[part], sem_out.at[i])

    index = pltpu.make_async_copy(src_hbm, src, sem)
    index.start()
    for i in range(chunks):
        fetch(i).start()
    index.wait()

    @pl.loop(0, chunks)
    def _(i):
        fetch(i).wait()
        for b in range(STEP):
            at = i * STEP + b
            taken = [blocks[src[k, at]] for k in range(per_block)]
            edges = [tiles[at, k] for k in range(per_block)]
            agg[rows_of(at, tile), :] = jnp.dot(
                jnp.concatenate(edges, 1), jnp.concatenate(taken, 0), preferred_element_type=F32
            )
        store(i).start()

    wait([store(i) for i in range(chunks)])


def local_aggregate(src, tiles, blocks):
    count, per_block, tile, _ = tiles.shape
    width = blocks.shape[-1]
    agg = (count * tile, width)
    return pl.pallas_call(
        local_kernel,
        out_shape=pltpu.HBM(agg, F32),
        in_specs=[HBM_SPEC] * 2 + [VMEM_SPEC],
        out_specs=HBM_SPEC,
        scratch_shapes=[
            pltpu.SMEM(src.shape, jnp.int32),
            pltpu.VMEM(tiles.shape, BF16),
            pltpu.VMEM(agg, F32),
            pltpu.SemaphoreType.DMA,
            pltpu.SemaphoreType.DMA((count // STEP,)),
            pltpu.SemaphoreType.DMA((count // STEP,)),
        ],
        compiler_params=params(),
        cost_estimate=pl.CostEstimate(
            flops=10**10, bytes_accessed=64 << 20, transcendentals=0
        ),
        name="local_aggregate",
    )(hbm(src), hbm(tiles), vmem(blocks))


def layer_kernel(src_hbm, *refs):
    lists = len(OFFSETS)
    tiles_hbm, rows_hbm, agg_hbm, d_hbm = refs[:4]
    halos, refs = refs[4 : 4 + lists], refs[4 + lists :]
    hub, self_hbm, neigh_hbm, bias_hbm, hidden_hbm, d_pre_out, d_agg_hbm = refs[:7]
    backs, refs = refs[7 : 7 + lists], refs[7 + lists :]
    mine, theirs, src, weights, bias, table, rem_grad, backs_out, w_grad, b_grad = refs[:10]
    spread, pack_out, tiles, rows, agg_local, d_hidden, hidden, d_agg_out = refs[10:18]
    sem_t, sem_back, sem_in, sem_out = refs[18:]
    count, per_block, tile, _ = tiles.shape
    width = rows.shape[-1]
    per_list = halos[0].shape[0]
    halo_count = lists * per_list
    hub_blocks = hub.shape[0]
    slots = [j ^ 1 for j in lists_of_ways()]
    pairs = [
        (src_hbm, src),
        (hub, table.at[pl.ds(halo_count, hub_blocks)]),
        (self_hbm, weights.at[pl.ds(0, width)]),
        (neigh_hbm, weights.at[pl.ds(width, width)]),
        (bias_hbm, bias),
    ]
    for w, s in enumerate(slots):
        pairs.append((halos[w], table.at[pl.ds(s * per_list, per_list)]))
    moves = [pltpu.make_async_copy(*p, sem_t.at[n]) for n, p in enumerate(pairs)]
    chunks = count // STEP

    def fetch(i):
        few, many = pl.ds(i * STEP, STEP), rows_of(i, STEP * tile)
        pairs = (
            (tiles_hbm.at[few], tiles.at[few]),
            (agg_hbm.at[many], agg_local.at[many]),
            (rows_hbm.at[many], rows.at[many]),
            (d_hbm.at[many], d_hidden.at[many]),
        )
        return [pltpu.make_async_copy(*p, sem_in.at[i, n]) for n, p in enumerate(pairs)]

    def store(i):
        few, many = pl.ds(i * STEP, STEP), rows_of(i, STEP * tile)
        pairs = (
            (hidden.at[many], hidden_hbm.at[many]),
            (d_agg_out.at[few], d_agg_hbm.at[few]),
        )
        return [pltpu.make_async_copy(*p, sem_out.at[i, n]) for n, p in enumerate(pairs)]

    start(moves)
    for i in range(chunks):
        start(fetch(i))
    rem_grad[...] = jnp.zeros_like(rem_grad)
    w_grad[...] = jnp.zeros_like(w_grad)
    b_grad[...] = jnp.zeros_like(b_grad)
    wait(moves)

    @pl.loop(0, chunks)
    def _(i):
        wait(fetch(i))
        many = rows_of(i, STEP * tile)

        def edges(b):
            return jnp.concatenate([tiles[i * STEP + b, k] for k in range(per_block)], 1)

        sources = [[src[k, i * STEP + b] for k in range(per_block)] for b in range(STEP)]
        remote = [
            jnp.dot(
                edges(b),
                jnp.concatenate([table[s] for s in sources[b]], 0),
                preferred_element_type=F32,
            )
            for b in range(STEP)
        ]
        agg = agg_local[many, :] + jnp.concatenate(remote, 0)
        both = jnp.concatenate([rows[many, :], agg.astype(BF16)], 1)
        pre = jnp.dot(both, weights[...], preferred_element_type=F32) + bias[...]
        sig = jax.nn.sigmoid(pre)
        hidden[many, :] = (pre * sig).astype(BF16)
        d_pre = d_hidden[many, :].astype(F32) * (sig * (1.0 + pre * (1.0 - sig)))
        b_grad[...] += jnp.sum(d_pre.reshape(-1, 8, d_pre.shape[-1]), 0)
        d_pre_b = d_pre.astype(BF16)
        d_pre_out[many, :] = d_pre_b
        d_agg = lax.dot_general(weights[width:, :], d_pre_b, NT, preferred_element_type=F32)
        d_agg = d_agg.astype(BF16)
        for b in range(STEP):
            own = d_agg[:, b * tile : (b + 1) * tile]
            d_agg_out[i * STEP + b] = own
            terms = jnp.dot(own, edges(b), preferred_element_type=F32)
            for k, s in enumerate(sources[b]):
                rem_grad[s] += terms[:, k * tile : (k + 1) * tile]
        start(store(i))
        w_grad[...] += lax.dot_general(d_pre_b, both, TN, preferred_element_type=F32)

    sent = []
    for w, s in enumerate(slots):
        backs_out[w] = rem_grad[pl.ds(s * per_list, per_list)].astype(BF16)
        sent.append(pltpu.make_async_copy(backs_out.at[w], backs[w], sem_back.at[w]))
    start(sent)
    half, chunk, _ = mine.shape
    parts = 2 * half
    owned = hub_blocks * tile // parts
    hub_rows = jnp.concatenate(
        [jnp.transpose(rem_grad[halo_count + q]) for q in range(hub_blocks)], 0
    )
    split = hub_rows.reshape(parts, owned, width)
    for i in range(owned):
        spread[pl.ds(i, parts, stride=chunk), :] = split[:, i, :]
    spread[pl.ds(owned, parts, stride=chunk), :] = w_grad[:, :width]
    spread[pl.ds(owned + 1, parts, stride=chunk), :] = w_grad[:, width:]
    total = jnp.sum(b_grad[...], 0, keepdims=True)
    high = total.astype(BF16).astype(F32)
    lane = lax.broadcasted_iota(jnp.int32, (width, parts), 0)
    two = jnp.where(lane == 0, high, jnp.where(lane == 1, total - high, 0.0))
    spread[pl.ds(owned + 2, parts, stride=chunk), :] = jnp.transpose(two)
    for i in range(owned + 3, chunk):
        spread[pl.ds(i, parts, stride=chunk), :] = jnp.zeros((parts, width), F32)
    by_core = spread[...].reshape(half, 2, chunk, width)
    odd = lists_of_ways()[0] == 1
    pack_out[...] = jnp.where(odd, by_core[:, 0], by_core[:, 1]).astype(BF16)
    last = pltpu.make_async_copy(pack_out, theirs, sem_back.at[lists])
    last.start()
    mine[...] = jnp.where(odd, by_core[:, 1], by_core[:, 0])
    wait(sent)
    for i in range(chunks):
        wait(store(i))
    last.wait()


def layer(src, tiles, rows, agg_local, halos, hub, w_self, w_neigh, bias, d_hidden, parts):
    count, per_block, tile, _ = tiles.shape
    nodes, width = rows.shape
    units = d_hidden.shape[-1]
    lists, per_list = len(halos), halos[0].shape[0]
    table = lists * per_list + hub.shape[0]
    pieces = (parts // 2, CHUNK, width)
    chunks = count // STEP
    return pl.pallas_call(
        layer_kernel,
        out_shape=[
            pltpu.HBM((nodes, units), BF16),
            pltpu.VMEM((nodes, units), BF16),
            pltpu.HBM((count, width, tile), BF16),
        ]
        + [pltpu.HBM((per_list, width, tile), BF16)] * lists
        + [pltpu.VMEM(pieces, F32), pltpu.HBM(pieces, BF16)],
        in_specs=[HBM_SPEC] * 5 + [ANY_SPEC] * (lists + 1) + [HBM_SPEC] * 3,
        out_specs=[HBM_SPEC, VMEM_SPEC] + [HBM_SPEC] * (lists + 1) + [VMEM_SPEC, HBM_SPEC],
        scratch_shapes=[
            pltpu.SMEM(src.shape, jnp.int32),
            pltpu.VMEM((2 * width, units), BF16),
            pltpu.VMEM((1, units), F32),
            pltpu.VMEM((table, tile, width), BF16),
            pltpu.VMEM((table, width, tile), F32),
            pltpu.VMEM((lists, per_list, width, tile), BF16),
            pltpu.VMEM((units, 2 * width), F32),
            pltpu.VMEM((8, units), F32),
            pltpu.VMEM((parts * CHUNK, width), F32),
            pltpu.VMEM(pieces, BF16),
            pltpu.VMEM(tiles.shape, BF16),
            pltpu.VMEM((nodes, width), BF16),
            pltpu.VMEM((nodes, width), F32),
            pltpu.VMEM((nodes, units), BF16),
            pltpu.VMEM((nodes, units), BF16),
            pltpu.VMEM((count, width, tile), BF16),
            pltpu.SemaphoreType.DMA((lists + 5,)),
            pltpu.SemaphoreType.DMA((lists + 1,)),
            pltpu.SemaphoreType.DMA((chunks, 4)),
            pltpu.SemaphoreType.DMA((chunks, 2)),
        ],
        compiler_params=params(),
        cost_estimate=pl.CostEstimate(
            flops=4 * tiles.size * width + 12 * nodes * width * units,
            bytes_accessed=14 << 20,
            transcendentals=nodes * units,
        ),
        name="layer",
    )(
        hbm(src),
        hbm(tiles),
        hbm(rows),
        hbm(agg_local),
        hbm(d_hidden),
        *halos,
        hub,
        hbm(w_self),
        hbm(w_neigh),
        hbm(bias),
    )


def add_kernel(mine, theirs_any, out_hbm, theirs, out, sems):
    load = pltpu.make_async_copy(theirs_any, theirs, sems.at[0])
    load.start()
    load.wait()
    out[...] = (mine[...] + theirs[...].astype(F32)).astype(BF16)
    save = pltpu.make_async_copy(out, out_hbm, sems.at[1])
    save.start()
    save.wait()


def add_pieces(mine, theirs):
    return pl.pallas_call(
        add_kernel,
        out_shape=pltpu.HBM(theirs.shape, BF16),
        in_specs=[VMEM_SPEC, ANY_SPEC],
        out_specs=HBM_SPEC,
        scratch_shapes=[
            pltpu.VMEM(theirs.shape, BF16),
            pltpu.VMEM(theirs.shape, BF16),
            pltpu.SemaphoreType.DMA((2,)),
        ],
        compiler_params=params(),
        name="add_pieces",
    )(vmem(mine), theirs)


def back_kernel(
    src_hbm, weight_hbm, tiles_hbm, d_hbm, d_pre, total, src, weight, tiles, d_agg, sems, sem_in
):
    count, per_block, tile, _ = tiles.shape
    size = STEP * tile

    def fetch(i):
        part = pl.ds(i * STEP, STEP)
        pairs = ((tiles_hbm.at[part], tiles.at[part]), (d_hbm.at[part], d_agg.at[part]))
        return [pltpu.make_async_copy(*p, sem_in.at[i, n]) for n, p in enumerate(pairs)]

    loads = [
        pltpu.make_async_copy(src_hbm, src, sems.at[0]),
        pltpu.make_async_copy(weight_hbm, weight, sems.at[1]),
    ]
    start(loads)
    for i in range(count // STEP):
        start(fetch(i))
    total[...] = jnp.zeros_like(total)
    wait(loads)

    @pl.loop(0, count // STEP)
    def _(i):
        wait(fetch(i))
        own = lax.dot_general(
            weight[...], d_pre[rows_of(i, size), :], NT, preferred_element_type=F32
        )
        for b in range(STEP):
            at = i * STEP + b
            total[at] += own[:, b * tile : (b + 1) * tile]
            edges = jnp.concatenate([tiles[at, k] for k in range(per_block)], 1)
            terms = jnp.dot(d_agg[at], edges, preferred_element_type=F32)
            for k in range(per_block):
                s = src[k, at]
                total[s] += terms[:, k * tile : (k + 1) * tile]


def local_backward(src, tiles, d_pre, d_agg, weight):
    count, per_block, tile, _ = tiles.shape
    width, units = weight.shape
    return pl.pallas_call(
        back_kernel,
        out_shape=pltpu.VMEM((count, width, tile), F32),
        in_specs=[HBM_SPEC] * 4 + [VMEM_SPEC],
        out_specs=VMEM_SPEC,
        scratch_shapes=[
            pltpu.SMEM(src.shape, jnp.int32),
            pltpu.VMEM(weight.shape, BF16),
            pltpu.VMEM(tiles.shape, BF16),
            pltpu.VMEM(d_agg.shape, BF16),
            pltpu.SemaphoreType.DMA((2,)),
            pltpu.SemaphoreType.DMA((count // STEP, 2)),
        ],
        compiler_params=params(),
        cost_estimate=pl.CostEstimate(
            flops=10**10, bytes_accessed=64 << 20, transcendentals=0
        ),
        name="local_backward",
    )(hbm(src), hbm(weight), hbm(tiles), hbm(d_agg), vmem(d_pre))


def collect_kernel(send_hbm, hubs_hbm, _, *refs):
    lists, per_list = send_hbm.shape
    halos_hbm = refs[:lists]
    total, out, near, send, hubs, halos, turned, sem_in, sem_out = refs[lists:]
    count, width, tile = total.shape
    pairs = [(send_hbm, send), (hubs_hbm, hubs)]
    pairs += [(halos_hbm[way], halos.at[way]) for way in range(lists)]
    loads = [pltpu.make_async_copy(*p, sem_in.at[n]) for n, p in enumerate(pairs)]
    start(loads)
    wait(loads)
    for way, j in enumerate(lists_of_ways()):
        for h in range(per_list):
            total[send[j, h]] += halos[way, h].astype(F32)
    chunks = sem_out.shape[0]
    each = count // chunks
    stores = []
    for c in range(chunks):
        for b in range(c * each, (c + 1) * each):
            turned[b * tile : (b + 1) * tile, :] = jnp.transpose(total[b]).astype(BF16)
        part = pl.ds(c * each * tile, each * tile)
        stores.append(pltpu.make_async_copy(turned.at[part], out.at[part], sem_out.at[c]))
        stores[-1].start()
    for i in range(hubs.shape[0]):
        row = hubs[i]
        block = jnp.transpose(total[row // tile])
        want = lax.rem(row, tile) // GROUP
        part = jnp.zeros((GROUP, width), F32)
        for g in range(tile // GROUP):
            part = jnp.where(want == g, block[g * GROUP : (g + 1) * GROUP], part)
        near[i] = part
    wait(stores)


def collect(send, hubs, grad, halos):
    count, width, tile = grad.shape
    lists = len(halos)
    near = (hubs.shape[0], GROUP, width)
    return pl.pallas_call(
        collect_kernel,
        out_shape=[
            pltpu.VMEM(grad.shape, F32),
            pltpu.HBM((count * tile, width), BF16),
            pltpu.VMEM(near, F32),
        ],
        in_specs=[HBM_SPEC] * 2 + [VMEM_SPEC] + [ANY_SPEC] * lists,
        out_specs=[VMEM_SPEC, HBM_SPEC, VMEM_SPEC],
        scratch_shapes=[
            pltpu.SMEM(send.shape, jnp.int32),
            pltpu.SMEM(hubs.shape, jnp.int32),
            pltpu.VMEM((lists,) + halos[0].shape, BF16),
            pltpu.VMEM((count * tile, width), BF16),
            pltpu.SemaphoreType.DMA((2 + lists,)),
            pltpu.SemaphoreType.DMA((4,)),
        ],
        input_output_aliases={2: 0},
        compiler_params=params(),
        cost_estimate=pl.CostEstimate(
            flops=grad.size * 8, bytes_accessed=4 << 20, transcendentals=0
        ),
        name="collect",
    )(hbm(send), hbm(hubs), vmem(grad), *halos)[1:]


def finish_kernel(
    hubs_hbm, pieces_hbm, near, _, grad, g_self, g_neigh, g_bias, hubs, pieces, rows, sem_in, sems
):
    owned = hubs.shape[0]
    chunks = sem_in.shape[0] - 1
    each = pieces.shape[0] // chunks
    index = pltpu.make_async_copy(hubs_hbm, hubs, sem_in.at[chunks])
    index.start()
    loads = []
    for c in range(chunks):
        part = pl.ds(c * each, each)
        loads.append(pltpu.make_async_copy(pieces_hbm.at[part], pieces.at[part], sem_in.at[c]))
    start(loads)
    index.wait()
    total = jnp.zeros(pieces.shape[1:], F32)
    for c in range(chunks):
        loads[c].wait()
        total += jnp.sum(pieces[c * each : (c + 1) * each].astype(F32), 0)
    g_self[...] = total[owned : owned + 1, :]
    g_neigh[...] = total[owned + 1 : owned + 2, :]
    last = total[owned + 2 : owned + 3, :]
    g_bias[...] = jnp.broadcast_to(last[:, 0:1] + last[:, 1:2], last.shape)
    place = lax.broadcasted_iota(jnp.int32, (GROUP, total.shape[-1]), 0)
    for i in range(owned):
        value = near[i]
        for m in range(owned):
            same = hubs[m] // GROUP == hubs[i] // GROUP
            hit = jnp.logical_and(place == lax.rem(hubs[m], GROUP), same)
            value = value + jnp.where(hit, total[m : m + 1, :], 0.0)
        rows[i] = value.astype(BF16)

    def fresh(i):
        new = hubs[i] >= 0
        for m in range(i):
            new = jnp.logical_and(new, hubs[m] // GROUP != hubs[i] // GROUP)
        return new

    def move(i):
        base = pl.multiple_of(hubs[i] // GROUP * GROUP, GROUP)
        return pltpu.make_async_copy(rows.at[i], grad.at[pl.ds(base, GROUP), :], sems.at[i])

    for i in range(owned):
        pl.when(fresh(i))(lambda i=i: move(i).start())
    for i in range(owned):
        pl.when(fresh(i))(lambda i=i: move(i).wait())


def finish(hubs, pieces, near, grad):
    owned, _, width = near.shape
    line = jax.ShapeDtypeStruct((1, width), F32)
    return pl.pallas_call(
        finish_kernel,
        out_shape=[pltpu.HBM(grad.shape, grad.dtype), line, line, line],
        in_specs=[HBM_SPEC, ANY_SPEC, VMEM_SPEC, HBM_SPEC],
        out_specs=[HBM_SPEC, VMEM_SPEC, VMEM_SPEC, VMEM_SPEC],
        scratch_shapes=[
            pltpu.SMEM(hubs.shape, jnp.int32),
            pltpu.VMEM(pieces.shape, BF16),
            pltpu.VMEM((owned, GROUP, width), BF16),
            pltpu.SemaphoreType.DMA((5,)),
            pltpu.SemaphoreType.DMA((owned,)),
        ],
        input_output_aliases={3: 0},
        compiler_params=params(),
        name="finish",
    )(hbm(hubs), pieces, vmem(near), hbm(grad))


def shards(
    features,
    local_tiles,
    local_src,
    remote_tiles,
    remote_src,
    send_blocks,
    hub_rows,
    w_self,
    w_neigh,
    bias,
    d_hidden,
):
    parts = lax.axis_size("dom")
    nodes, width = features.shape
    tile = local_tiles.shape[-1]
    owned = hub_rows.shape[0]
    blocks = features.reshape(nodes // tile, tile, width)
    *sends, hub_mine, own = gather_sends(send_blocks, hub_rows, blocks, parts)
    halos = [swapped(b, way) for way, b in enumerate(sends)]
    hub_all = lax.all_to_all(spread_hubs(vmem(hub_mine), halos[0], parts), "dom", 0, 0)
    agg_local = local_aggregate(local_src.T, local_tiles, own)
    hidden, d_pre, d_agg, *rest = layer(
        remote_src.T,
        remote_tiles,
        features,
        agg_local,
        halos,
        hub_all.reshape(parts * owned // tile, tile, width),
        w_self,
        w_neigh,
        bias[None],
        d_hidden,
        parts,
    )
    *backs, mine, theirs = rest
    packed = add_pieces(mine, swapped(theirs, 0))
    same_core = [list(range(c, parts, 2)) for c in range(2)]
    pieces = lax.all_to_all(packed, "dom", 0, 0, axis_index_groups=same_core)
    returned = [swapped(b, way) for way, b in enumerate(backs)]
    grad_t = local_backward(local_src.T, local_tiles, d_pre, d_agg, w_self)
    rough, near = collect(send_blocks, hub_rows, grad_t, returned)
    grad, g_self, g_neigh, g_bias = finish(hub_rows, pieces, near, rough)
    return (hidden, grad, g_self.reshape(width, 1), g_neigh.reshape(width, 1), g_bias[0, :1])


def solution(mesh):
    in_specs = (
        P("dom", None),
        P("dom", None, None, None),
        P("dom", None),
        P("dom", None, None, None),
        P("dom", None),
        P("dom", None),
        P("dom"),
        P(),
        P(),
        P(),
        P("dom", None),
    )
    out_specs = (P("dom", None), P("dom", None), P(None, "dom"), P(None, "dom"), P("dom"))
    return jax.shard_map(shards, mesh=mesh, in_specs=in_specs, out_specs=out_specs, check_vma=False)
```

```python
import functools

import jax
import jax.numpy as jnp
from jax import lax
from jax.experimental import pallas as pl
from jax.experimental.pallas import tpu as pltpu
from jax.sharding import PartitionSpec as P

OFFSETS = (1, -1, 2, -2)
F32 = jnp.float32
BF16 = jnp.bfloat16
NT = (((1,), (1,)), ((), ()))
TN = (((0,), (0,)), ((), ()))
GROUP = 16
CHUNK = 8
STEP = 8


QUAD = 4


def partner(i, way, n):
    if way == 0:
        return i ^ 1
    if way == 4:
        return i ^ 3
    if way == 1:
        return (i + (1 if i & 1 else -1)) % n
    ahead = (i >> 1) & 1 == way - 2
    return (i + (2 if ahead else -2)) % n


def swapped(block, way):
    n = lax.axis_size("dom")
    return lax.ppermute(block, "dom", [(i, partner(i, way, n)) for i in range(n)])


def lists_of_ways():
    me = lax.axis_index("dom")
    odd, odd_chip = me & 1, (me >> 1) & 1
    return odd, 1 - odd, 2 + odd_chip, 3 - odd_chip


SHARING = (0, 2, 4)


def same_place(n):
    return [list(range(c, n, QUAD)) for c in range(QUAD)]


def rows_of(chunk, size):
    return pl.ds(pl.multiple_of(chunk * size, size), size)


def params():
    return pltpu.CompilerParams(vmem_limit_bytes=40 << 20)


def hbm(x):
    return pltpu.with_memory_space_constraint(x, pltpu.HBM)


def vmem(x):
    return pltpu.with_memory_space_constraint(x, pltpu.VMEM)


ANY_SPEC = pl.BlockSpec(memory_space=pl.ANY)
HBM_SPEC = pl.BlockSpec(memory_space=pltpu.HBM)
VMEM_SPEC = pl.BlockSpec(memory_space=pltpu.VMEM)


def start(copies):
    for c in copies:
        c.start()


def wait(copies):
    for c in copies:
        c.wait()


def whole(shape):
    return pl.BlockSpec(shape, lambda *_: (0,) * len(shape))


def send_kernel(send_hbm, hubs_hbm, blocks_hbm, *refs):
    lists, per_list = send_hbm.shape
    outs, refs = refs[:lists], refs[lists:]
    hub_out, blocks, send, hubs, sem_in, sems = refs
    owned = hubs.shape[0]
    count, tile, width = blocks.shape
    pairs = [(send_hbm, send), (hubs_hbm, hubs)]
    half = count // 2
    for part in (pl.ds(0, half), pl.ds(half, half)):
        pairs.append((blocks_hbm.at[part], blocks.at[part]))
    loads = [pltpu.make_async_copy(*p, sem_in.at[n]) for n, p in enumerate(pairs)]
    start(loads)
    wait(loads)
    moves = []
    for way, j in enumerate(lists_of_ways()):
        for h in range(per_list):
            moves.append(
                pltpu.make_async_copy(
                    blocks.at[send[j, h]], outs[way].at[h], sems.at[way * per_list + h]
                )
            )
    start(moves)
    place = lax.broadcasted_iota(jnp.int32, (GROUP, width), 0)
    rows = []
    for i in range(owned):
        row = hubs[i]
        base = pl.multiple_of(lax.rem(row, tile) // GROUP * GROUP, GROUP)
        near = blocks[row // tile, pl.ds(base, GROUP), :].astype(F32)
        chosen = jnp.where(place == lax.rem(row, GROUP), near, 0.0)
        rows.append(jnp.sum(chosen, 0, keepdims=True))
    hub_out[...] = jnp.concatenate(rows, 0)
    wait(moves)


def spread_kernel(hub, _, out):
    out[...] = jnp.broadcast_to(hub[...].astype(BF16)[None], out.shape)


def spread_hubs(hub, after, parts):
    return pl.pallas_call(
        spread_kernel,
        out_shape=jax.ShapeDtypeStruct((parts,) + hub.shape, BF16),
        in_specs=[VMEM_SPEC, ANY_SPEC],
        out_specs=VMEM_SPEC,
        compiler_params=params(),
        name="spread_hubs",
    )(hub, after)


def gather_sends(send, hubs, blocks, parts):
    lists, per_list = send.shape
    _, tile, width = blocks.shape
    return pl.pallas_call(
        send_kernel,
        out_shape=[pltpu.HBM((per_list, tile, width), BF16)] * lists
        + [
            pltpu.VMEM((hubs.shape[0], width), F32),
            pltpu.VMEM(blocks.shape, BF16),
        ],
        in_specs=[HBM_SPEC] * 3,
        out_specs=[HBM_SPEC] * lists + [VMEM_SPEC, VMEM_SPEC],
        scratch_shapes=[
            pltpu.SMEM(send.shape, jnp.int32),
            pltpu.SMEM(hubs.shape, jnp.int32),
            pltpu.SemaphoreType.DMA((4,)),
            pltpu.SemaphoreType.DMA((lists * per_list,)),
        ],
        compiler_params=params(),
        name="sends",
    )(hbm(send), hbm(hubs), hbm(blocks))


def local_kernel(
    src_hbm, tiles_hbm, blocks, agg_hbm, src, tiles, agg, sem, sem_in, sem_out
):
    count, per_block, tile, _ = tiles.shape
    chunks = count // STEP

    def fetch(i):
        part = pl.ds(i * STEP, STEP)
        return pltpu.make_async_copy(tiles_hbm.at[part], tiles.at[part], sem_in.at[i])

    def store(i):
        part = rows_of(i, STEP * tile)
        return pltpu.make_async_copy(agg.at[part], agg_hbm.at[part], sem_out.at[i])

    index = pltpu.make_async_copy(src_hbm, src, sem)
    index.start()
    for i in range(chunks):
        fetch(i).start()
    index.wait()

    @pl.loop(0, chunks)
    def _(i):
        fetch(i).wait()
        for b in range(STEP):
            at = i * STEP + b
            taken = [blocks[src[k, at]] for k in range(per_block)]
            edges = [tiles[at, k] for k in range(per_block)]
            agg[rows_of(at, tile), :] = jnp.dot(
                jnp.concatenate(edges, 1), jnp.concatenate(taken, 0), preferred_element_type=F32
            )
        store(i).start()

    wait([store(i) for i in range(chunks)])


def local_aggregate(src, tiles, blocks):
    count, per_block, tile, _ = tiles.shape
    width = blocks.shape[-1]
    agg = (count * tile, width)
    return pl.pallas_call(
        local_kernel,
        out_shape=pltpu.HBM(agg, F32),
        in_specs=[HBM_SPEC] * 2 + [VMEM_SPEC],
        out_specs=HBM_SPEC,
        scratch_shapes=[
            pltpu.SMEM(src.shape, jnp.int32),
            pltpu.VMEM(tiles.shape, BF16),
            pltpu.VMEM(agg, F32),
            pltpu.SemaphoreType.DMA,
            pltpu.SemaphoreType.DMA((count // STEP,)),
            pltpu.SemaphoreType.DMA((count // STEP,)),
        ],
        compiler_params=params(),
        cost_estimate=pl.CostEstimate(
            flops=10**10, bytes_accessed=64 << 20, transcendentals=0
        ),
        name="local_aggregate",
    )(hbm(src), hbm(tiles), vmem(blocks))


def layer_kernel(src_hbm, *refs):
    lists = len(OFFSETS)
    tiles_hbm, rows_hbm, agg_hbm, d_hbm = refs[:4]
    halos, refs = refs[4 : 4 + lists], refs[4 + lists :]
    hubs, refs = refs[:QUAD], refs[QUAD:]
    self_hbm, neigh_hbm, bias_hbm, hidden_hbm, d_pre_out, d_agg_hbm = refs[:6]
    backs, mine, refs = refs[6 : 6 + lists], refs[6 + lists], refs[7 + lists :]
    theirs, refs = refs[: QUAD - 1], refs[QUAD - 1 :]
    hubs_in, hubs_f32, hub_rows = refs[:3]
    refs = refs[3:]
    src, weights, bias, table, rem_grad, backs_out, w_grad, b_grad = refs[:8]
    w_self_grad, w_neigh_grad, b_rows = refs[8:11]
    refs = refs[11:]
    spread, pack_out, tiles, rows, agg_local, d_hidden, hidden, d_agg_out = refs[:8]
    sem_t, sem_back, sem_in, sem_out = refs[8:]
    count, per_block, tile, _ = tiles.shape
    width = rows.shape[-1]
    per_list = halos[0].shape[0]
    halo_count = lists * per_list
    hub_blocks = table.shape[0] - halo_count
    place = lax.axis_index("dom") % QUAD
    slots = [j ^ 1 for j in lists_of_ways()]
    pairs = [
        (src_hbm, src),
        (self_hbm, weights.at[pl.ds(0, width)]),
        (neigh_hbm, weights.at[pl.ds(width, width)]),
        (bias_hbm, bias),
    ]
    for w, s in enumerate(slots):
        pairs.append((halos[w], table.at[pl.ds(s * per_list, per_list)]))
    for x in range(QUAD):
        pairs.append((hubs[x], hubs_in.at[place ^ x]))
    moves = [pltpu.make_async_copy(*p, sem_t.at[n]) for n, p in enumerate(pairs)]
    chunks = count // STEP

    def fetch(i):
        few, many = pl.ds(i * STEP, STEP), rows_of(i, STEP * tile)
        pairs = (
            (tiles_hbm.at[few], tiles.at[few]),
            (agg_hbm.at[many], agg_local.at[many]),
            (rows_hbm.at[many], rows.at[many]),
            (d_hbm.at[many], d_hidden.at[many]),
        )
        return [pltpu.make_async_copy(*p, sem_in.at[i, n]) for n, p in enumerate(pairs)]

    def store(i):
        few, many = pl.ds(i * STEP, STEP), rows_of(i, STEP * tile)
        pairs = (
            (hidden.at[many], hidden_hbm.at[many]),
            (d_agg_out.at[few], d_agg_hbm.at[few]),
        )
        return [pltpu.make_async_copy(*p, sem_out.at[i, n]) for n, p in enumerate(pairs)]

    start(moves)
    for i in range(chunks):
        start(fetch(i))
    rem_grad[...] = jnp.zeros_like(rem_grad)
    w_grad[...] = jnp.zeros_like(w_grad)
    b_grad[...] = jnp.zeros_like(b_grad)
    wait(moves)
    parts = QUAD * mine.shape[0]
    owned = hub_blocks * tile // parts
    each = parts // QUAD
    for c in range(QUAD):
        hubs_f32[...] = hubs_in[c].astype(F32)
        for r in range(owned):
            hub_rows[pl.ds(c * owned + r, each, stride=QUAD * owned), :] = hubs_f32[
                pl.ds(r, each, stride=owned), :
            ]
    table[halo_count:] = hub_rows[...].reshape(hub_blocks, tile, width).astype(BF16)

    @pl.loop(0, chunks)
    def _(i):
        wait(fetch(i))
        many = rows_of(i, STEP * tile)

        def edges(b):
            return jnp.concatenate([tiles[i * STEP + b, k] for k in range(per_block)], 1)

        sources = [[src[k, i * STEP + b] for k in range(per_block)] for b in range(STEP)]
        remote = [
            jnp.dot(
                edges(b),
                jnp.concatenate([table[s] for s in sources[b]], 0),
                preferred_element_type=F32,
            )
            for b in range(STEP)
        ]
        agg = agg_local[many, :] + jnp.concatenate(remote, 0)
        both = jnp.concatenate([rows[many, :], agg.astype(BF16)], 1)
        pre = jnp.dot(both, weights[...], preferred_element_type=F32) + bias[...]
        sig = jax.nn.sigmoid(pre)
        hidden[many, :] = (pre * sig).astype(BF16)
        d_pre = d_hidden[many, :].astype(F32) * (sig * (1.0 + pre * (1.0 - sig)))
        b_grad[...] += jnp.sum(d_pre.reshape(-1, 8, d_pre.shape[-1]), 0)
        d_pre_b = d_pre.astype(BF16)
        d_pre_out[many, :] = d_pre_b
        d_agg = lax.dot_general(weights[width:, :], d_pre_b, NT, preferred_element_type=F32)
        d_agg = d_agg.astype(BF16)
        for b in range(STEP):
            own = d_agg[:, b * tile : (b + 1) * tile]
            d_agg_out[i * STEP + b] = own
            terms = jnp.dot(own, edges(b), preferred_element_type=F32)
            for k, s in enumerate(sources[b]):
                rem_grad[s] += terms[:, k * tile : (k + 1) * tile]
        start(store(i))
        w_grad[...] += lax.dot_general(d_pre_b, both, TN, preferred_element_type=F32)

    sent = []
    for w, s in enumerate(slots):
        backs_out[w] = rem_grad[pl.ds(s * per_list, per_list)].astype(BF16)
        sent.append(pltpu.make_async_copy(backs_out.at[w], backs[w], sem_back.at[w]))
    start(sent)
    chunk = mine.shape[1]
    w_self_grad[...] = w_grad[:, :width]
    w_neigh_grad[...] = w_grad[:, width:]
    for q in range(hub_blocks):
        hub_rows[q * tile : (q + 1) * tile, :] = jnp.transpose(rem_grad[halo_count + q])
    total = jnp.sum(b_grad[...], 0, keepdims=True)
    high = total.astype(BF16).astype(F32)
    lane = lax.broadcasted_iota(jnp.int32, (width, parts), 0)
    two = jnp.where(lane == 0, high, jnp.where(lane == 1, total - high, 0.0))
    b_rows[...] = jnp.transpose(two)
    for c in range(QUAD):
        base = c * each * chunk
        for i in range(owned):
            spread[pl.ds(base + i, each, stride=chunk), :] = hub_rows[
                pl.ds(c * owned + i, each, stride=QUAD * owned), :
            ]
        every = pl.ds(c, each, stride=QUAD)
        spread[pl.ds(base + owned, each, stride=chunk), :] = w_self_grad[every, :]
        spread[pl.ds(base + owned + 1, each, stride=chunk), :] = w_neigh_grad[every, :]
        spread[pl.ds(base + owned + 2, each, stride=chunk), :] = b_rows[every, :]
        for i in range(owned + 3, chunk):
            spread[pl.ds(base + i, each, stride=chunk), :] = jnp.zeros((each, width), F32)
    for x in range(1, QUAD):
        part = spread[rows_of(place ^ x, each * chunk), :].reshape(each, chunk, width)
        pack_out[x - 1] = part.astype(BF16)
        sent.append(
            pltpu.make_async_copy(pack_out.at[x - 1], theirs[x - 1], sem_back.at[lists + x - 1])
        )
        sent[-1].start()
    mine[...] = spread[rows_of(place, each * chunk), :].reshape(each, chunk, width)
    wait(sent)
    for i in range(chunks):
        wait(store(i))


def layer(src, tiles, rows, agg_local, halos, hubs, w_self, w_neigh, bias, d_hidden, parts):
    count, per_block, tile, _ = tiles.shape
    nodes, width = rows.shape
    units = d_hidden.shape[-1]
    lists, per_list = len(halos), halos[0].shape[0]
    hub_total = QUAD * hubs[0].shape[0]
    table = lists * per_list + hub_total // tile
    pieces = (parts // QUAD, CHUNK, width)
    chunks = count // STEP
    return pl.pallas_call(
        layer_kernel,
        out_shape=[
            pltpu.HBM((nodes, units), BF16),
            pltpu.VMEM((nodes, units), BF16),
            pltpu.HBM((count, width, tile), BF16),
        ]
        + [pltpu.HBM((per_list, width, tile), BF16)] * lists
        + [pltpu.VMEM(pieces, F32)]
        + [pltpu.HBM(pieces, BF16)] * (QUAD - 1),
        in_specs=[HBM_SPEC] * 5 + [ANY_SPEC] * (lists + QUAD) + [HBM_SPEC] * 3,
        out_specs=[HBM_SPEC, VMEM_SPEC]
        + [HBM_SPEC] * (lists + 1)
        + [VMEM_SPEC]
        + [HBM_SPEC] * (QUAD - 1),
        scratch_shapes=[
            pltpu.VMEM((QUAD,) + hubs[0].shape, BF16),
            pltpu.VMEM(hubs[0].shape, F32),
            pltpu.VMEM((hub_total, width), F32),
            pltpu.SMEM(src.shape, jnp.int32),
            pltpu.VMEM((2 * width, units), BF16),
            pltpu.VMEM((1, units), F32),
            pltpu.VMEM((table, tile, width), BF16),
            pltpu.VMEM((table, width, tile), F32),
            pltpu.VMEM((lists, per_list, width, tile), BF16),
            pltpu.VMEM((units, 2 * width), F32),
            pltpu.VMEM((8, units), F32),
            pltpu.VMEM((units, width), F32),
            pltpu.VMEM((units, width), F32),
            pltpu.VMEM((units, width), F32),
            pltpu.VMEM((parts * CHUNK, width), F32),
            pltpu.VMEM((QUAD - 1,) + pieces, BF16),
            pltpu.VMEM(tiles.shape, BF16),
            pltpu.VMEM((nodes, width), BF16),
            pltpu.VMEM((nodes, width), F32),
            pltpu.VMEM((nodes, units), BF16),
            pltpu.VMEM((nodes, units), BF16),
            pltpu.VMEM((count, width, tile), BF16),
            pltpu.SemaphoreType.DMA((lists + 4 + QUAD,)),
            pltpu.SemaphoreType.DMA((lists + QUAD - 1,)),
            pltpu.SemaphoreType.DMA((chunks, 4)),
            pltpu.SemaphoreType.DMA((chunks, 2)),
        ],
        compiler_params=params(),
        cost_estimate=pl.CostEstimate(
            flops=4 * tiles.size * width + 12 * nodes * width * units,
            bytes_accessed=14 << 20,
            transcendentals=nodes * units,
        ),
        name="layer",
    )(
        hbm(src),
        hbm(tiles),
        hbm(rows),
        hbm(agg_local),
        hbm(d_hidden),
        *halos,
        *hubs,
        hbm(w_self),
        hbm(w_neigh),
        hbm(bias),
    )


def add_kernel(mine, *refs):
    theirs_any, (out_hbm, theirs, out, sems, sem_out) = refs[: QUAD - 1], refs[QUAD - 1 :]
    loads = [
        pltpu.make_async_copy(t, theirs.at[x], sems.at[x]) for x, t in enumerate(theirs_any)
    ]
    start(loads)
    wait(loads)
    total = mine[...]
    for x in range(QUAD - 1):
        total = total + theirs[x].astype(F32)
    out[...] = total.astype(BF16)
    save = pltpu.make_async_copy(out, out_hbm, sem_out)
    save.start()
    save.wait()


def add_pieces(mine, theirs):
    return pl.pallas_call(
        add_kernel,
        out_shape=pltpu.HBM(mine.shape, BF16),
        in_specs=[VMEM_SPEC] + [ANY_SPEC] * (QUAD - 1),
        out_specs=HBM_SPEC,
        scratch_shapes=[
            pltpu.VMEM((QUAD - 1,) + mine.shape, BF16),
            pltpu.VMEM(mine.shape, BF16),
            pltpu.SemaphoreType.DMA((QUAD - 1,)),
            pltpu.SemaphoreType.DMA,
        ],
        compiler_params=params(),
        name="add_pieces",
    )(vmem(mine), *theirs)


def back_kernel(
    src_hbm, weight_hbm, tiles_hbm, d_hbm, d_pre, total, src, weight, tiles, d_agg, sems, sem_in
):
    count, per_block, tile, _ = tiles.shape
    size = STEP * tile

    def fetch(i):
        part = pl.ds(i * STEP, STEP)
        pairs = ((tiles_hbm.at[part], tiles.at[part]), (d_hbm.at[part], d_agg.at[part]))
        return [pltpu.make_async_copy(*p, sem_in.at[i, n]) for n, p in enumerate(pairs)]

    loads = [
        pltpu.make_async_copy(src_hbm, src, sems.at[0]),
        pltpu.make_async_copy(weight_hbm, weight, sems.at[1]),
    ]
    start(loads)
    for i in range(count // STEP):
        start(fetch(i))
    total[...] = jnp.zeros_like(total)
    wait(loads)

    @pl.loop(0, count // STEP)
    def _(i):
        wait(fetch(i))
        own = lax.dot_general(
            weight[...], d_pre[rows_of(i, size), :], NT, preferred_element_type=F32
        )
        for b in range(STEP):
            at = i * STEP + b
            total[at] += own[:, b * tile : (b + 1) * tile]
            edges = jnp.concatenate([tiles[at, k] for k in range(per_block)], 1)
            terms = jnp.dot(d_agg[at], edges, preferred_element_type=F32)
            for k in range(per_block):
                s = src[k, at]
                total[s] += terms[:, k * tile : (k + 1) * tile]


def local_backward(src, tiles, d_pre, d_agg, weight):
    count, per_block, tile, _ = tiles.shape
    width, units = weight.shape
    return pl.pallas_call(
        back_kernel,
        out_shape=pltpu.VMEM((count, width, tile), F32),
        in_specs=[HBM_SPEC] * 4 + [VMEM_SPEC],
        out_specs=VMEM_SPEC,
        scratch_shapes=[
            pltpu.SMEM(src.shape, jnp.int32),
            pltpu.VMEM(weight.shape, BF16),
            pltpu.VMEM(tiles.shape, BF16),
            pltpu.VMEM(d_agg.shape, BF16),
            pltpu.SemaphoreType.DMA((2,)),
            pltpu.SemaphoreType.DMA((count // STEP, 2)),
        ],
        compiler_params=params(),
        cost_estimate=pl.CostEstimate(
            flops=10**10, bytes_accessed=64 << 20, transcendentals=0
        ),
        name="local_backward",
    )(hbm(src), hbm(weight), hbm(tiles), hbm(d_agg), vmem(d_pre))


def collect_kernel(send_hbm, hubs_hbm, _, *refs):
    lists, per_list = send_hbm.shape
    halos_hbm = refs[:lists]
    total, out, near, send, hubs, halos, turned, sem_in, sem_out = refs[lists:]
    count, width, tile = total.shape
    pairs = [(send_hbm, send), (hubs_hbm, hubs)]
    pairs += [(halos_hbm[way], halos.at[way]) for way in range(lists)]
    loads = [pltpu.make_async_copy(*p, sem_in.at[n]) for n, p in enumerate(pairs)]
    start(loads)
    wait(loads)
    for way, j in enumerate(lists_of_ways()):
        for h in range(per_list):
            total[send[j, h]] += halos[way, h].astype(F32)
    chunks = sem_out.shape[0]
    each = count // chunks
    stores = []
    for c in range(chunks):
        for b in range(c * each, (c + 1) * each):
            turned[b * tile : (b + 1) * tile, :] = jnp.transpose(total[b]).astype(BF16)
        part = pl.ds(c * each * tile, each * tile)
        stores.append(pltpu.make_async_copy(turned.at[part], out.at[part], sem_out.at[c]))
        stores[-1].start()
    for i in range(hubs.shape[0]):
        row = hubs[i]
        block = jnp.transpose(total[row // tile])
        want = lax.rem(row, tile) // GROUP
        part = jnp.zeros((GROUP, width), F32)
        for g in range(tile // GROUP):
            part = jnp.where(want == g, block[g * GROUP : (g + 1) * GROUP], part)
        near[i] = part
    wait(stores)


def collect(send, hubs, grad, halos):
    count, width, tile = grad.shape
    lists = len(halos)
    near = (hubs.shape[0], GROUP, width)
    return pl.pallas_call(
        collect_kernel,
        out_shape=[
            pltpu.VMEM(grad.shape, F32),
            pltpu.HBM((count * tile, width), BF16),
            pltpu.VMEM(near, F32),
        ],
        in_specs=[HBM_SPEC] * 2 + [VMEM_SPEC] + [ANY_SPEC] * lists,
        out_specs=[VMEM_SPEC, HBM_SPEC, VMEM_SPEC],
        scratch_shapes=[
            pltpu.SMEM(send.shape, jnp.int32),
            pltpu.SMEM(hubs.shape, jnp.int32),
            pltpu.VMEM((lists,) + halos[0].shape, BF16),
            pltpu.VMEM((count * tile, width), BF16),
            pltpu.SemaphoreType.DMA((2 + lists,)),
            pltpu.SemaphoreType.DMA((4,)),
        ],
        input_output_aliases={2: 0},
        compiler_params=params(),
        cost_estimate=pl.CostEstimate(
            flops=grad.size * 8, bytes_accessed=4 << 20, transcendentals=0
        ),
        name="collect",
    )(hbm(send), hbm(hubs), vmem(grad), *halos)[1:]


def finish_kernel(
    hubs_hbm, pieces_hbm, near, _, grad, g_self, g_neigh, g_bias, hubs, pieces, rows, sem_in, sems
):
    owned = hubs.shape[0]
    chunks = sem_in.shape[0] - 1
    each = pieces.shape[0] // chunks
    index = pltpu.make_async_copy(hubs_hbm, hubs, sem_in.at[chunks])
    index.start()
    loads = []
    for c in range(chunks):
        part = pl.ds(c * each, each)
        loads.append(pltpu.make_async_copy(pieces_hbm.at[part], pieces.at[part], sem_in.at[c]))
    start(loads)
    index.wait()
    total = jnp.zeros(pieces.shape[1:], F32)
    for c in range(chunks):
        loads[c].wait()
        total += jnp.sum(pieces[c * each : (c + 1) * each].astype(F32), 0)
    g_self[...] = total[owned : owned + 1, :]
    g_neigh[...] = total[owned + 1 : owned + 2, :]
    last = total[owned + 2 : owned + 3, :]
    g_bias[...] = jnp.broadcast_to(last[:, 0:1] + last[:, 1:2], last.shape)
    place = lax.broadcasted_iota(jnp.int32, (GROUP, total.shape[-1]), 0)
    for i in range(owned):
        value = near[i]
        for m in range(owned):
            same = hubs[m] // GROUP == hubs[i] // GROUP
            hit = jnp.logical_and(place == lax.rem(hubs[m], GROUP), same)
            value = value + jnp.where(hit, total[m : m + 1, :], 0.0)
        rows[i] = value.astype(BF16)

    def fresh(i):
        new = hubs[i] >= 0
        for m in range(i):
            new = jnp.logical_and(new, hubs[m] // GROUP != hubs[i] // GROUP)
        return new

    def move(i):
        base = pl.multiple_of(hubs[i] // GROUP * GROUP, GROUP)
        return pltpu.make_async_copy(rows.at[i], grad.at[pl.ds(base, GROUP), :], sems.at[i])

    for i in range(owned):
        pl.when(fresh(i))(lambda i=i: move(i).start())
    for i in range(owned):
        pl.when(fresh(i))(lambda i=i: move(i).wait())


def finish(hubs, pieces, near, grad):
    owned, _, width = near.shape
    line = jax.ShapeDtypeStruct((1, width), F32)
    return pl.pallas_call(
        finish_kernel,
        out_shape=[pltpu.HBM(grad.shape, grad.dtype), line, line, line],
        in_specs=[HBM_SPEC, ANY_SPEC, VMEM_SPEC, HBM_SPEC],
        out_specs=[HBM_SPEC, VMEM_SPEC, VMEM_SPEC, VMEM_SPEC],
        scratch_shapes=[
            pltpu.SMEM(hubs.shape, jnp.int32),
            pltpu.VMEM(pieces.shape, BF16),
            pltpu.VMEM((owned, GROUP, width), BF16),
            pltpu.SemaphoreType.DMA((5,)),
            pltpu.SemaphoreType.DMA((owned,)),
        ],
        input_output_aliases={3: 0},
        compiler_params=params(),
        name="finish",
    )(hbm(hubs), pieces, vmem(near), hbm(grad))


def shards(
    features,
    local_tiles,
    local_src,
    remote_tiles,
    remote_src,
    send_blocks,
    hub_rows,
    w_self,
    w_neigh,
    bias,
    d_hidden,
):
    parts = lax.axis_size("dom")
    nodes, width = features.shape
    tile = local_tiles.shape[-1]
    blocks = features.reshape(nodes // tile, tile, width)
    *sends, hub_mine, own = gather_sends(send_blocks, hub_rows, blocks, parts)
    halos = [swapped(b, way) for way, b in enumerate(sends)]
    groups = same_place(parts)
    spread = spread_hubs(vmem(hub_mine), halos[0], parts // QUAD)
    hub_quarter = lax.all_to_all(spread, "dom", 0, 0, axis_index_groups=groups)
    hub_quarter = hub_quarter.reshape(-1, width)
    agg_local = local_aggregate(local_src.T, local_tiles, own)
    hidden, d_pre, d_agg, *rest = layer(
        remote_src.T,
        remote_tiles,
        features,
        agg_local,
        halos,
        [hub_quarter] + [swapped(hub_quarter, way) for way in SHARING],
        w_self,
        w_neigh,
        bias[None],
        d_hidden,
        parts,
    )
    backs, mine, theirs = rest[: len(OFFSETS)], rest[len(OFFSETS)], rest[len(OFFSETS) + 1 :]
    packed = add_pieces(mine, [swapped(x, way) for x, way in zip(theirs, SHARING)])
    pieces = lax.all_to_all(packed, "dom", 0, 0, axis_index_groups=groups)
    returned = [swapped(b, way) for way, b in enumerate(backs)]
    grad_t = local_backward(local_src.T, local_tiles, d_pre, d_agg, w_self)
    rough, near = collect(send_blocks, hub_rows, grad_t, returned)
    grad, g_self, g_neigh, g_bias = finish(hub_rows, pieces, near, rough)
    return (hidden, grad, g_self.reshape(width, 1), g_neigh.reshape(width, 1), g_bias[0, :1])


def solution(mesh):
    in_specs = (
        P("dom", None),
        P("dom", None, None, None),
        P("dom", None),
        P("dom", None, None, None),
        P("dom", None),
        P("dom", None),
        P("dom"),
        P(),
        P(),
        P(),
        P("dom", None),
    )
    out_specs = (P("dom", None), P("dom", None), P(None, "dom"), P(None, "dom"), P("dom"))
    return jax.shard_map(shards, mesh=mesh, in_specs=in_specs, out_specs=out_specs, check_vma=False)
```

```python
import functools

import jax
import jax.numpy as jnp
from jax import lax
from jax.experimental import pallas as pl
from jax.experimental.pallas import tpu as pltpu
from jax.sharding import PartitionSpec as P

OFFSETS = (1, -1, 2, -2)
F32 = jnp.float32
BF16 = jnp.bfloat16
NT = (((1,), (1,)), ((), ()))
TN = (((0,), (0,)), ((), ()))
GROUP = 16
CHUNK = 8
STEP = 8


QUAD = 4


def partner(i, way, n):
    if way == 0:
        return i ^ 1
    if way == 4:
        return i ^ 3
    if way == 1:
        return (i + (1 if i & 1 else -1)) % n
    ahead = (i >> 1) & 1 == way - 2
    return (i + (2 if ahead else -2)) % n


def swapped(block, way):
    n = lax.axis_size("dom")
    return lax.ppermute(block, "dom", [(i, partner(i, way, n)) for i in range(n)])


def lists_of_ways():
    me = lax.axis_index("dom")
    odd, odd_chip = me & 1, (me >> 1) & 1
    return odd, 1 - odd, 2 + odd_chip, 3 - odd_chip


SHARING = (0, 2, 4)


def same_place(n):
    return [list(range(c, n, QUAD)) for c in range(QUAD)]


def rows_of(chunk, size):
    return pl.ds(pl.multiple_of(chunk * size, size), size)


def params():
    return pltpu.CompilerParams(vmem_limit_bytes=40 << 20)


def hbm(x):
    return pltpu.with_memory_space_constraint(x, pltpu.HBM)


def vmem(x):
    return pltpu.with_memory_space_constraint(x, pltpu.VMEM)


ANY_SPEC = pl.BlockSpec(memory_space=pl.ANY)
HBM_SPEC = pl.BlockSpec(memory_space=pltpu.HBM)
VMEM_SPEC = pl.BlockSpec(memory_space=pltpu.VMEM)


def start(copies):
    for c in copies:
        c.start()


def wait(copies):
    for c in copies:
        c.wait()


def whole(shape):
    return pl.BlockSpec(shape, lambda *_: (0,) * len(shape))


def send_kernel(send_hbm, hubs_hbm, blocks_hbm, *refs):
    lists, per_list = send_hbm.shape
    outs, refs = refs[:lists], refs[lists:]
    hub_out, blocks, send, hubs, sem_in, sems = refs
    owned = hubs.shape[0]
    count, tile, width = blocks.shape
    pairs = [(send_hbm, send), (hubs_hbm, hubs)]
    half = count // 2
    for part in (pl.ds(0, half), pl.ds(half, half)):
        pairs.append((blocks_hbm.at[part], blocks.at[part]))
    loads = [pltpu.make_async_copy(*p, sem_in.at[n]) for n, p in enumerate(pairs)]
    start(loads)
    wait(loads)
    moves = []
    for way, j in enumerate(lists_of_ways()):
        for h in range(per_list):
            moves.append(
                pltpu.make_async_copy(
                    blocks.at[send[j, h]], outs[way].at[h], sems.at[way * per_list + h]
                )
            )
    start(moves)
    place = lax.broadcasted_iota(jnp.int32, (GROUP, width), 0)
    rows = []
    for i in range(owned):
        row = hubs[i]
        base = pl.multiple_of(lax.rem(row, tile) // GROUP * GROUP, GROUP)
        near = blocks[row // tile, pl.ds(base, GROUP), :].astype(F32)
        chosen = jnp.where(place == lax.rem(row, GROUP), near, 0.0)
        rows.append(jnp.sum(chosen, 0, keepdims=True))
    hub_out[...] = jnp.broadcast_to(jnp.concatenate(rows, 0).astype(BF16)[None], hub_out.shape)
    wait(moves)


def gather_sends(send, hubs, blocks, parts):
    lists, per_list = send.shape
    _, tile, width = blocks.shape
    return pl.pallas_call(
        send_kernel,
        out_shape=[pltpu.HBM((per_list, tile, width), BF16)] * lists
        + [
            jax.ShapeDtypeStruct((parts, hubs.shape[0], width), BF16),
            pltpu.VMEM(blocks.shape, BF16),
        ],
        in_specs=[HBM_SPEC] * 3,
        out_specs=[HBM_SPEC] * lists + [VMEM_SPEC, VMEM_SPEC],
        scratch_shapes=[
            pltpu.SMEM(send.shape, jnp.int32),
            pltpu.SMEM(hubs.shape, jnp.int32),
            pltpu.SemaphoreType.DMA((4,)),
            pltpu.SemaphoreType.DMA((lists * per_list,)),
        ],
        compiler_params=params(),
        name="sends",
    )(hbm(send), hbm(hubs), hbm(blocks))


def local_kernel(
    src_hbm, tiles_hbm, blocks, agg_hbm, src, tiles, agg, sem, sem_in, sem_out
):
    count, per_block, tile, _ = tiles.shape
    chunks = count // STEP

    def fetch(i):
        part = pl.ds(i * STEP, STEP)
        return pltpu.make_async_copy(tiles_hbm.at[part], tiles.at[part], sem_in.at[i])

    def store(i):
        part = rows_of(i, STEP * tile)
        return pltpu.make_async_copy(agg.at[part], agg_hbm.at[part], sem_out.at[i])

    index = pltpu.make_async_copy(src_hbm, src, sem)
    index.start()
    for i in range(chunks):
        fetch(i).start()
    index.wait()

    @pl.loop(0, chunks)
    def _(i):
        fetch(i).wait()
        for b in range(STEP):
            at = i * STEP + b
            taken = [blocks[src[k, at]] for k in range(per_block)]
            edges = [tiles[at, k] for k in range(per_block)]
            agg[rows_of(at, tile), :] = jnp.dot(
                jnp.concatenate(edges, 1), jnp.concatenate(taken, 0), preferred_element_type=F32
            )
        store(i).start()

    wait([store(i) for i in range(chunks)])


def local_aggregate(src, tiles, blocks):
    count, per_block, tile, _ = tiles.shape
    width = blocks.shape[-1]
    agg = (count * tile, width)
    return pl.pallas_call(
        local_kernel,
        out_shape=pltpu.HBM(agg, F32),
        in_specs=[HBM_SPEC] * 2 + [VMEM_SPEC],
        out_specs=HBM_SPEC,
        scratch_shapes=[
            pltpu.SMEM(src.shape, jnp.int32),
            pltpu.VMEM(tiles.shape, BF16),
            pltpu.VMEM(agg, F32),
            pltpu.SemaphoreType.DMA,
            pltpu.SemaphoreType.DMA((count // STEP,)),
            pltpu.SemaphoreType.DMA((count // STEP,)),
        ],
        compiler_params=params(),
        cost_estimate=pl.CostEstimate(
            flops=10**10, bytes_accessed=64 << 20, transcendentals=0
        ),
        name="local_aggregate",
    )(hbm(src), hbm(tiles), vmem(blocks))


def layer_kernel(src_hbm, *refs):
    lists = len(OFFSETS)
    tiles_hbm, rows_hbm, agg_hbm, d_hbm = refs[:4]
    halos, refs = refs[4 : 4 + lists], refs[4 + lists :]
    hub, self_hbm, neigh_hbm, bias_hbm, hidden_hbm, d_pre_out, d_agg_hbm = refs[:7]
    backs, mine, refs = refs[7 : 7 + lists], refs[7 + lists], refs[8 + lists :]
    theirs, hub_rows, refs = refs[: QUAD - 1], refs[QUAD - 1], refs[QUAD:]
    src, weights, bias, table, rem_grad, backs_out, w_grad, b_grad = refs[:8]
    w_self_grad, w_neigh_grad, b_rows = refs[8:11]
    refs = refs[11:]
    spread, pack_out, tiles, rows, agg_local, d_hidden, hidden, d_agg_out = refs[:8]
    sem_t, sem_back, sem_in, sem_out = refs[8:]
    count, per_block, tile, _ = tiles.shape
    width = rows.shape[-1]
    per_list = halos[0].shape[0]
    halo_count = lists * per_list
    hub_blocks = hub.shape[0]
    place = lax.axis_index("dom") % QUAD
    slots = [j ^ 1 for j in lists_of_ways()]
    pairs = [
        (src_hbm, src),
        (hub, table.at[pl.ds(halo_count, hub_blocks)]),
        (self_hbm, weights.at[pl.ds(0, width)]),
        (neigh_hbm, weights.at[pl.ds(width, width)]),
        (bias_hbm, bias),
    ]
    for w, s in enumerate(slots):
        pairs.append((halos[w], table.at[pl.ds(s * per_list, per_list)]))
    moves = [pltpu.make_async_copy(*p, sem_t.at[n]) for n, p in enumerate(pairs)]
    chunks = count // STEP

    def fetch(i):
        few, many = pl.ds(i * STEP, STEP), rows_of(i, STEP * tile)
        pairs = (
            (tiles_hbm.at[few], tiles.at[few]),
            (agg_hbm.at[many], agg_local.at[many]),
            (rows_hbm.at[many], rows.at[many]),
            (d_hbm.at[many], d_hidden.at[many]),
        )
        return [pltpu.make_async_copy(*p, sem_in.at[i, n]) for n, p in enumerate(pairs)]

    def store(i):
        few, many = pl.ds(i * STEP, STEP), rows_of(i, STEP * tile)
        pairs = (
            (hidden.at[many], hidden_hbm.at[many]),
            (d_agg_out.at[few], d_agg_hbm.at[few]),
        )
        return [pltpu.make_async_copy(*p, sem_out.at[i, n]) for n, p in enumerate(pairs)]

    start(moves)
    for i in range(chunks):
        start(fetch(i))
    rem_grad[...] = jnp.zeros_like(rem_grad)
    w_grad[...] = jnp.zeros_like(w_grad)
    b_grad[...] = jnp.zeros_like(b_grad)
    wait(moves)
    parts = QUAD * mine.shape[0]
    owned = hub_blocks * tile // parts
    each = parts // QUAD

    @pl.loop(0, chunks)
    def _(i):
        wait(fetch(i))
        many = rows_of(i, STEP * tile)

        def edges(b):
            return jnp.concatenate([tiles[i * STEP + b, k] for k in range(per_block)], 1)

        per = STEP // 2
        rows_per = per * tile

        def lines(g):
            return rows_of(i * 2 + g, rows_per)

        def stage_a(g):
            remote = []
            for b in range(g * per, (g + 1) * per):
                taken = [table[src[k, i * STEP + b]] for k in range(per_block)]
                remote.append(
                    jnp.dot(edges(b), jnp.concatenate(taken, 0), preferred_element_type=F32)
                )
            agg = agg_local[lines(g), :] + jnp.concatenate(remote, 0)
            both = jnp.concatenate([rows[lines(g), :], agg.astype(BF16)], 1)
            return both, jnp.dot(both, weights[...], preferred_element_type=F32) + bias[...]

        def stage_b(g, pre):
            sig = jax.nn.sigmoid(pre)
            hid = pre * sig
            hidden[lines(g), :] = hid.astype(BF16)
            d_pre = d_hidden[lines(g), :].astype(F32) * (sig + hid * (1.0 - sig))
            b_grad[...] += jnp.sum(d_pre.reshape(-1, 8, d_pre.shape[-1]), 0)
            d_pre_b = d_pre.astype(BF16)
            d_pre_out[lines(g), :] = d_pre_b
            return d_pre_b

        def stage_c(g, both, d_pre_b):
            d_agg = lax.dot_general(weights[width:, :], d_pre_b, NT, preferred_element_type=F32)
            d_agg = d_agg.astype(BF16)
            for n in range(per):
                b = g * per + n
                own = d_agg[:, n * tile : (n + 1) * tile]
                d_agg_out[i * STEP + b] = own
                terms = jnp.dot(own, edges(b), preferred_element_type=F32)
                for k in range(per_block):
                    rem_grad[src[k, i * STEP + b]] += terms[:, k * tile : (k + 1) * tile]
            w_grad[...] += lax.dot_general(d_pre_b, both, TN, preferred_element_type=F32)

        held = {}
        for stage, g in [(0, 0), (1, 0), (0, 1), (2, 0), (1, 1), (2, 1)]:
            if stage == 0:
                held[g] = stage_a(g)
            elif stage == 1:
                held[g] = (held[g][0], stage_b(g, held[g][1]))
            else:
                stage_c(g, *held[g])
        start(store(i))

    sent = []
    for w, s in enumerate(slots):
        backs_out[w] = rem_grad[pl.ds(s * per_list, per_list)].astype(BF16)
        sent.append(pltpu.make_async_copy(backs_out.at[w], backs[w], sem_back.at[w]))
    start(sent)
    chunk = mine.shape[1]
    w_self_grad[...] = w_grad[:, :width]
    w_neigh_grad[...] = w_grad[:, width:]
    for q in range(hub_blocks):
        hub_rows[q * tile : (q + 1) * tile, :] = jnp.transpose(rem_grad[halo_count + q])
    total = jnp.sum(b_grad[...], 0, keepdims=True)
    high = total.astype(BF16).astype(F32)
    lane = lax.broadcasted_iota(jnp.int32, (width, parts), 0)
    two = jnp.where(lane == 0, high, jnp.where(lane == 1, total - high, 0.0))
    b_rows[...] = jnp.transpose(two)
    for c in range(QUAD):
        base = c * each * chunk
        for i in range(owned):
            spread[pl.ds(base + i, each, stride=chunk), :] = hub_rows[
                pl.ds(c * owned + i, each, stride=QUAD * owned), :
            ]
        every = pl.ds(c, each, stride=QUAD)
        spread[pl.ds(base + owned, each, stride=chunk), :] = w_self_grad[every, :]
        spread[pl.ds(base + owned + 1, each, stride=chunk), :] = w_neigh_grad[every, :]
        spread[pl.ds(base + owned + 2, each, stride=chunk), :] = b_rows[every, :]
        for i in range(owned + 3, chunk):
            spread[pl.ds(base + i, each, stride=chunk), :] = jnp.zeros((each, width), F32)
    for x in range(1, QUAD):
        part = spread[rows_of(place ^ x, each * chunk), :].reshape(each, chunk, width)
        pack_out[x - 1] = part.astype(BF16)
        sent.append(
            pltpu.make_async_copy(pack_out.at[x - 1], theirs[x - 1], sem_back.at[lists + x - 1])
        )
        sent[-1].start()
    mine[...] = spread[rows_of(place, each * chunk), :].reshape(each, chunk, width)
    wait(sent)
    for i in range(chunks):
        wait(store(i))


def layer(src, tiles, rows, agg_local, halos, hub, w_self, w_neigh, bias, d_hidden, parts):
    count, per_block, tile, _ = tiles.shape
    nodes, width = rows.shape
    units = d_hidden.shape[-1]
    lists, per_list = len(halos), halos[0].shape[0]
    table = lists * per_list + hub.shape[0]
    pieces = (parts // QUAD, CHUNK, width)
    chunks = count // STEP
    return pl.pallas_call(
        layer_kernel,
        out_shape=[
            pltpu.HBM((nodes, units), BF16),
            pltpu.VMEM((nodes, units), BF16),
            pltpu.HBM((count, width, tile), BF16),
        ]
        + [pltpu.HBM((per_list, width, tile), BF16)] * lists
        + [pltpu.VMEM(pieces, F32)]
        + [pltpu.HBM(pieces, BF16)] * (QUAD - 1),
        in_specs=[HBM_SPEC] * 5 + [ANY_SPEC] * (lists + 1) + [HBM_SPEC] * 3,
        out_specs=[HBM_SPEC, VMEM_SPEC]
        + [HBM_SPEC] * (lists + 1)
        + [VMEM_SPEC]
        + [HBM_SPEC] * (QUAD - 1),
        scratch_shapes=[
            pltpu.VMEM((hub.shape[0] * tile, width), F32),
            pltpu.SMEM(src.shape, jnp.int32),
            pltpu.VMEM((2 * width, units), BF16),
            pltpu.VMEM((1, units), F32),
            pltpu.VMEM((table, tile, width), BF16),
            pltpu.VMEM((table, width, tile), F32),
            pltpu.VMEM((lists, per_list, width, tile), BF16),
            pltpu.VMEM((units, 2 * width), F32),
            pltpu.VMEM((8, units), F32),
            pltpu.VMEM((units, width), F32),
            pltpu.VMEM((units, width), F32),
            pltpu.VMEM((units, width), F32),
            pltpu.VMEM((parts * CHUNK, width), F32),
            pltpu.VMEM((QUAD - 1,) + pieces, BF16),
            pltpu.VMEM(tiles.shape, BF16),
            pltpu.VMEM((nodes, width), BF16),
            pltpu.VMEM((nodes, width), F32),
            pltpu.VMEM((nodes, units), BF16),
            pltpu.VMEM((nodes, units), BF16),
            pltpu.VMEM((count, width, tile), BF16),
            pltpu.SemaphoreType.DMA((lists + 5,)),
            pltpu.SemaphoreType.DMA((lists + QUAD - 1,)),
            pltpu.SemaphoreType.DMA((chunks, 4)),
            pltpu.SemaphoreType.DMA((chunks, 2)),
        ],
        compiler_params=params(),
        cost_estimate=pl.CostEstimate(
            flops=4 * tiles.size * width + 12 * nodes * width * units,
            bytes_accessed=14 << 20,
            transcendentals=nodes * units,
        ),
        name="layer",
    )(
        hbm(src),
        hbm(tiles),
        hbm(rows),
        hbm(agg_local),
        hbm(d_hidden),
        *halos,
        hub,
        hbm(w_self),
        hbm(w_neigh),
        hbm(bias),
    )


def add_kernel(mine, *refs):
    theirs_any, (out_hbm, theirs, out, sems, sem_out) = refs[: QUAD - 1], refs[QUAD - 1 :]
    loads = [
        pltpu.make_async_copy(t, theirs.at[x], sems.at[x]) for x, t in enumerate(theirs_any)
    ]
    start(loads)
    wait(loads)
    total = mine[...]
    for x in range(QUAD - 1):
        total = total + theirs[x].astype(F32)
    out[...] = total.astype(BF16)
    save = pltpu.make_async_copy(out, out_hbm, sem_out)
    save.start()
    save.wait()


def add_pieces(mine, theirs):
    return pl.pallas_call(
        add_kernel,
        out_shape=pltpu.HBM(mine.shape, BF16),
        in_specs=[VMEM_SPEC] + [ANY_SPEC] * (QUAD - 1),
        out_specs=HBM_SPEC,
        scratch_shapes=[
            pltpu.VMEM((QUAD - 1,) + mine.shape, BF16),
            pltpu.VMEM(mine.shape, BF16),
            pltpu.SemaphoreType.DMA((QUAD - 1,)),
            pltpu.SemaphoreType.DMA,
        ],
        compiler_params=params(),
        name="add_pieces",
    )(vmem(mine), *theirs)


def back_kernel(
    src_hbm, weight_hbm, tiles_hbm, d_hbm, d_pre, total, src, weight, tiles, d_agg, sems, sem_in
):
    count, per_block, tile, _ = tiles.shape
    size = STEP * tile

    def fetch(i):
        part = pl.ds(i * STEP, STEP)
        pairs = ((tiles_hbm.at[part], tiles.at[part]), (d_hbm.at[part], d_agg.at[part]))
        return [pltpu.make_async_copy(*p, sem_in.at[i, n]) for n, p in enumerate(pairs)]

    loads = [
        pltpu.make_async_copy(src_hbm, src, sems.at[0]),
        pltpu.make_async_copy(weight_hbm, weight, sems.at[1]),
    ]
    start(loads)
    for i in range(count // STEP):
        start(fetch(i))
    total[...] = jnp.zeros_like(total)
    wait(loads)

    @pl.loop(0, count // STEP)
    def _(i):
        wait(fetch(i))
        own = lax.dot_general(
            weight[...], d_pre[rows_of(i, size), :], NT, preferred_element_type=F32
        )
        for b in range(STEP):
            at = i * STEP + b
            total[at] += own[:, b * tile : (b + 1) * tile]
            edges = jnp.concatenate([tiles[at, k] for k in range(per_block)], 1)
            terms = jnp.dot(d_agg[at], edges, preferred_element_type=F32)
            for k in range(per_block):
                s = src[k, at]
                total[s] += terms[:, k * tile : (k + 1) * tile]


def local_backward(src, tiles, d_pre, d_agg, weight):
    count, per_block, tile, _ = tiles.shape
    width, units = weight.shape
    return pl.pallas_call(
        back_kernel,
        out_shape=pltpu.VMEM((count, width, tile), F32),
        in_specs=[HBM_SPEC] * 4 + [VMEM_SPEC],
        out_specs=VMEM_SPEC,
        scratch_shapes=[
            pltpu.SMEM(src.shape, jnp.int32),
            pltpu.VMEM(weight.shape, BF16),
            pltpu.VMEM(tiles.shape, BF16),
            pltpu.VMEM(d_agg.shape, BF16),
            pltpu.SemaphoreType.DMA((2,)),
            pltpu.SemaphoreType.DMA((count // STEP, 2)),
        ],
        compiler_params=params(),
        cost_estimate=pl.CostEstimate(
            flops=10**10, bytes_accessed=64 << 20, transcendentals=0
        ),
        name="local_backward",
    )(hbm(src), hbm(weight), hbm(tiles), hbm(d_agg), vmem(d_pre))


def collect_kernel(send_hbm, hubs_hbm, _, *refs):
    lists, per_list = send_hbm.shape
    halos_hbm = refs[:lists]
    total, out, near, send, hubs, halos, turned, sem_in, sem_out = refs[lists:]
    count, width, tile = total.shape
    pairs = [(send_hbm, send), (hubs_hbm, hubs)]
    pairs += [(halos_hbm[way], halos.at[way]) for way in range(lists)]
    loads = [pltpu.make_async_copy(*p, sem_in.at[n]) for n, p in enumerate(pairs)]
    start(loads)
    wait(loads)
    for way, j in enumerate(lists_of_ways()):
        for h in range(per_list):
            total[send[j, h]] += halos[way, h].astype(F32)
    chunks = sem_out.shape[0]
    each = count // chunks
    stores = []
    for c in range(chunks):
        for b in range(c * each, (c + 1) * each):
            turned[b * tile : (b + 1) * tile, :] = jnp.transpose(total[b]).astype(BF16)
        part = pl.ds(c * each * tile, each * tile)
        stores.append(pltpu.make_async_copy(turned.at[part], out.at[part], sem_out.at[c]))
        stores[-1].start()
    for i in range(hubs.shape[0]):
        row = hubs[i]
        block = jnp.transpose(total[row // tile])
        want = lax.rem(row, tile) // GROUP
        part = jnp.zeros((GROUP, width), F32)
        for g in range(tile // GROUP):
            part = jnp.where(want == g, block[g * GROUP : (g + 1) * GROUP], part)
        near[i] = part
    wait(stores)


def collect(send, hubs, grad, halos):
    count, width, tile = grad.shape
    lists = len(halos)
    near = (hubs.shape[0], GROUP, width)
    return pl.pallas_call(
        collect_kernel,
        out_shape=[
            pltpu.VMEM(grad.shape, F32),
            pltpu.HBM((count * tile, width), BF16),
            pltpu.VMEM(near, F32),
        ],
        in_specs=[HBM_SPEC] * 2 + [VMEM_SPEC] + [ANY_SPEC] * lists,
        out_specs=[VMEM_SPEC, HBM_SPEC, VMEM_SPEC],
        scratch_shapes=[
            pltpu.SMEM(send.shape, jnp.int32),
            pltpu.SMEM(hubs.shape, jnp.int32),
            pltpu.VMEM((lists,) + halos[0].shape, BF16),
            pltpu.VMEM((count * tile, width), BF16),
            pltpu.SemaphoreType.DMA((2 + lists,)),
            pltpu.SemaphoreType.DMA((4,)),
        ],
        input_output_aliases={2: 0},
        compiler_params=params(),
        cost_estimate=pl.CostEstimate(
            flops=grad.size * 8, bytes_accessed=4 << 20, transcendentals=0
        ),
        name="collect",
    )(hbm(send), hbm(hubs), vmem(grad), *halos)[1:]


def finish_kernel(
    hubs_hbm, pieces_hbm, near, _, grad, g_self, g_neigh, g_bias, hubs, pieces, rows, sem_in, sems
):
    owned = hubs.shape[0]
    chunks = sem_in.shape[0] - 1
    each = pieces.shape[0] // chunks
    index = pltpu.make_async_copy(hubs_hbm, hubs, sem_in.at[chunks])
    index.start()
    loads = []
    for c in range(chunks):
        part = pl.ds(c * each, each)
        loads.append(pltpu.make_async_copy(pieces_hbm.at[part], pieces.at[part], sem_in.at[c]))
    start(loads)
    index.wait()
    total = jnp.zeros(pieces.shape[1:], F32)
    for c in range(chunks):
        loads[c].wait()
        total += jnp.sum(pieces[c * each : (c + 1) * each].astype(F32), 0)
    g_self[...] = total[owned : owned + 1, :]
    g_neigh[...] = total[owned + 1 : owned + 2, :]
    last = total[owned + 2 : owned + 3, :]
    g_bias[...] = jnp.broadcast_to(last[:, 0:1] + last[:, 1:2], last.shape)
    place = lax.broadcasted_iota(jnp.int32, (GROUP, total.shape[-1]), 0)
    for i in range(owned):
        value = near[i]
        for m in range(owned):
            same = hubs[m] // GROUP == hubs[i] // GROUP
            hit = jnp.logical_and(place == lax.rem(hubs[m], GROUP), same)
            value = value + jnp.where(hit, total[m : m + 1, :], 0.0)
        rows[i] = value.astype(BF16)

    def fresh(i):
        new = hubs[i] >= 0
        for m in range(i):
            new = jnp.logical_and(new, hubs[m] // GROUP != hubs[i] // GROUP)
        return new

    def move(i):
        base = pl.multiple_of(hubs[i] // GROUP * GROUP, GROUP)
        return pltpu.make_async_copy(rows.at[i], grad.at[pl.ds(base, GROUP), :], sems.at[i])

    for i in range(owned):
        pl.when(fresh(i))(lambda i=i: move(i).start())
    for i in range(owned):
        pl.when(fresh(i))(lambda i=i: move(i).wait())


def finish(hubs, pieces, near, grad):
    owned, _, width = near.shape
    line = jax.ShapeDtypeStruct((1, width), F32)
    return pl.pallas_call(
        finish_kernel,
        out_shape=[pltpu.HBM(grad.shape, grad.dtype), line, line, line],
        in_specs=[HBM_SPEC, ANY_SPEC, VMEM_SPEC, HBM_SPEC],
        out_specs=[HBM_SPEC, VMEM_SPEC, VMEM_SPEC, VMEM_SPEC],
        scratch_shapes=[
            pltpu.SMEM(hubs.shape, jnp.int32),
            pltpu.VMEM(pieces.shape, BF16),
            pltpu.VMEM((owned, GROUP, width), BF16),
            pltpu.SemaphoreType.DMA((5,)),
            pltpu.SemaphoreType.DMA((owned,)),
        ],
        input_output_aliases={3: 0},
        compiler_params=params(),
        name="finish",
    )(hbm(hubs), pieces, vmem(near), hbm(grad))


def shards(
    features,
    local_tiles,
    local_src,
    remote_tiles,
    remote_src,
    send_blocks,
    hub_rows,
    w_self,
    w_neigh,
    bias,
    d_hidden,
):
    parts = lax.axis_size("dom")
    nodes, width = features.shape
    tile = local_tiles.shape[-1]
    blocks = features.reshape(nodes // tile, tile, width)
    *sends, hub_mine, own = gather_sends(send_blocks, hub_rows, blocks, parts)
    hub_all = lax.all_to_all(hub_mine, "dom", 0, 0)
    halos = [swapped(b, way) for way, b in enumerate(sends)]
    agg_local = local_aggregate(local_src.T, local_tiles, own)
    hidden, d_pre, d_agg, *rest = layer(
        remote_src.T,
        remote_tiles,
        features,
        agg_local,
        halos,
        hub_all.reshape(-1, tile, width),
        w_self,
        w_neigh,
        bias[None],
        d_hidden,
        parts,
    )
    backs, mine, theirs = rest[: len(OFFSETS)], rest[len(OFFSETS)], rest[len(OFFSETS) + 1 :]
    packed = add_pieces(mine, [swapped(x, way) for x, way in zip(theirs, SHARING)])
    pieces = lax.all_to_all(packed, "dom", 0, 0, axis_index_groups=same_place(parts))
    returned = [swapped(b, way) for way, b in enumerate(backs)]
    grad_t = local_backward(local_src.T, local_tiles, d_pre, d_agg, w_self)
    rough, near = collect(send_blocks, hub_rows, grad_t, returned)
    grad, g_self, g_neigh, g_bias = finish(hub_rows, pieces, near, rough)
    return (hidden, grad, g_self.reshape(width, 1), g_neigh.reshape(width, 1), g_bias[0, :1])


def solution(mesh):
    in_specs = (
        P("dom", None),
        P("dom", None, None, None),
        P("dom", None),
        P("dom", None, None, None),
        P("dom", None),
        P("dom", None),
        P("dom"),
        P(),
        P(),
        P(),
        P("dom", None),
    )
    out_specs = (P("dom", None), P("dom", None), P(None, "dom"), P(None, "dom"), P("dom"))
    return jax.shard_map(shards, mesh=mesh, in_specs=in_specs, out_specs=out_specs, check_vma=False)
```

```python
import functools

import jax
import jax.numpy as jnp
from jax import lax
from jax.experimental import pallas as pl
from jax.experimental.pallas import tpu as pltpu
from jax.sharding import PartitionSpec as P

OFFSETS = (1, -1, 2, -2)
F32 = jnp.float32
BF16 = jnp.bfloat16
NT = (((1,), (1,)), ((), ()))
TN = (((0,), (0,)), ((), ()))
GROUP = 16
CHUNK = 8
STEP = 8


def partner(i, way, n):
    if way == 0:
        return i ^ 1
    if way == 1:
        return (i + (1 if i & 1 else -1)) % n
    ahead = (i >> 1) & 1 == way - 2
    return (i + (2 if ahead else -2)) % n


def swapped(block, way):
    n = lax.axis_size("dom")
    return lax.ppermute(block, "dom", [(i, partner(i, way, n)) for i in range(n)])


def lists_of_ways():
    me = lax.axis_index("dom")
    odd, odd_chip = me & 1, (me >> 1) & 1
    return odd, 1 - odd, 2 + odd_chip, 3 - odd_chip


def rows_of(chunk, size):
    return pl.ds(pl.multiple_of(chunk * size, size), size)


def params():
    return pltpu.CompilerParams(vmem_limit_bytes=40 << 20)


def hbm(x):
    return pltpu.with_memory_space_constraint(x, pltpu.HBM)


def vmem(x):
    return pltpu.with_memory_space_constraint(x, pltpu.VMEM)


ANY_SPEC = pl.BlockSpec(memory_space=pl.ANY)
HBM_SPEC = pl.BlockSpec(memory_space=pltpu.HBM)
VMEM_SPEC = pl.BlockSpec(memory_space=pltpu.VMEM)


def start(copies):
    for c in copies:
        c.start()


def wait(copies):
    for c in copies:
        c.wait()


def whole(shape):
    return pl.BlockSpec(shape, lambda *_: (0,) * len(shape))


def send_kernel(send_hbm, hubs_hbm, blocks_hbm, *refs):
    lists, per_list = send_hbm.shape
    outs, refs = refs[:lists], refs[lists:]
    hub_out, blocks, send, hubs, sem_in, sems = refs
    owned = hubs.shape[0]
    count, tile, width = blocks.shape
    pairs = [(send_hbm, send), (hubs_hbm, hubs)]
    half = count // 2
    for part in (pl.ds(0, half), pl.ds(half, half)):
        pairs.append((blocks_hbm.at[part], blocks.at[part]))
    loads = [pltpu.make_async_copy(*p, sem_in.at[n]) for n, p in enumerate(pairs)]
    start(loads)
    wait(loads)
    moves = []
    for way, j in enumerate(lists_of_ways()):
        for h in range(per_list):
            moves.append(
                pltpu.make_async_copy(
                    blocks.at[send[j, h]], outs[way].at[h], sems.at[way * per_list + h]
                )
            )
    start(moves)
    place = lax.broadcasted_iota(jnp.int32, (GROUP, width), 0)
    rows = []
    for i in range(owned):
        row = hubs[i]
        base = pl.multiple_of(lax.rem(row, tile) // GROUP * GROUP, GROUP)
        near = blocks[row // tile, pl.ds(base, GROUP), :].astype(F32)
        chosen = jnp.where(place == lax.rem(row, GROUP), near, 0.0)
        rows.append(jnp.sum(chosen, 0, keepdims=True))
    hub_out[...] = jnp.broadcast_to(jnp.concatenate(rows, 0).astype(BF16)[None], hub_out.shape)
    wait(moves)


def gather_sends(send, hubs, blocks, parts):
    lists, per_list = send.shape
    _, tile, width = blocks.shape
    return pl.pallas_call(
        send_kernel,
        out_shape=[pltpu.HBM((per_list, tile, width), BF16)] * lists
        + [
            jax.ShapeDtypeStruct((parts, hubs.shape[0], width), BF16),
            pltpu.VMEM(blocks.shape, BF16),
        ],
        in_specs=[HBM_SPEC] * 3,
        out_specs=[HBM_SPEC] * lists + [VMEM_SPEC, VMEM_SPEC],
        scratch_shapes=[
            pltpu.SMEM(send.shape, jnp.int32),
            pltpu.SMEM(hubs.shape, jnp.int32),
            pltpu.SemaphoreType.DMA((4,)),
            pltpu.SemaphoreType.DMA((lists * per_list,)),
        ],
        compiler_params=params(),
        name="sends",
    )(hbm(send), hbm(hubs), hbm(blocks))


def local_kernel(
    src_hbm, tiles_hbm, blocks, agg_hbm, src, tiles, agg, sem, sem_in, sem_out
):
    count, per_block, tile, _ = tiles.shape
    chunks = count // STEP

    def fetch(i):
        part = pl.ds(i * STEP, STEP)
        return pltpu.make_async_copy(tiles_hbm.at[part], tiles.at[part], sem_in.at[i])

    def store(i):
        part = rows_of(i, STEP * tile)
        return pltpu.make_async_copy(agg.at[part], agg_hbm.at[part], sem_out.at[i])

    index = pltpu.make_async_copy(src_hbm, src, sem)
    index.start()
    for i in range(chunks):
        fetch(i).start()
    index.wait()

    @pl.loop(0, chunks)
    def _(i):
        fetch(i).wait()
        for b in range(STEP):
            at = i * STEP + b
            taken = [blocks[src[k, at]] for k in range(per_block)]
            edges = [tiles[at, k] for k in range(per_block)]
            agg[rows_of(at, tile), :] = jnp.dot(
                jnp.concatenate(edges, 1), jnp.concatenate(taken, 0), preferred_element_type=F32
            )
        store(i).start()

    wait([store(i) for i in range(chunks)])


def local_aggregate(src, tiles, blocks):
    count, per_block, tile, _ = tiles.shape
    width = blocks.shape[-1]
    agg = (count * tile, width)
    return pl.pallas_call(
        local_kernel,
        out_shape=pltpu.HBM(agg, F32),
        in_specs=[HBM_SPEC] * 2 + [VMEM_SPEC],
        out_specs=HBM_SPEC,
        scratch_shapes=[
            pltpu.SMEM(src.shape, jnp.int32),
            pltpu.VMEM(tiles.shape, BF16),
            pltpu.VMEM(agg, F32),
            pltpu.SemaphoreType.DMA,
            pltpu.SemaphoreType.DMA((count // STEP,)),
            pltpu.SemaphoreType.DMA((count // STEP,)),
        ],
        compiler_params=params(),
        cost_estimate=pl.CostEstimate(
            flops=2 * tiles.size * width, bytes_accessed=8 << 20, transcendentals=0
        ),
        name="local_aggregate",
    )(hbm(src), hbm(tiles), vmem(blocks))


def layer_kernel(src_hbm, *refs):
    lists = len(OFFSETS)
    tiles_hbm, rows_hbm, agg_hbm, d_hbm = refs[:4]
    halos, refs = refs[4 : 4 + lists], refs[4 + lists :]
    hub, self_hbm, neigh_hbm, bias_hbm, hidden_hbm, d_pre_hbm, d_agg_hbm = refs[:7]
    backs, refs = refs[7 : 7 + lists], refs[7 + lists :]
    mine, theirs, src, weights, bias, table, rem_grad, backs_out, w_grad, b_grad = refs[:10]
    spread, pack_out, tiles, rows, agg_local, d_hidden, hidden, d_agg_out = refs[10:18]
    d_pre_out, sem_t, sem_back, sem_in, sem_out = refs[18:]
    count, per_block, tile, _ = tiles.shape
    width = rows.shape[-1]
    per_list = halos[0].shape[0]
    halo_count = lists * per_list
    hub_blocks = hub.shape[0]
    slots = [j ^ 1 for j in lists_of_ways()]
    pairs = [
        (src_hbm, src),
        (hub, table.at[pl.ds(halo_count, hub_blocks)]),
        (self_hbm, weights.at[pl.ds(0, width)]),
        (neigh_hbm, weights.at[pl.ds(width, width)]),
        (bias_hbm, bias),
    ]
    for w, s in enumerate(slots):
        pairs.append((halos[w], table.at[pl.ds(s * per_list, per_list)]))
    moves = [pltpu.make_async_copy(*p, sem_t.at[n]) for n, p in enumerate(pairs)]
    chunks = count // STEP

    def fetch(i):
        few, many = pl.ds(i * STEP, STEP), rows_of(i, STEP * tile)
        pairs = (
            (tiles_hbm.at[few], tiles.at[few]),
            (agg_hbm.at[many], agg_local.at[many]),
            (rows_hbm.at[many], rows.at[many]),
            (d_hbm.at[many], d_hidden.at[many]),
        )
        return [pltpu.make_async_copy(*p, sem_in.at[i, n]) for n, p in enumerate(pairs)]

    def store(i):
        few, many = pl.ds(i * STEP, STEP), rows_of(i, STEP * tile)
        pairs = (
            (hidden.at[many], hidden_hbm.at[many]),
            (d_agg_out.at[few], d_agg_hbm.at[few]),
            (d_pre_out.at[many], d_pre_hbm.at[many]),
        )
        return [pltpu.make_async_copy(*p, sem_out.at[i, n]) for n, p in enumerate(pairs)]

    start(moves)
    for i in range(chunks):
        start(fetch(i))
    rem_grad[...] = jnp.zeros_like(rem_grad)
    w_grad[...] = jnp.zeros_like(w_grad)
    b_grad[...] = jnp.zeros_like(b_grad)
    wait(moves)

    @pl.loop(0, chunks)
    def _(i):
        wait(fetch(i))
        many = rows_of(i, STEP * tile)

        def edges(b):
            return jnp.concatenate([tiles[i * STEP + b, k] for k in range(per_block)], 1)

        per = STEP // 2
        rows_per = per * tile

        def lines(g):
            return rows_of(i * 2 + g, rows_per)

        def stage_a(g):
            remote = []
            for b in range(g * per, (g + 1) * per):
                taken = [table[src[k, i * STEP + b]] for k in range(per_block)]
                remote.append(
                    jnp.dot(edges(b), jnp.concatenate(taken, 0), preferred_element_type=F32)
                )
            agg = agg_local[lines(g), :] + jnp.concatenate(remote, 0)
            both = jnp.concatenate([rows[lines(g), :], agg.astype(BF16)], 1)
            return both, jnp.dot(both, weights[...], preferred_element_type=F32) + bias[...]

        def stage_b(g, pre):
            sig = jax.nn.sigmoid(pre)
            hid = pre * sig
            hidden[lines(g), :] = hid.astype(BF16)
            d_pre = d_hidden[lines(g), :].astype(F32) * (sig + hid * (1.0 - sig))
            b_grad[...] += jnp.sum(d_pre.reshape(-1, 8, d_pre.shape[-1]), 0)
            d_pre_b = d_pre.astype(BF16)
            d_pre_out[lines(g), :] = d_pre_b
            return d_pre_b

        def stage_c(g, both, d_pre_b):
            d_agg = lax.dot_general(weights[width:, :], d_pre_b, NT, preferred_element_type=F32)
            d_agg = d_agg.astype(BF16)
            for n in range(per):
                b = g * per + n
                own = d_agg[:, n * tile : (n + 1) * tile]
                d_agg_out[i * STEP + b] = own
                terms = jnp.dot(own, edges(b), preferred_element_type=F32)
                for k in range(per_block):
                    rem_grad[src[k, i * STEP + b]] += terms[:, k * tile : (k + 1) * tile]
            w_grad[...] += lax.dot_general(d_pre_b, both, TN, preferred_element_type=F32)

        held = {}
        for stage, g in [(0, 0), (1, 0), (0, 1), (2, 0), (1, 1), (2, 1)]:
            if stage == 0:
                held[g] = stage_a(g)
            elif stage == 1:
                held[g] = (held[g][0], stage_b(g, held[g][1]))
            else:
                stage_c(g, *held[g])
        start(store(i))

    sent = []
    for w, s in enumerate(slots):
        backs_out[w] = rem_grad[pl.ds(s * per_list, per_list)].astype(BF16)
        sent.append(pltpu.make_async_copy(backs_out.at[w], backs[w], sem_back.at[w]))
    start(sent)
    half, chunk, _ = mine.shape
    parts = 2 * half
    owned = hub_blocks * tile // parts
    hub_rows = jnp.concatenate(
        [jnp.transpose(rem_grad[halo_count + q]) for q in range(hub_blocks)], 0
    )
    split = hub_rows.reshape(parts, owned, width)
    for i in range(owned):
        spread[pl.ds(i, parts, stride=chunk), :] = split[:, i, :]
    spread[pl.ds(owned, parts, stride=chunk), :] = w_grad[:, :width]
    spread[pl.ds(owned + 1, parts, stride=chunk), :] = w_grad[:, width:]
    total = jnp.sum(b_grad[...], 0, keepdims=True)
    high = total.astype(BF16).astype(F32)
    lane = lax.broadcasted_iota(jnp.int32, (width, parts), 0)
    two = jnp.where(lane == 0, high, jnp.where(lane == 1, total - high, 0.0))
    spread[pl.ds(owned + 2, parts, stride=chunk), :] = jnp.transpose(two)
    for i in range(owned + 3, chunk):
        spread[pl.ds(i, parts, stride=chunk), :] = jnp.zeros((parts, width), F32)
    by_core = spread[...].reshape(half, 2, chunk, width)
    odd = lists_of_ways()[0] == 1
    pack_out[...] = jnp.where(odd, by_core[:, 0], by_core[:, 1]).astype(BF16)
    last = pltpu.make_async_copy(pack_out, theirs, sem_back.at[lists])
    last.start()
    mine[...] = jnp.where(odd, by_core[:, 1], by_core[:, 0])
    wait(sent)
    for i in range(chunks):
        wait(store(i))
    last.wait()


def layer(src, tiles, rows, agg_local, halos, hub, w_self, w_neigh, bias, d_hidden, parts):
    count, per_block, tile, _ = tiles.shape
    nodes, width = rows.shape
    units = d_hidden.shape[-1]
    lists, per_list = len(halos), halos[0].shape[0]
    table = lists * per_list + hub.shape[0]
    pieces = (parts // 2, CHUNK, width)
    chunks = count // STEP
    return pl.pallas_call(
        layer_kernel,
        out_shape=[
            pltpu.HBM((nodes, units), BF16),
            pltpu.HBM((nodes, units), BF16),
            pltpu.HBM((count, width, tile), BF16),
        ]
        + [pltpu.HBM((per_list, width, tile), BF16)] * lists
        + [pltpu.VMEM(pieces, F32), pltpu.HBM(pieces, BF16)],
        in_specs=[HBM_SPEC] * 5 + [ANY_SPEC] * (lists + 1) + [HBM_SPEC] * 3,
        out_specs=[HBM_SPEC] * (lists + 3) + [VMEM_SPEC, HBM_SPEC],
        scratch_shapes=[
            pltpu.SMEM(src.shape, jnp.int32),
            pltpu.VMEM((2 * width, units), BF16),
            pltpu.VMEM((1, units), F32),
            pltpu.VMEM((table, tile, width), BF16),
            pltpu.VMEM((table, width, tile), F32),
            pltpu.VMEM((lists, per_list, width, tile), BF16),
            pltpu.VMEM((units, 2 * width), F32),
            pltpu.VMEM((8, units), F32),
            pltpu.VMEM((parts * CHUNK, width), F32),
            pltpu.VMEM(pieces, BF16),
            pltpu.VMEM(tiles.shape, BF16),
            pltpu.VMEM((nodes, width), BF16),
            pltpu.VMEM((nodes, width), F32),
            pltpu.VMEM((nodes, units), BF16),
            pltpu.VMEM((nodes, units), BF16),
            pltpu.VMEM((count, width, tile), BF16),
            pltpu.VMEM((nodes, units), BF16),
            pltpu.SemaphoreType.DMA((lists + 5,)),
            pltpu.SemaphoreType.DMA((lists + 1,)),
            pltpu.SemaphoreType.DMA((chunks, 4)),
            pltpu.SemaphoreType.DMA((chunks, 3)),
        ],
        compiler_params=params(),
        cost_estimate=pl.CostEstimate(
            flops=4 * tiles.size * width + 12 * nodes * width * units,
            bytes_accessed=14 << 20,
            transcendentals=nodes * units,
        ),
        name="layer",
    )(
        hbm(src),
        hbm(tiles),
        hbm(rows),
        hbm(agg_local),
        hbm(d_hidden),
        *halos,
        hub,
        hbm(w_self),
        hbm(w_neigh),
        hbm(bias),
    )


def add_kernel(mine, theirs_any, out_hbm, theirs, out, sems):
    load = pltpu.make_async_copy(theirs_any, theirs, sems.at[0])
    load.start()
    load.wait()
    out[...] = (mine[...] + theirs[...].astype(F32)).astype(BF16)
    save = pltpu.make_async_copy(out, out_hbm, sems.at[1])
    save.start()
    save.wait()


def add_pieces(mine, theirs):
    return pl.pallas_call(
        add_kernel,
        out_shape=pltpu.HBM(theirs.shape, BF16),
        in_specs=[VMEM_SPEC, ANY_SPEC],
        out_specs=HBM_SPEC,
        scratch_shapes=[
            pltpu.VMEM(theirs.shape, BF16),
            pltpu.VMEM(theirs.shape, BF16),
            pltpu.SemaphoreType.DMA((2,)),
        ],
        compiler_params=params(),
        name="add_pieces",
    )(vmem(mine), theirs)


def back_kernel(
    src_hbm, weight_hbm, tiles_hbm, d_hbm, p_hbm, total, src, weight, tiles, d_agg, d_pre, sems, sem_in
):
    count, per_block, tile, _ = tiles.shape
    size = STEP * tile

    def fetch(i):
        part = pl.ds(i * STEP, STEP)
        many = rows_of(i, size)
        pairs = (
            (p_hbm.at[many], d_pre.at[many]),
            (tiles_hbm.at[part], tiles.at[part]),
            (d_hbm.at[part], d_agg.at[part]),
        )
        return [pltpu.make_async_copy(*p, sem_in.at[i, n]) for n, p in enumerate(pairs)]

    loads = [
        pltpu.make_async_copy(src_hbm, src, sems.at[0]),
        pltpu.make_async_copy(weight_hbm, weight, sems.at[1]),
    ]
    start(loads)
    for i in range(count // STEP):
        start(fetch(i))
    total[...] = jnp.zeros_like(total)
    wait(loads)

    @pl.loop(0, count // STEP)
    def _(i):
        wait(fetch(i))
        own = lax.dot_general(
            weight[...], d_pre[rows_of(i, size), :], NT, preferred_element_type=F32
        )
        for b in range(STEP):
            at = i * STEP + b
            total[at] += own[:, b * tile : (b + 1) * tile]
            edges = jnp.concatenate([tiles[at, k] for k in range(per_block)], 1)
            terms = jnp.dot(d_agg[at], edges, preferred_element_type=F32)
            for k in range(per_block):
                s = src[k, at]
                total[s] += terms[:, k * tile : (k + 1) * tile]


def local_backward(src, tiles, d_pre, d_agg, weight):
    count, per_block, tile, _ = tiles.shape
    width, units = weight.shape
    return pl.pallas_call(
        back_kernel,
        out_shape=pltpu.VMEM((count, width, tile), F32),
        in_specs=[HBM_SPEC] * 5,
        out_specs=VMEM_SPEC,
        scratch_shapes=[
            pltpu.SMEM(src.shape, jnp.int32),
            pltpu.VMEM(weight.shape, BF16),
            pltpu.VMEM(tiles.shape, BF16),
            pltpu.VMEM(d_agg.shape, BF16),
            pltpu.VMEM(d_pre.shape, BF16),
            pltpu.SemaphoreType.DMA((2,)),
            pltpu.SemaphoreType.DMA((count // STEP, 3)),
        ],
        compiler_params=params(),
        cost_estimate=pl.CostEstimate(
            flops=2 * tiles.size * width + 2 * d_pre.size * width,
            bytes_accessed=8 << 20,
            transcendentals=0,
        ),
        name="local_backward",
    )(hbm(src), hbm(weight), hbm(tiles), hbm(d_agg), hbm(d_pre))


def collect_kernel(send_hbm, hubs_hbm, _, pieces_any, *refs):
    lists, per_list = send_hbm.shape
    halos_any, refs = refs[:lists], refs[lists:]
    total, out, g_self, g_neigh, g_bias = refs[:5]
    send, hubs, halos, pieces, turned, sem_in, sem_out = refs[5:]
    count, width, tile = total.shape
    owned = hubs.shape[0]
    pairs = [(send_hbm, send), (hubs_hbm, hubs)]
    pairs += [(halos_any[way], halos.at[way]) for way in range(lists)]
    pairs.append((pieces_any, pieces))
    loads = [pltpu.make_async_copy(*p, sem_in.at[n]) for n, p in enumerate(pairs)]
    start(loads)
    wait(loads)
    for way, j in enumerate(lists_of_ways()):
        for h in range(per_list):
            total[send[j, h]] += halos[way, h].astype(F32)
    summed = jnp.sum(pieces[...].astype(F32), 0)
    g_self[...] = summed[owned : owned + 1, :]
    g_neigh[...] = summed[owned + 1 : owned + 2, :]
    last = summed[owned + 2 : owned + 3, :]
    g_bias[...] = jnp.broadcast_to(last[:, 0:1] + last[:, 1:2], last.shape)
    lane = lax.broadcasted_iota(jnp.int32, (width, tile), 1)
    for i in range(owned):
        row = hubs[i]
        column = jnp.transpose(jnp.broadcast_to(summed[i : i + 1, :], (tile, width)))
        total[row // tile] += jnp.where(lane == lax.rem(row, tile), column, 0.0)
    chunks = sem_out.shape[0]
    each = count // chunks
    stores = []
    for c in range(chunks):
        for b in range(c * each, (c + 1) * each):
            turned[b * tile : (b + 1) * tile, :] = jnp.transpose(total[b]).astype(BF16)
        part = pl.ds(c * each * tile, each * tile)
        stores.append(pltpu.make_async_copy(turned.at[part], out.at[part], sem_out.at[c]))
        stores[-1].start()
    wait(stores)


def collect(send, hubs, grad, pieces, halos):
    count, width, tile = grad.shape
    lists = len(halos)
    line = jax.ShapeDtypeStruct((1, width), F32)
    return pl.pallas_call(
        collect_kernel,
        out_shape=[pltpu.VMEM(grad.shape, F32), pltpu.HBM((count * tile, width), BF16)]
        + [line] * 3,
        in_specs=[HBM_SPEC] * 2 + [VMEM_SPEC] + [ANY_SPEC] * (1 + lists),
        out_specs=[VMEM_SPEC, HBM_SPEC] + [VMEM_SPEC] * 3,
        scratch_shapes=[
            pltpu.SMEM(send.shape, jnp.int32),
            pltpu.SMEM(hubs.shape, jnp.int32),
            pltpu.VMEM((lists,) + halos[0].shape, BF16),
            pltpu.VMEM(pieces.shape, BF16),
            pltpu.VMEM((count * tile, width), BF16),
            pltpu.SemaphoreType.DMA((3 + lists,)),
            pltpu.SemaphoreType.DMA((4,)),
        ],
        input_output_aliases={2: 0},
        compiler_params=params(),
        name="collect",
    )(hbm(send), hbm(hubs), vmem(grad), pieces, *halos)[1:]


def shards(
    features,
    local_tiles,
    local_src,
    remote_tiles,
    remote_src,
    send_blocks,
    hub_rows,
    w_self,
    w_neigh,
    bias,
    d_hidden,
):
    parts = lax.axis_size("dom")
    nodes, width = features.shape
    tile = local_tiles.shape[-1]
    owned = hub_rows.shape[0]
    blocks = features.reshape(nodes // tile, tile, width)
    *sends, hub_mine, own = gather_sends(send_blocks, hub_rows, blocks, parts)
    hub_all = lax.all_to_all(hub_mine, "dom", 0, 0)
    halos = [swapped(b, way) for way, b in enumerate(sends)]
    agg_local = local_aggregate(local_src.T, local_tiles, own)
    hidden, d_pre, d_agg, *rest = layer(
        remote_src.T,
        remote_tiles,
        features,
        agg_local,
        halos,
        hub_all.reshape(parts * owned // tile, tile, width),
        w_self,
        w_neigh,
        bias[None],
        d_hidden,
        parts,
    )
    *backs, mine, theirs = rest
    packed = add_pieces(mine, swapped(theirs, 0))
    same_core = [list(range(c, parts, 2)) for c in range(2)]
    pieces = lax.all_to_all(packed, "dom", 0, 0, axis_index_groups=same_core)
    returned = [swapped(b, way) for way, b in enumerate(backs)]
    grad_t = local_backward(local_src.T, local_tiles, d_pre, d_agg, w_self)
    grad, g_self, g_neigh, g_bias = collect(send_blocks, hub_rows, grad_t, pieces, returned)
    return (hidden, grad, g_self.reshape(width, 1), g_neigh.reshape(width, 1), g_bias[0, :1])


def solution(mesh):
    in_specs = (
        P("dom", None),
        P("dom", None, None, None),
        P("dom", None),
        P("dom", None, None, None),
        P("dom", None),
        P("dom", None),
        P("dom"),
        P(),
        P(),
        P(),
        P("dom", None),
    )
    out_specs = (P("dom", None), P("dom", None), P(None, "dom"), P(None, "dom"), P("dom"))
    return jax.shard_map(shards, mesh=mesh, in_specs=in_specs, out_specs=out_specs, check_vma=False)
```

```python
import functools

import jax
import jax.numpy as jnp
from jax import lax
from jax.experimental import pallas as pl
from jax.experimental.pallas import tpu as pltpu
from jax.sharding import PartitionSpec as P

OFFSETS = (1, -1, 2, -2)
F32 = jnp.float32
BF16 = jnp.bfloat16
NT = (((1,), (1,)), ((), ()))
TN = (((0,), (0,)), ((), ()))
GROUP = 16
CHUNK = 8
STEP = 8


def partner(i, way, n):
    if way == 0:
        return i ^ 1
    if way == 1:
        return (i + (1 if i & 1 else -1)) % n
    ahead = (i >> 1) & 1 == way - 2
    return (i + (2 if ahead else -2)) % n


def swapped(block, way):
    n = lax.axis_size("dom")
    return lax.ppermute(block, "dom", [(i, partner(i, way, n)) for i in range(n)])


def lists_of_ways():
    me = lax.axis_index("dom")
    odd, odd_chip = me & 1, (me >> 1) & 1
    return odd, 1 - odd, 2 + odd_chip, 3 - odd_chip


def rows_of(chunk, size):
    return pl.ds(pl.multiple_of(chunk * size, size), size)


def params():
    return pltpu.CompilerParams(vmem_limit_bytes=40 << 20)


def hbm(x):
    return pltpu.with_memory_space_constraint(x, pltpu.HBM)


def vmem(x):
    return pltpu.with_memory_space_constraint(x, pltpu.VMEM)


ANY_SPEC = pl.BlockSpec(memory_space=pl.ANY)
HBM_SPEC = pl.BlockSpec(memory_space=pltpu.HBM)
VMEM_SPEC = pl.BlockSpec(memory_space=pltpu.VMEM)


def start(copies):
    for c in copies:
        c.start()


def wait(copies):
    for c in copies:
        c.wait()


def whole(shape):
    return pl.BlockSpec(shape, lambda *_: (0,) * len(shape))


def send_kernel(send_hbm, hubs_hbm, blocks_hbm, *refs):
    lists, per_list = send_hbm.shape
    outs, refs = refs[:lists], refs[lists:]
    hub_out, blocks, send, hubs, spread, sem_in, sems = refs
    owned = hubs.shape[0]
    count, tile, width = blocks.shape
    pairs = [(send_hbm, send), (hubs_hbm, hubs)]
    half = count // 2
    for part in (pl.ds(0, half), pl.ds(half, half)):
        pairs.append((blocks_hbm.at[part], blocks.at[part]))
    loads = [pltpu.make_async_copy(*p, sem_in.at[n]) for n, p in enumerate(pairs)]
    start(loads)
    wait(loads)
    place = lax.broadcasted_iota(jnp.int32, (GROUP, width), 0)
    moves = []
    for way, j in enumerate(lists_of_ways()):
        for h in range(per_list):
            moves.append(
                pltpu.make_async_copy(
                    blocks.at[send[j, h]], outs[way].at[h], sems.at[way * per_list + h]
                )
            )
    start(moves)
    rows = []
    for i in range(owned):
        row = hubs[i]
        base = pl.multiple_of(lax.rem(row, tile) // GROUP * GROUP, GROUP)
        near = blocks[row // tile, pl.ds(base, GROUP), :].astype(F32)
        chosen = jnp.where(place == lax.rem(row, GROUP), near, 0.0)
        rows.append(jnp.sum(chosen, 0, keepdims=True))
    spread[...] = jnp.broadcast_to(jnp.concatenate(rows, 0).astype(BF16)[None], spread.shape)
    last = pltpu.make_async_copy(spread, hub_out, sems.at[lists * per_list])
    last.start()
    wait(moves)
    last.wait()


def gather_sends(send, hubs, blocks, parts):
    lists, per_list = send.shape
    _, tile, width = blocks.shape
    return pl.pallas_call(
        send_kernel,
        out_shape=[pltpu.HBM((per_list, tile, width), BF16)] * lists
        + [
            pltpu.HBM((parts, hubs.shape[0], width), BF16),
            pltpu.VMEM(blocks.shape, BF16),
        ],
        in_specs=[HBM_SPEC] * 3,
        out_specs=[HBM_SPEC] * lists + [HBM_SPEC, VMEM_SPEC],
        scratch_shapes=[
            pltpu.SMEM(send.shape, jnp.int32),
            pltpu.SMEM(hubs.shape, jnp.int32),
            pltpu.VMEM((parts, hubs.shape[0], width), BF16),
            pltpu.SemaphoreType.DMA((4,)),
            pltpu.SemaphoreType.DMA((lists * per_list + 1,)),
        ],
        compiler_params=params(),
        name="sends",
    )(hbm(send), hbm(hubs), hbm(blocks))


def local_kernel(
    src_hbm, tiles_hbm, blocks, agg_hbm, src, tiles, agg, sem, sem_in, sem_out
):
    count, per_block, tile, _ = tiles.shape
    chunks = count // STEP

    def fetch(i):
        part = pl.ds(i * STEP, STEP)
        return pltpu.make_async_copy(tiles_hbm.at[part], tiles.at[part], sem_in.at[i])

    def store(i):
        part = rows_of(i, STEP * tile)
        return pltpu.make_async_copy(agg.at[part], agg_hbm.at[part], sem_out.at[i])

    index = pltpu.make_async_copy(src_hbm, src, sem)
    index.start()
    for i in range(chunks):
        fetch(i).start()
    index.wait()

    @pl.loop(0, chunks)
    def _(i):
        fetch(i).wait()
        for b in range(STEP):
            at = i * STEP + b
            taken = [blocks[src[k, at]] for k in range(per_block)]
            edges = [tiles[at, k] for k in range(per_block)]
            agg[rows_of(at, tile), :] = jnp.dot(
                jnp.concatenate(edges, 1), jnp.concatenate(taken, 0), preferred_element_type=F32
            )
        store(i).start()

    wait([store(i) for i in range(chunks)])


def local_aggregate(src, tiles, blocks):
    count, per_block, tile, _ = tiles.shape
    width = blocks.shape[-1]
    agg = (count * tile, width)
    return pl.pallas_call(
        local_kernel,
        out_shape=pltpu.HBM(agg, F32),
        in_specs=[HBM_SPEC] * 2 + [VMEM_SPEC],
        out_specs=HBM_SPEC,
        scratch_shapes=[
            pltpu.SMEM(src.shape, jnp.int32),
            pltpu.VMEM(tiles.shape, BF16),
            pltpu.VMEM(agg, F32),
            pltpu.SemaphoreType.DMA,
            pltpu.SemaphoreType.DMA((count // STEP,)),
            pltpu.SemaphoreType.DMA((count // STEP,)),
        ],
        compiler_params=params(),
        cost_estimate=pl.CostEstimate(
            flops=2 * tiles.size * width, bytes_accessed=8 << 20, transcendentals=0
        ),
        name="local_aggregate",
    )(hbm(src), hbm(tiles), vmem(blocks))


def layer_kernel(src_hbm, *refs):
    lists = len(OFFSETS)
    tiles_hbm, rows_hbm, agg_hbm, d_hbm = refs[:4]
    halos, refs = refs[4 : 4 + lists], refs[4 + lists :]
    hub, self_hbm, neigh_hbm, bias_hbm, hidden_hbm, d_pre_hbm, d_agg_hbm = refs[:7]
    backs, refs = refs[7 : 7 + lists], refs[7 + lists :]
    mine, theirs, src, weights, bias, table, rem_grad, backs_out, w_grad, b_grad = refs[:10]
    spread, pack_out, tiles, rows, agg_local, d_hidden, hidden, d_agg_out = refs[10:18]
    d_pre_out, sem_t, sem_back, sem_in, sem_out = refs[18:]
    count, per_block, tile, _ = tiles.shape
    width = rows.shape[-1]
    per_list = halos[0].shape[0]
    halo_count = lists * per_list
    hub_blocks = hub.shape[0]
    slots = [j ^ 1 for j in lists_of_ways()]
    pairs = [
        (src_hbm, src),
        (hub, table.at[pl.ds(halo_count, hub_blocks)]),
        (self_hbm, weights.at[pl.ds(0, width)]),
        (neigh_hbm, weights.at[pl.ds(width, width)]),
        (bias_hbm, bias),
    ]
    for w, s in enumerate(slots):
        pairs.append((halos[w], table.at[pl.ds(s * per_list, per_list)]))
    moves = [pltpu.make_async_copy(*p, sem_t.at[n]) for n, p in enumerate(pairs)]
    chunks = count // STEP

    def fetch(i):
        few, many = pl.ds(i * STEP, STEP), rows_of(i, STEP * tile)
        pairs = (
            (tiles_hbm.at[few], tiles.at[few]),
            (agg_hbm.at[many], agg_local.at[many]),
            (rows_hbm.at[many], rows.at[many]),
            (d_hbm.at[many], d_hidden.at[many]),
        )
        return [pltpu.make_async_copy(*p, sem_in.at[i, n]) for n, p in enumerate(pairs)]

    def store(i):
        few, many = pl.ds(i * STEP, STEP), rows_of(i, STEP * tile)
        pairs = (
            (hidden.at[many], hidden_hbm.at[many]),
            (d_agg_out.at[few], d_agg_hbm.at[few]),
            (d_pre_out.at[many], d_pre_hbm.at[many]),
        )
        return [pltpu.make_async_copy(*p, sem_out.at[i, n]) for n, p in enumerate(pairs)]

    start(moves)
    for i in range(chunks):
        start(fetch(i))
    rem_grad[...] = jnp.zeros_like(rem_grad)
    w_grad[...] = jnp.zeros_like(w_grad)
    b_grad[...] = jnp.zeros_like(b_grad)
    wait(moves)

    @pl.loop(0, chunks)
    def _(i):
        wait(fetch(i))
        many = rows_of(i, STEP * tile)

        def edges(b):
            return jnp.concatenate([tiles[i * STEP + b, k] for k in range(per_block)], 1)

        per = STEP // 2
        rows_per = per * tile

        def lines(g):
            return rows_of(i * 2 + g, rows_per)

        def stage_a(g):
            remote = []
            for b in range(g * per, (g + 1) * per):
                taken = [table[src[k, i * STEP + b]] for k in range(per_block)]
                remote.append(
                    jnp.dot(edges(b), jnp.concatenate(taken, 0), preferred_element_type=F32)
                )
            agg = agg_local[lines(g), :] + jnp.concatenate(remote, 0)
            both = jnp.concatenate([rows[lines(g), :], agg.astype(BF16)], 1)
            return both, jnp.dot(both, weights[...], preferred_element_type=F32) + bias[...]

        def stage_b(g, pre):
            sig = jax.nn.sigmoid(pre)
            hid = pre * sig
            hidden[lines(g), :] = hid.astype(BF16)
            d_pre = d_hidden[lines(g), :].astype(F32) * (sig + hid * (1.0 - sig))
            b_grad[...] += jnp.sum(d_pre.reshape(-1, 8, d_pre.shape[-1]), 0)
            d_pre_b = d_pre.astype(BF16)
            d_pre_out[lines(g), :] = d_pre_b
            return d_pre_b

        def stage_c(g, both, d_pre_b):
            d_agg = lax.dot_general(weights[width:, :], d_pre_b, NT, preferred_element_type=F32)
            d_agg = d_agg.astype(BF16)
            for n in range(per):
                b = g * per + n
                own = d_agg[:, n * tile : (n + 1) * tile]
                d_agg_out[i * STEP + b] = own
                terms = jnp.dot(own, edges(b), preferred_element_type=F32)
                for k in range(per_block):
                    rem_grad[src[k, i * STEP + b]] += terms[:, k * tile : (k + 1) * tile]
            w_grad[...] += lax.dot_general(d_pre_b, both, TN, preferred_element_type=F32)

        held = {}
        for stage, g in [(0, 0), (1, 0), (0, 1), (2, 0), (1, 1), (2, 1)]:
            if stage == 0:
                held[g] = stage_a(g)
            elif stage == 1:
                held[g] = (held[g][0], stage_b(g, held[g][1]))
            else:
                stage_c(g, *held[g])
        start(store(i))

    sent = []
    for w, s in enumerate(slots):
        backs_out[w] = rem_grad[pl.ds(s * per_list, per_list)].astype(BF16)
        sent.append(pltpu.make_async_copy(backs_out.at[w], backs[w], sem_back.at[w]))
    start(sent)
    half, chunk, _ = mine.shape
    parts = 2 * half
    owned = hub_blocks * tile // parts
    hub_rows = jnp.concatenate(
        [jnp.transpose(rem_grad[halo_count + q]) for q in range(hub_blocks)], 0
    )
    split = hub_rows.reshape(parts, owned, width)
    for i in range(owned):
        spread[pl.ds(i, parts, stride=chunk), :] = split[:, i, :]
    spread[pl.ds(owned, parts, stride=chunk), :] = w_grad[:, :width]
    spread[pl.ds(owned + 1, parts, stride=chunk), :] = w_grad[:, width:]
    total = jnp.sum(b_grad[...], 0, keepdims=True)
    high = total.astype(BF16).astype(F32)
    lane = lax.broadcasted_iota(jnp.int32, (width, parts), 0)
    two = jnp.where(lane == 0, high, jnp.where(lane == 1, total - high, 0.0))
    spread[pl.ds(owned + 2, parts, stride=chunk), :] = jnp.transpose(two)
    for i in range(owned + 3, chunk):
        spread[pl.ds(i, parts, stride=chunk), :] = jnp.zeros((parts, width), F32)
    by_core = spread[...].reshape(half, 2, chunk, width)
    odd = lists_of_ways()[0] == 1
    pack_out[...] = jnp.where(odd, by_core[:, 0], by_core[:, 1]).astype(BF16)
    last = pltpu.make_async_copy(pack_out, theirs, sem_back.at[lists])
    last.start()
    mine[...] = jnp.where(odd, by_core[:, 1], by_core[:, 0])
    wait(sent)
    for i in range(chunks):
        wait(store(i))
    last.wait()


def layer(src, tiles, rows, agg_local, halos, hub, w_self, w_neigh, bias, d_hidden, parts):
    count, per_block, tile, _ = tiles.shape
    nodes, width = rows.shape
    units = d_hidden.shape[-1]
    lists, per_list = len(halos), halos[0].shape[0]
    table = lists * per_list + hub.shape[0]
    pieces = (parts // 2, CHUNK, width)
    chunks = count // STEP
    return pl.pallas_call(
        layer_kernel,
        out_shape=[
            pltpu.HBM((nodes, units), BF16),
            pltpu.HBM((nodes, units), BF16),
            pltpu.HBM((count, width, tile), BF16),
        ]
        + [pltpu.HBM((per_list, width, tile), BF16)] * lists
        + [pltpu.VMEM(pieces, F32), pltpu.HBM(pieces, BF16)],
        in_specs=[HBM_SPEC] * 5 + [ANY_SPEC] * (lists + 1) + [HBM_SPEC] * 3,
        out_specs=[HBM_SPEC] * (lists + 3) + [VMEM_SPEC, HBM_SPEC],
        scratch_shapes=[
            pltpu.SMEM(src.shape, jnp.int32),
            pltpu.VMEM((2 * width, units), BF16),
            pltpu.VMEM((1, units), F32),
            pltpu.VMEM((table, tile, width), BF16),
            pltpu.VMEM((table, width, tile), F32),
            pltpu.VMEM((lists, per_list, width, tile), BF16),
            pltpu.VMEM((units, 2 * width), F32),
            pltpu.VMEM((8, units), F32),
            pltpu.VMEM((parts * CHUNK, width), F32),
            pltpu.VMEM(pieces, BF16),
            pltpu.VMEM(tiles.shape, BF16),
            pltpu.VMEM((nodes, width), BF16),
            pltpu.VMEM((nodes, width), F32),
            pltpu.VMEM((nodes, units), BF16),
            pltpu.VMEM((nodes, units), BF16),
            pltpu.VMEM((count, width, tile), BF16),
            pltpu.VMEM((nodes, units), BF16),
            pltpu.SemaphoreType.DMA((lists + 5,)),
            pltpu.SemaphoreType.DMA((lists + 1,)),
            pltpu.SemaphoreType.DMA((chunks, 4)),
            pltpu.SemaphoreType.DMA((chunks, 3)),
        ],
        compiler_params=params(),
        cost_estimate=pl.CostEstimate(
            flops=4 * tiles.size * width + 12 * nodes * width * units,
            bytes_accessed=14 << 20,
            transcendentals=nodes * units,
        ),
        name="layer",
    )(
        hbm(src),
        hbm(tiles),
        hbm(rows),
        hbm(agg_local),
        hbm(d_hidden),
        *halos,
        hub,
        hbm(w_self),
        hbm(w_neigh),
        hbm(bias),
    )


def add_kernel(mine, theirs_any, relay, *refs):
    backs, (out_hbm, *joined), refs = refs[:2], refs[2:5], refs[5:]
    theirs, out, both, sem_in, sem_out = refs
    per_list = relay.shape[0]
    first, second = pl.ds(0, per_list), pl.ds(per_list, per_list)
    pairs = [(theirs_any, theirs)]
    for n in range(2):
        pairs += [(backs[n], both.at[n, first]), (relay, both.at[n, second])]
    loads = [pltpu.make_async_copy(*p, sem_in.at[n]) for n, p in enumerate(pairs)]
    start(loads)
    loads[0].wait()
    out[...] = (mine[...] + theirs[...].astype(F32)).astype(BF16)
    saves = [pltpu.make_async_copy(out, out_hbm, sem_out.at[0])]
    saves[0].start()
    wait(loads[1:])
    for n in range(2):
        saves.append(pltpu.make_async_copy(both.at[n], joined[n], sem_out.at[1 + n]))
        saves[-1].start()
    wait(saves)


def add_pieces(mine, theirs, relay, backs):
    joined = (2 * relay.shape[0],) + relay.shape[1:]
    return pl.pallas_call(
        add_kernel,
        out_shape=[pltpu.HBM(theirs.shape, BF16)] + [pltpu.HBM(joined, BF16)] * 2,
        in_specs=[VMEM_SPEC] + [ANY_SPEC] * 4,
        out_specs=[HBM_SPEC] * 3,
        scratch_shapes=[
            pltpu.VMEM(theirs.shape, BF16),
            pltpu.VMEM(theirs.shape, BF16),
            pltpu.VMEM((2,) + joined, BF16),
            pltpu.SemaphoreType.DMA((5,)),
            pltpu.SemaphoreType.DMA((3,)),
        ],
        compiler_params=params(),
        name="add_pieces",
    )(vmem(mine), theirs, relay, *[hbm(b) for b in backs])


def back_kernel(
    src_hbm, weight_hbm, tiles_hbm, d_hbm, p_hbm, total, src, weight, tiles, d_agg, d_pre, sems, sem_in
):
    count, per_block, tile, _ = tiles.shape
    size = STEP * tile

    def fetch(i):
        part = pl.ds(i * STEP, STEP)
        many = rows_of(i, size)
        pairs = (
            (p_hbm.at[many], d_pre.at[many]),
            (tiles_hbm.at[part], tiles.at[part]),
            (d_hbm.at[part], d_agg.at[part]),
        )
        return [pltpu.make_async_copy(*p, sem_in.at[i, n]) for n, p in enumerate(pairs)]

    loads = [
        pltpu.make_async_copy(src_hbm, src, sems.at[0]),
        pltpu.make_async_copy(weight_hbm, weight, sems.at[1]),
    ]
    start(loads)
    for i in range(count // STEP):
        start(fetch(i))
    total[...] = jnp.zeros_like(total)
    wait(loads)

    @pl.loop(0, count // STEP)
    def _(i):
        wait(fetch(i))
        own = lax.dot_general(
            weight[...], d_pre[rows_of(i, size), :], NT, preferred_element_type=F32
        )
        for b in range(STEP):
            at = i * STEP + b
            total[at] += own[:, b * tile : (b + 1) * tile]
            edges = jnp.concatenate([tiles[at, k] for k in range(per_block)], 1)
            terms = jnp.dot(d_agg[at], edges, preferred_element_type=F32)
            for k in range(per_block):
                s = src[k, at]
                total[s] += terms[:, k * tile : (k + 1) * tile]


def local_backward(src, tiles, d_pre, d_agg, weight):
    count, per_block, tile, _ = tiles.shape
    width, units = weight.shape
    return pl.pallas_call(
        back_kernel,
        out_shape=pltpu.VMEM((count, width, tile), F32),
        in_specs=[HBM_SPEC] * 5,
        out_specs=VMEM_SPEC,
        scratch_shapes=[
            pltpu.SMEM(src.shape, jnp.int32),
            pltpu.VMEM(weight.shape, BF16),
            pltpu.VMEM(tiles.shape, BF16),
            pltpu.VMEM(d_agg.shape, BF16),
            pltpu.VMEM(d_pre.shape, BF16),
            pltpu.SemaphoreType.DMA((2,)),
            pltpu.SemaphoreType.DMA((count // STEP, 3)),
        ],
        compiler_params=params(),
        cost_estimate=pl.CostEstimate(
            flops=2 * tiles.size * width + 2 * d_pre.size * width,
            bytes_accessed=8 << 20,
            transcendentals=0,
        ),
        name="local_backward",
    )(hbm(src), hbm(weight), hbm(tiles), hbm(d_agg), hbm(d_pre))


def collect_kernel(send_hbm, hubs_hbm, _, pieces_any, *refs):
    lists, per_list = send_hbm.shape
    near_any, *chips_any = refs[:3]
    refs = refs[3:]
    total, out, g_self, g_neigh, g_bias = refs[:5]
    send, hubs, halos, pieces, turned, sem_in, sem_out = refs[5:]
    count, width, tile = total.shape
    owned = hubs.shape[0]
    pairs = [(send_hbm, send), (hubs_hbm, hubs)]
    first, second = pl.ds(0, per_list), pl.ds(per_list, per_list)
    pairs += [(pieces_any, pieces), (near_any, halos.at[0])]
    for n in range(2):
        pairs.append((chips_any[n].at[first], halos.at[2 + n]))
        pairs.append((chips_any[n].at[second], halos.at[4 + n]))
    loads = [pltpu.make_async_copy(*p, sem_in.at[n]) for n, p in enumerate(pairs)]
    start(loads)
    wait(loads)
    ways = lists_of_ways()
    relayed = jnp.where((ways[0] + ways[2]) % 2 == 1, 4, 5)
    for n, j in zip((0, relayed, 2, 3), ways):
        for h in range(per_list):
            total[send[j, h]] += halos[n, h].astype(F32)
    summed = jnp.sum(pieces[...].astype(F32), 0)
    g_self[...] = summed[owned : owned + 1, :]
    g_neigh[...] = summed[owned + 1 : owned + 2, :]
    last = summed[owned + 2 : owned + 3, :]
    g_bias[...] = jnp.broadcast_to(last[:, 0:1] + last[:, 1:2], last.shape)
    lane = lax.broadcasted_iota(jnp.int32, (width, tile), 1)
    for i in range(owned):
        row = hubs[i]
        column = jnp.transpose(jnp.broadcast_to(summed[i : i + 1, :], (tile, width)))
        total[row // tile] += jnp.where(lane == lax.rem(row, tile), column, 0.0)
    chunks = sem_out.shape[0]
    each = count // chunks
    stores = []
    for c in range(chunks):
        for b in range(c * each, (c + 1) * each):
            turned[b * tile : (b + 1) * tile, :] = jnp.transpose(total[b]).astype(BF16)
        part = pl.ds(c * each * tile, each * tile)
        stores.append(pltpu.make_async_copy(turned.at[part], out.at[part], sem_out.at[c]))
        stores[-1].start()
    wait(stores)


def collect(send, hubs, grad, pieces, halos):
    count, width, tile = grad.shape
    line = jax.ShapeDtypeStruct((1, width), F32)
    return pl.pallas_call(
        collect_kernel,
        out_shape=[pltpu.VMEM(grad.shape, F32), pltpu.HBM((count * tile, width), BF16)]
        + [line] * 3,
        in_specs=[HBM_SPEC] * 2 + [VMEM_SPEC] + [ANY_SPEC] * 4,
        out_specs=[VMEM_SPEC, HBM_SPEC] + [VMEM_SPEC] * 3,
        scratch_shapes=[
            pltpu.SMEM(send.shape, jnp.int32),
            pltpu.SMEM(hubs.shape, jnp.int32),
            pltpu.VMEM((6,) + halos[0].shape, BF16),
            pltpu.VMEM(pieces.shape, BF16),
            pltpu.VMEM((count * tile, width), BF16),
            pltpu.SemaphoreType.DMA((8,)),
            pltpu.SemaphoreType.DMA((4,)),
        ],
        input_output_aliases={2: 0},
        compiler_params=params(),
        name="collect",
    )(hbm(send), hbm(hubs), vmem(grad), pieces, *halos)[1:]


def shards(
    features,
    local_tiles,
    local_src,
    remote_tiles,
    remote_src,
    send_blocks,
    hub_rows,
    w_self,
    w_neigh,
    bias,
    d_hidden,
):
    parts = lax.axis_size("dom")
    nodes, width = features.shape
    tile = local_tiles.shape[-1]
    owned = hub_rows.shape[0]
    blocks = features.reshape(nodes // tile, tile, width)
    *sends, hub_mine, own = gather_sends(send_blocks, hub_rows, blocks, parts)
    hub_all = lax.all_to_all(hub_mine, "dom", 0, 0)
    halos = [swapped(b, way) for way, b in enumerate(sends)]
    agg_local = local_aggregate(local_src.T, local_tiles, own)
    hidden, d_pre, d_agg, *rest = layer(
        remote_src.T,
        remote_tiles,
        features,
        agg_local,
        halos,
        hub_all.reshape(parts * owned // tile, tile, width),
        w_self,
        w_neigh,
        bias[None],
        d_hidden,
        parts,
    )
    *backs, mine, theirs = rest
    packed, *joined = add_pieces(mine, swapped(theirs, 0), swapped(backs[1], 0), backs[2:])
    same_core = [list(range(c, parts, 2)) for c in range(2)]
    pieces = lax.all_to_all(packed, "dom", 0, 0, axis_index_groups=same_core)
    returned = [swapped(x, way) for x, way in zip([backs[0]] + joined, (0, 2, 3))]
    grad_t = local_backward(local_src.T, local_tiles, d_pre, d_agg, w_self)
    grad, g_self, g_neigh, g_bias = collect(send_blocks, hub_rows, grad_t, pieces, returned)
    return (hidden, grad, g_self.reshape(width, 1), g_neigh.reshape(width, 1), g_bias[0, :1])


def solution(mesh):
    in_specs = (
        P("dom", None),
        P("dom", None, None, None),
        P("dom", None),
        P("dom", None, None, None),
        P("dom", None),
        P("dom", None),
        P("dom"),
        P(),
        P(),
        P(),
        P("dom", None),
    )
    out_specs = (P("dom", None), P("dom", None), P(None, "dom"), P(None, "dom"), P("dom"))
    return jax.shard_map(shards, mesh=mesh, in_specs=in_specs, out_specs=out_specs, check_vma=False)
```
